32 devices in a mesh: section: 2 (over x), dp: 16 (over z, y, core).
Axes of the slice: x: 2, y: 2, z: 4, core: 2. Of those that a mesh axis runs over, the one named last changes fastest.
Arguments:
- inputs: bfloat16 [24448, 384], P('dp'), may hold values from -6 to 6
- cotangent: bfloat16 [24448, 384], P('dp'), may hold values from -6 to 6
- wide_weights: float32 [2, 384, 2688], P('section', 'dp'), may hold values from -0.3125 to 0.3125
- wide_first: float32 [2, 384, 2688], P('section', 'dp'), may hold values from -469.07569 to 469.07569
- wide_second: float32 [2, 384, 2688], P('section', 'dp'), may hold values from 0 to 48896
- tall_weights: float32 [2, 1920, 384], P('section', 'dp'), as said below
- tall_first: float32 [2, 1920, 384], P('section', 'dp'), may hold values from -469.07569 to 469.07569
- tall_second: float32 [2, 1920, 384], P('section', 'dp'), may hold values from 0 to 48896
- vectors: float32 [2, 12, 384], P('section', None, 'dp'), as said below
- vector_first: float32 [2, 12, 384], P('section', None, 'dp'), may hold values from -469.07569 to 469.07569
- vector_second: float32 [2, 12, 384], P('section', None, 'dp'), may hold values from 0 to 48896
Outputs:
- activations: bfloat16 [2, 24448, 384], P('section', 'dp')
- input_grads: bfloat16 [2, 24448, 384], P('section', 'dp')
- new_wide_first: float32 [2, 384, 2688], P('section', 'dp')
- new_wide_second: float32 [2, 384, 2688], P('section', 'dp')
- new_wide_weights: float32 [2, 384, 2688], P('section', 'dp')
- new_tall_first: float32 [2, 1920, 384], P('section', 'dp')
- new_tall_second: float32 [2, 1920, 384], P('section', 'dp')
- new_tall_weights: float32 [2, 1920, 384], P('section', 'dp')
- new_vector_first: float32 [2, 12, 384], P('section', None, 'dp')
- new_vector_second: float32 [2, 12, 384], P('section', None, 'dp')
- new_vectors: float32 [2, 12, 384], P('section', None, 'dp')
The draws below stay inside these ranges and needn't reach their ends.
Inputs may be any that keep to these rules, and one draw needn't show every extreme that they name: `tall_weights`: rows below 384 of each layer are about 4 / sqrt(384) in spread, the rest about 1.5 / sqrt(1536). `vectors`: rows 0 and 5 of each layer are gains near 1; the others are biases.
All inputs are finite; a program needn't handle non-finite values.
Results may differ from the reference program's by a relative error of at most 0.014.
Values may be sent and summed in bfloat16 or wider, within the bound.
A program may use at most 192 MiB of HBM per device.

```python
import math
import jax
import jax.numpy as jnp
from jax import lax

D = 384
HEADS = 6
HEAD_DIM = 64
FF = 1536
GLOBAL = 2
GLOBAL_LEN = 197
LOCAL = 10
LOCAL_LEN = 37
STEP = 5
IMG_TOK = 764
TOKENS = 24448


def wide_scale():
    column_index = jnp.arange(3 * D + FF)
    return jnp.where(column_index < 3 * D, 0.1, 0.3)[None, None, :] * math.sqrt(TOKENS)


def tall_scale():
    row_index = jnp.arange(D + FF)
    return jnp.where(row_index < D, 0.2, 0.4)[None, :, None] * math.sqrt(TOKENS)


def first_moment(key, shape, scale):
    magnitude = jax.random.uniform(jax.random.fold_in(key, 1), shape, jnp.float32, 0.5, 2.0)
    signs = jnp.where(jax.random.bernoulli(jax.random.fold_in(key, 2), 0.5, shape), 1.0, -1.0)
    return signs * magnitude * scale * 0.8


def second_moment(key, shape, scale):
    factor = jnp.exp(jax.random.uniform(key, shape, jnp.float32, 0.0, math.log(4.0)))
    return factor * scale * scale


def draw_tall_weights(key, part):
    key = jax.random.fold_in(key, 11)
    samples = jax.random.normal(key, (2, D + FF, D), jnp.float32)
    row_index = jnp.arange(D + FF)
    factor = jnp.where(row_index < D, 4.0 / math.sqrt(D), 1.5 / math.sqrt(FF))
    return samples * factor[None, :, None]


def draw_vectors(key, part):
    key = jax.random.fold_in(key, 7)
    samples = jax.random.normal(key, (2, 12, D), jnp.float32)
    row_index = jnp.arange(12)
    gain_rows = (row_index == 0) | (row_index == 5)
    return jnp.where(gain_rows[None, :, None], 1.0 + 0.15 * samples, 0.3 * samples)


def draw_wide_first(key, part):
    key = jax.random.fold_in(key, 21)
    return first_moment(key, (2, D, 3 * D + FF), wide_scale())


def draw_wide_second(key, part):
    key = jax.random.fold_in(key, 22)
    return second_moment(key, (2, D, 3 * D + FF), wide_scale())


def draw_tall_first(key, part):
    key = jax.random.fold_in(key, 23)
    return first_moment(key, (2, D + FF, D), tall_scale())


def draw_tall_second(key, part):
    key = jax.random.fold_in(key, 24)
    return second_moment(key, (2, D + FF, D), tall_scale())


def draw_vector_first(key, part):
    key = jax.random.fold_in(key, 25)
    return first_moment(key, (2, 12, D), 0.5 * math.sqrt(TOKENS))


def draw_vector_second(key, part):
    key = jax.random.fold_in(key, 26)
    return second_moment(key, (2, 12, D), 0.5 * math.sqrt(TOKENS))


def raised(drawn, stream_key, source, target, blocks, factor):
    owner, partner = [(jnp.arange(drawn.shape[dim]) // (drawn.shape[dim] // blocks)).reshape([-1 if axis == dim else 1 for axis in range(drawn.ndim)]) for dim in (source, target)]
    chosen = jax.random.permutation(stream_key, blocks)[partner]
    strong = (owner == chosen) | (owner == (partner + blocks // 2) % blocks)
    return jnp.where(strong, factor * drawn, drawn)


def block_levels(rng, dims, cuts, least, high):
    def one(position, blocks):
        steps = jax.random.uniform(jax.random.fold_in(jax.random.fold_in(rng, 6), position), (blocks,), jnp.float32, least / len(cuts), high / len(cuts))
        return jnp.repeat(jnp.exp(steps), dims[position] // blocks).reshape((-1,) + (1,) * (len(dims) - position - 1))

    gain = one(*cuts[0])
    for cut in cuts[1:]:
        gain = gain * one(*cut)
    return gain


def bell_draw(stream_key, extent, deviation, reach, pieces=(), kind=jnp.bfloat16):
    factor_of = block_levels(stream_key, extent, pieces, -0.22, 0.18) if pieces else 1.0
    drawn = jax.random.normal(stream_key, extent, jnp.float32) * deviation * factor_of
    return jnp.minimum(jnp.maximum(drawn, -reach), reach).astype(kind)


def noise_with(own_key, extent, spread, limit, split, heavy, held_as=jnp.bfloat16):
    entries = spread * jax.random.normal(own_key, extent, jnp.float32)
    if split:
        entries = entries * block_levels(own_key, extent, split, -0.22, 0.18)
    return jnp.clip(raised(entries, jax.random.fold_in(own_key, 3), *heavy), -limit, limit).astype(held_as)


def setup_inputs(seed: int = 0) -> dict:
    arg_keys = jax.random.split(jax.random.key(seed), 12)
    inputs = noise_with(arg_keys[0], (TOKENS, D), 1.0, 6.0, ((0, 16),), (0, 1, 16, 2.0))
    cotangent = bell_draw(arg_keys[1], (TOKENS, D), 1.0, 6.0, ((0, 16),))
    wide_weights = bell_draw(arg_keys[2], (2, D, 4 * D + FF - D), D ** -0.5, 0.3125, ((0, 2), (1, 16)), jnp.float32)
    wide_first = draw_wide_first(jax.random.fold_in(arg_keys[11], 71), 0)
    wide_second = draw_wide_second(jax.random.fold_in(arg_keys[11], 71), 0)
    tall_weights = draw_tall_weights(jax.random.fold_in(arg_keys[11], 71), 0)
    tall_first = draw_tall_first(jax.random.fold_in(arg_keys[11], 71), 0)
    tall_second = draw_tall_second(jax.random.fold_in(arg_keys[11], 71), 0)
    vectors = draw_vectors(jax.random.fold_in(arg_keys[11], 71), 0)
    vector_first = draw_vector_first(jax.random.fold_in(arg_keys[11], 71), 0)
    vector_second = draw_vector_second(jax.random.fold_in(arg_keys[11], 71), 0)
    return {"inputs": inputs, "cotangent": cotangent, "wide_weights": wide_weights, "wide_first": wide_first, "wide_second": wide_second, "tall_weights": tall_weights, "tall_first": tall_first, "tall_second": tall_second, "vectors": vectors, "vector_first": vector_first, "vector_second": vector_second}


NORM_EPS = 1e-06
BETA_ONE = 0.5
BETA_TWO = 0.5
ADAM_EPS = 1e-08
RATE_MATRIX = 0.05
RATE_VECTOR = 0.2
DECAY = 0.05
ERF_SCALE = 0.7071067811865476

@jax.custom_vjp
def low(v):
    return lax.optimization_barrier(v.astype(jnp.bfloat16)).astype(jnp.float32)

@jax.custom_vjp
def low_back(v):
    return v

def low_keep(v):
    return (low(v), None)

def low_pass(kept, grad):
    return (grad,)

def back_keep(v):
    return (v, None)

def back_low(kept, grad):
    return (low(grad),)
low.defvjp(low_keep, low_pass)
low_back.defvjp(back_keep, back_low)

def matmul(former, latter):
    return jnp.dot(former, latter, precision=lax.Precision.HIGHEST)

def standard(values):
    centre = values - lax.optimization_barrier(jnp.mean(values, axis=-1, keepdims=True))
    return centre * lax.rsqrt(lax.optimization_barrier(jnp.mean(centre * centre, axis=-1, keepdims=True)) + NORM_EPS)

def attend(packed, crop_count, length):
    by_head = packed.reshape(crop_count, length, 3, HEADS, HEAD_DIM)
    queries = by_head[:, :, 0]
    key_rows = by_head[:, :, 1]
    value_rows = by_head[:, :, 2]
    scores = low_back(jnp.einsum('cqhd,ckhd->chqk', queries, key_rows, precision=lax.Precision.HIGHEST) * HEAD_DIM ** (-0.5))
    largest = lax.optimization_barrier(jnp.max(scores, axis=-1, keepdims=True))
    exponent = jnp.exp(scores - largest)
    weights = low(exponent / lax.optimization_barrier(jnp.sum(exponent, axis=-1, keepdims=True)))
    mixture = jnp.einsum('chqk,ckhd->cqhd', weights, value_rows, precision=lax.Precision.HIGHEST)
    return mixture.reshape(crop_count * length, HEADS * HEAD_DIM)

def layer(current, wide_w, tall_w, gains):
    width = tall_w.shape[1]
    global_rows = GLOBAL * GLOBAL_LEN
    mix_input = low(standard(current) * gains[0] + gains[1])
    bias_row = jnp.concatenate((gains[2], jnp.zeros((width,), jnp.float32), gains[3]))
    packed = low_back(low(matmul(mix_input, wide_w[:, :3 * width]) + bias_row))
    mixture = jnp.concatenate((attend(packed[:global_rows], GLOBAL, GLOBAL_LEN), attend(packed[global_rows:], LOCAL, LOCAL_LEN)))
    mixture = low_back(low(mixture))
    hidden = current + low_back(matmul(mixture, tall_w[:width]) + gains[4])
    feed_input = low(standard(hidden) * gains[5] + gains[6])
    pre_gelu = low_back(matmul(feed_input, wide_w[:, 3 * width:]) + gains[8:].reshape(-1))
    activated = low(0.5 * pre_gelu * (1.0 + lax.erf(pre_gelu * ERF_SCALE)))
    return hidden + matmul(activated, tall_w[width:]) + gains[7]

def adamw(weights, first, second, grads, rate, decay):
    first_new = BETA_ONE * first + (1.0 - BETA_ONE) * grads
    second_new = BETA_TWO * second + (1.0 - BETA_TWO) * grads * grads
    corrected = first_new / (1.0 - BETA_ONE ** STEP) / (jnp.sqrt(second_new / (1.0 - BETA_TWO ** STEP)) + ADAM_EPS)
    return (first_new, second_new, weights - rate * (corrected + decay * weights))

def reference(inputs, cotangent, wide_weights, wide_first, wide_second, tall_weights, tall_first, tall_second, vectors, vector_first, vector_second):
    image_count = inputs.shape[0] // IMG_TOK
    width = inputs.shape[1]
    image_rows = inputs.astype(jnp.float32).reshape(image_count, IMG_TOK, width)
    probes = jnp.zeros_like(image_rows)

    def whole(wide_w, tall_w, gains, image_in, probe_in):
        wide_c = low(wide_w)
        tall_c = low(tall_w)
        gain_c = low(gains)

        def one_image(pair):
            first_in, probe_one = pair
            sent = low(layer(first_in, wide_c[0], tall_c[0], gain_c[0]))
            second_in = low_back(sent + probe_one)
            return (sent, layer(second_in, wide_c[1], tall_c[1], gain_c[1]))
        return lax.map(jax.checkpoint(one_image), (image_in, probe_in))
    outcome, pullback = jax.vjp(whole, wide_weights, tall_weights, vectors, image_rows, probes)
    sent_all, final_all = outcome
    grad_wide, grad_tall, grad_vec, grad_inputs, grad_probes = pullback((jnp.zeros_like(sent_all), cotangent.astype(jnp.float32).reshape(image_count, IMG_TOK, width)))
    activations = jnp.stack((sent_all.reshape(-1, width), final_all.reshape(-1, width))).astype(jnp.bfloat16)
    input_grads = jnp.stack((grad_inputs.reshape(-1, width), grad_probes.reshape(-1, width))).astype(jnp.bfloat16)
    wide_m, wide_s, wide_n = adamw(wide_weights, wide_first, wide_second, grad_wide, RATE_MATRIX, DECAY)
    tall_m, tall_s, tall_n = adamw(tall_weights, tall_first, tall_second, grad_tall, RATE_MATRIX, DECAY)
    vec_m, vec_s, vec_n = adamw(vectors, vector_first, vector_second, grad_vec, RATE_VECTOR, 0.0)
    return (activations, input_grads, wide_m, wide_s, wide_n, tall_m, tall_s, tall_n, vec_m, vec_s, vec_n)
```

```python
import functools

import jax
import jax.numpy as jnp
from jax import lax
from jax.experimental import pallas as pl
from jax.experimental.pallas import tpu as pltpu
from jax.sharding import PartitionSpec as P

D = 384
HEADS = 6
HEAD_DIM = 64
FF = 1536
GLOBAL = 2
GLOBAL_LEN = 197
LOCAL = 10
LOCAL_LEN = 37
STEP = 5
IMG_TOK = GLOBAL * GLOBAL_LEN + LOCAL * LOCAL_LEN

NORM_EPS = 1e-06
BETA_ONE = 0.5
BETA_TWO = 0.5
ADAM_EPS = 1e-08
RATE_MATRIX = 0.05
RATE_VECTOR = 0.2
DECAY = 0.05

ROWS = 768
BLOCK = 256
BLOCKS = ROWS // BLOCK
WINDOW = 208
WINDOWS = 4
CHUNK = 512
CHUNKS = FF // CHUNK
F32 = jnp.float32
BF16 = jnp.bfloat16


def window_start(index):
    return pl.multiple_of(jnp.minimum(index * 192, ROWS - WINDOW), 16)


def row_segment(row):
    local = ((row - GLOBAL * GLOBAL_LEN) * 1772) >> 16
    segment = jnp.where(row < GLOBAL * GLOBAL_LEN, jnp.where(row < GLOBAL_LEN, 0, 1), local + GLOBAL)
    return jnp.where(row < IMG_TOK, segment, 99)


def window_of(segment):
    return jnp.where(segment < 2, segment, jnp.where(segment < 7, 2, jnp.where(segment < 12, 3, 9)))


def dot(a, b):
    return jnp.dot(a, b, preferred_element_type=F32)


def dot_t(a, b):
    return lax.dot_general(a, b, (((1,), (1,)), ((), ())), preferred_element_type=F32)


def t_dot(a, b):
    return lax.dot_general(a, b, (((0,), (0,)), ((), ())), preferred_element_type=F32)


def standard(values):
    centre = values - jnp.mean(values, axis=-1, keepdims=True)
    inverse = lax.rsqrt(jnp.mean(centre * centre, axis=-1, keepdims=True) + NORM_EPS)
    return centre * inverse, inverse


def norm_back(normed, inverse, gain, incoming):
    scaled = incoming * gain
    return inverse * (
        scaled
        - jnp.mean(scaled, axis=-1, keepdims=True)
        - normed * jnp.mean(scaled * normed, axis=-1, keepdims=True)
    )


def gelu_pair(f):
    t = 1.0 / (1.0 + (0.3275911 * 0.7071067811865476) * jnp.abs(f))
    e = jnp.exp(-0.5 * f * f)
    poly = t * (
        0.5 * 0.254829592
        + t * (0.5 * -0.284496736 + t * (0.5 * 1.421413741 + t * (0.5 * -1.453152027 + t * (0.5 * 1.061405429))))
    )
    tail = poly * e
    below = jnp.where(f >= 0, 1.0 - tail, tail)
    return f * below, below + f * e * 0.3989422804014327


def column_sum(values):
    return jnp.sum(values, axis=0, keepdims=True)


def forward_layer(l, u_ref, out_ref, wide, tall, vec, s):
    def first(i, _):
        rows = pl.ds(pl.multiple_of(i * BLOCK, BLOCK), BLOCK)
        normed, _unused = standard(u_ref[rows, :].astype(F32))
        a = (normed * vec[l, 0:1, :] + vec[l, 1:2, :]).astype(BF16)
        s.a[l, rows, :] = a
        for third in range(3):
            cols = slice(third * D, (third + 1) * D)
            part = dot(a, wide[l, :, cols])
            if third != 1:
                part = part + vec[l, 2 + third // 2 : 3 + third // 2, :]
            s.qkv[l, rows, cols] = part.astype(BF16)
        return 0

    lax.fori_loop(0, BLOCKS, first, 0)
    s.o[l] = jnp.zeros((ROWS, D), BF16)
    low = lax.broadcasted_iota(jnp.int32, (1, 128), 1) < HEAD_DIM

    def attend(w, _):
        rows = pl.ds(window_start(w), WINDOW)
        bias = s.bias[w]
        for pair in range(HEADS // 2):
            base = pair * 128
            q = s.qkv[l, rows, base : base + 128]
            k = s.qkv[l, rows, D + base : D + base + 128]
            v = s.qkv[l, rows, 2 * D + base : 2 * D + base + 128]
            total = None
            for half in range(2):
                keep = low if half == 0 else jnp.logical_not(low)
                scores = dot_t(jnp.where(keep, k, jnp.zeros_like(k)), q) * (HEAD_DIM**-0.5) + bias
                top = jnp.maximum(jnp.max(scores, axis=0, keepdims=True), -1e20)
                weights = jnp.exp(scores - top)
                summed = jnp.sum(weights, axis=0, keepdims=True)
                weights = (weights * (1.0 / jnp.maximum(summed, 1e-20))).astype(BF16)
                s.p[l, w, 2 * pair + half] = weights
                part = t_dot(weights, jnp.where(keep, v, jnp.zeros_like(v)))
                total = part if total is None else total + part
            old = s.o[l, rows, base : base + 128]
            s.o[l, rows, base : base + 128] = old + total.astype(BF16)
        return 0

    lax.fori_loop(0, WINDOWS, attend, 0)

    def second(i, _):
        rows = pl.ds(pl.multiple_of(i * BLOCK, BLOCK), BLOCK)
        hidden = u_ref[rows, :].astype(F32) + dot(s.o[l, rows, :], tall[l, 0:D, :]) + vec[l, 4:5, :]
        s.h[l, rows, :] = hidden
        normed, _unused = standard(hidden)
        c = (normed * vec[l, 5:6, :] + vec[l, 6:7, :]).astype(BF16)
        s.c[l, rows, :] = c
        total = hidden + vec[l, 7:8, :]
        for j in range(CHUNKS):
            cols = slice(j * CHUNK, (j + 1) * CHUNK)
            f = dot(c, wide[l, :, 3 * D + j * CHUNK : 3 * D + (j + 1) * CHUNK]) + s.bup[l, 0:1, cols]
            value, slope = gelu_pair(f)
            z = value.astype(BF16)
            s.z[l, rows, cols] = z
            s.slope[l, rows, cols] = slope.astype(BF16)
            total = total + dot(z, tall[l, D + j * CHUNK : D + (j + 1) * CHUNK, :])
        out_ref[rows, :] = total.astype(BF16)
        return 0

    lax.fori_loop(0, BLOCKS, second, 0)


def backward_layer(l, u_ref, dy_ref, du_ref, wide, tall, vec, gwide, gtall, gvec, s):
    gvec[l] = jnp.zeros_like(gvec[l])
    s.dbup[...] = jnp.zeros_like(s.dbup)

    def first(i, _):
        rows = pl.ds(pl.multiple_of(i * BLOCK, BLOCK), BLOCK)
        dy = dy_ref[rows, :]
        dc = jnp.zeros((BLOCK, D), F32)
        for j in range(CHUNKS):
            cols = slice(j * CHUNK, (j + 1) * CHUNK)
            dz = dot_t(dy, tall[l, D + j * CHUNK : D + (j + 1) * CHUNK, :])
            df = (dz * s.slope[l, rows, cols].astype(F32)).astype(BF16)
            s.df[rows, cols] = df
            s.dbup[0:1, cols] += column_sum(df.astype(F32))
            dc = dc + dot_t(df, wide[l, :, 3 * D + j * CHUNK : 3 * D + (j + 1) * CHUNK])
        normed, inverse = standard(s.h[l, rows, :])
        top = dy.astype(F32)
        dh = top + norm_back(normed, inverse, vec[l, 5:6, :], dc)
        s.dh[rows, :] = dh
        dhb = dh.astype(BF16)
        s.dhb[rows, :] = dhb
        s.dout[rows, :] = dot_t(dhb, tall[l, 0:D, :]).astype(BF16)
        gvec[l, 4:5, :] += column_sum(dhb.astype(F32))
        gvec[l, 5:6, :] += column_sum(dc * normed)
        gvec[l, 6:7, :] += column_sum(dc)
        gvec[l, 7:8, :] += column_sum(top)
        return 0

    lax.fori_loop(0, BLOCKS, first, 0)
    for j in range(FF // D):
        gvec[l, 8 + j : 9 + j, :] = s.dbup[0:1, j * D : (j + 1) * D]

    def down(i, _):
        cols = pl.ds(pl.multiple_of(i * BLOCK, BLOCK), BLOCK)
        gtall[l, pl.ds(pl.multiple_of(D + i * BLOCK, 128), BLOCK), :] = t_dot(s.z[l, :, cols], dy_ref[...]).astype(gtall.dtype)
        return 0

    lax.fori_loop(0, FF // BLOCK, down, 0)

    def up(i, _):
        cols = pl.ds(pl.multiple_of(i * BLOCK, BLOCK), BLOCK)
        gwide[l, :, pl.ds(pl.multiple_of(3 * D + i * BLOCK, 128), BLOCK)] = t_dot(s.c[l], s.df[:, cols]).astype(gwide.dtype)
        return 0

    lax.fori_loop(0, FF // BLOCK, up, 0)
    gtall[l, 0:D, :] = t_dot(s.o[l], s.dhb[...]).astype(gtall.dtype)

    s.dqkv[...] = jnp.zeros_like(s.dqkv)
    low = lax.broadcasted_iota(jnp.int32, (1, 128), 1) < HEAD_DIM

    def attend(w, _):
        rows = pl.ds(window_start(w), WINDOW)
        for pair in range(HEADS // 2):
            base = pair * 128
            q = s.qkv[l, rows, base : base + 128]
            k = s.qkv[l, rows, D + base : D + base + 128]
            v = s.qkv[l, rows, 2 * D + base : 2 * D + base + 128]
            grad = s.dout[rows, base : base + 128]
            dq = dk = dv = None
            for half in range(2):
                keep = low if half == 0 else jnp.logical_not(low)

                def only(x, keep=keep):
                    return jnp.where(keep, x, jnp.zeros_like(x))

                weights = s.p[l, w, 2 * pair + half]
                grad_half = only(grad)
                dv_part = dot(weights, grad_half)
                dp = dot_t(v, grad_half)
                wide_weights = weights.astype(F32)
                product = dp * wide_weights
                ds = (product - wide_weights * jnp.sum(product, axis=0, keepdims=True)).astype(BF16)
                dk_part = dot(ds, only(q))
                dq_part = t_dot(ds, only(k))
                if half == 0:
                    dq, dk, dv = dq_part, dk_part, dv_part
                else:
                    dq, dk, dv = dq + dq_part, dk + dk_part, dv + dv_part
            scale = HEAD_DIM**-0.5
            for offset, value in ((0, dq * scale), (D, dk * scale), (2 * D, dv)):
                cols = slice(offset + base, offset + base + 128)
                s.dqkv[rows, cols] = s.dqkv[rows, cols] + value.astype(BF16)
        return 0

    lax.fori_loop(0, WINDOWS, attend, 0)

    def last(i, _):
        rows = pl.ds(pl.multiple_of(i * BLOCK, BLOCK), BLOCK)
        dqkv = s.dqkv[rows, :]
        da = dot_t(dqkv, wide[l, :, 0 : 3 * D])
        normed, inverse = standard(u_ref[rows, :].astype(F32))
        du = s.dh[rows, :] + norm_back(normed, inverse, vec[l, 0:1, :], da)
        du_ref[rows, :] = du.astype(BF16)
        gvec[l, 0:1, :] += column_sum(da * normed)
        gvec[l, 1:2, :] += column_sum(da)
        gvec[l, 2:3, :] += column_sum(dqkv[:, 0:D].astype(F32))
        gvec[l, 3:4, :] += column_sum(dqkv[:, 2 * D : 3 * D].astype(F32))
        return 0

    lax.fori_loop(0, BLOCKS, last, 0)

    def mix(i, _):
        cols = pl.ds(pl.multiple_of(i * D, 128), D)
        gwide[l, :, cols] = t_dot(s.a[l], s.dqkv[:, cols]).astype(gwide.dtype)
        return 0

    lax.fori_loop(0, 3, mix, 0)


class Scratch:
    pass


SCRATCH = (
    ("a", (2, ROWS, D), BF16),
    ("qkv", (2, ROWS, 3 * D), BF16),
    ("o", (2, ROWS, D), BF16),
    ("h", (2, ROWS, D), F32),
    ("c", (2, ROWS, D), BF16),
    ("z", (2, ROWS, FF), BF16),
    ("slope", (2, ROWS, FF), BF16),
    ("p", (2, WINDOWS, HEADS, WINDOW, WINDOW), BF16),
    ("bias", (WINDOWS, WINDOW, WINDOW), F32),
    ("bup", (2, 8, FF), F32),
    ("dbup", (8, FF), F32),
    ("df", (ROWS, FF), BF16),
    ("dh", (ROWS, D), F32),
    ("dhb", (ROWS, D), BF16),
    ("dout", (ROWS, D), BF16),
    ("dqkv", (ROWS, 3 * D), BF16),
)


def image_kernel(x, cot, wide, tall, vec, act, grads, gwide, gtall, gvec, *scratch):
    s = Scratch()
    for (name, _, _), ref in zip(SCRATCH, scratch):
        setattr(s, name, ref)

    def fill(w, _):
        start = window_start(w)
        key = row_segment(start + lax.broadcasted_iota(jnp.int32, (WINDOW, 1), 0))
        query = row_segment(start + lax.broadcasted_iota(jnp.int32, (1, WINDOW), 1))
        inside = (key == query) & (window_of(key) == w)
        s.bias[w] = jnp.where(inside, 0.0, -1e30).astype(F32)
        return 0

    lax.fori_loop(0, WINDOWS, fill, 0)
    for l in range(2):
        for j in range(FF // D):
            s.bup[l, 0:1, j * D : (j + 1) * D] = vec[l, 8 + j : 9 + j, :]
    forward_layer(0, x, act.at[0], wide, tall, vec, s)
    forward_layer(1, act.at[0], act.at[1], wide, tall, vec, s)
    backward_layer(1, act.at[0], cot, grads.at[1], wide, tall, vec, gwide, gtall, gvec, s)
    backward_layer(0, x, grads.at[1], grads.at[0], wide, tall, vec, gwide, gtall, gvec, s)


def one_image(x, cot, wide, tall, vec):
    whole = pl.BlockSpec(memory_space=pltpu.VMEM)
    return pl.pallas_call(
        image_kernel,
        out_shape=(
            jax.ShapeDtypeStruct((2, ROWS, D), BF16),
            jax.ShapeDtypeStruct((2, ROWS, D), BF16),
            jax.ShapeDtypeStruct(wide.shape, BF16),
            jax.ShapeDtypeStruct(tall.shape, BF16),
            jax.ShapeDtypeStruct(vec.shape, F32),
        ),
        in_specs=[whole] * 5,
        out_specs=(whole,) * 5,
        scratch_shapes=[pltpu.VMEM(shape, dtype) for _, shape, dtype in SCRATCH],
        compiler_params=pltpu.CompilerParams(vmem_limit_bytes=63 * 2**20),
        cost_estimate=pl.CostEstimate(flops=18 * 10**9, bytes_accessed=20 * 10**6, transcendentals=10**7),
    )(x, cot, wide, tall, vec)


def adamw(weights, first, second, grads, rate, decay):
    first_new = BETA_ONE * first + (1.0 - BETA_ONE) * grads
    second_new = BETA_TWO * second + (1.0 - BETA_TWO) * grads * grads
    corrected = (
        first_new
        / (1.0 - BETA_ONE**STEP)
        / (jnp.sqrt(second_new / (1.0 - BETA_TWO**STEP)) + ADAM_EPS)
    )
    return (first_new, second_new, weights - rate * (corrected + decay * weights))


def per_device(
    inputs, cotangent, wide_weights, wide_first, wide_second, tall_weights, tall_first, tall_second,
    vectors, vector_first, vector_second,
):
    section = lax.axis_index("section")
    both = ("section", "dp")
    wide = lax.all_gather(wide_weights[0].astype(BF16), both, axis=0, tiled=True).reshape(2, -1, 3 * D + FF)
    tall = lax.all_gather(tall_weights[0].astype(BF16), both, axis=0, tiled=True).reshape(2, -1, D)
    vec = lax.all_gather(vectors[0].astype(BF16), "dp", axis=1, tiled=True)
    vec = lax.all_gather(vec, "section", axis=0, tiled=False).astype(F32)
    vec = jnp.pad(vec, ((0, 0), (0, 4), (0, 0)))

    def own(array):
        return jnp.pad(lax.dynamic_slice_in_dim(array, section * IMG_TOK, IMG_TOK), ((0, ROWS - IMG_TOK), (0, 0)))

    act, grads, gwide, gtall, gvec = one_image(own(inputs), own(cotangent), wide, tall, vec)

    def exchange(array):
        array = array[:, :IMG_TOK]
        mine = lax.dynamic_index_in_dim(array, section, keepdims=False)
        other = lax.dynamic_index_in_dim(array, 1 - section, keepdims=False)
        other = lax.ppermute(other, "section", [(0, 1), (1, 0)])
        return jnp.where(section == 0, jnp.concatenate((mine, other)), jnp.concatenate((other, mine)))

    def reduced(array):
        array = lax.psum_scatter(array, "section", scatter_dimension=0, tiled=False)
        return lax.psum_scatter(array, "dp", scatter_dimension=0, tiled=True).astype(F32)

    total_wide = reduced(gwide)
    total_tall = reduced(gtall)
    total_vec = lax.psum_scatter(gvec[:, :12], "section", scatter_dimension=0, tiled=False)
    total_vec = lax.psum_scatter(total_vec, "dp", scatter_dimension=1, tiled=True)
    wide_m, wide_s, wide_n = adamw(wide_weights[0], wide_first[0], wide_second[0], total_wide, RATE_MATRIX, DECAY)
    tall_m, tall_s, tall_n = adamw(tall_weights[0], tall_first[0], tall_second[0], total_tall, RATE_MATRIX, DECAY)
    vec_m, vec_s, vec_n = adamw(vectors[0], vector_first[0], vector_second[0], total_vec, RATE_VECTOR, 0.0)
    outs = (exchange(act), exchange(grads), wide_m, wide_s, wide_n, tall_m, tall_s, tall_n, vec_m, vec_s, vec_n)
    return tuple(out[None] for out in outs)


def solution(mesh):
    data = P("dp", None)
    matrix = P("section", "dp", None)
    vector = P("section", None, "dp")
    in_specs = (data, data) + (matrix,) * 6 + (vector,) * 3
    out_specs = (matrix,) * 8 + (vector,) * 3
    return jax.shard_map(per_device, mesh=mesh, in_specs=in_specs, out_specs=out_specs, check_vma=False)
```

```python
import functools

import jax
import jax.numpy as jnp
from jax import lax
from jax.experimental import pallas as pl
from jax.experimental.pallas import tpu as pltpu
from jax.sharding import PartitionSpec as P

D = 384
HEADS = 6
HEAD_DIM = 64
FF = 1536
GLOBAL = 2
GLOBAL_LEN = 197
LOCAL = 10
LOCAL_LEN = 37
STEP = 5
IMG_TOK = GLOBAL * GLOBAL_LEN + LOCAL * LOCAL_LEN

NORM_EPS = 1e-06
BETA_ONE = 0.5
BETA_TWO = 0.5
ADAM_EPS = 1e-08
RATE_MATRIX = 0.05
RATE_VECTOR = 0.2
DECAY = 0.05

ROWS = 768
BLOCK = 256
BLOCKS = ROWS // BLOCK
WINDOW = 208
WINDOWS = 4
CHUNK = 512
CHUNKS = FF // CHUNK
TILE = 16
SLOTS = 8
HALF = 19 * TILE
STAGES = ((0, 6 * TILE), (6 * TILE, 7 * TILE), (13 * TILE, 6 * TILE))
MESH = pl.DeviceIdType.MESH
F32 = jnp.float32
BF16 = jnp.bfloat16


def window_start(index):
    return pl.multiple_of(jnp.minimum(index * 192, ROWS - WINDOW), 16)


def row_segment(row):
    local = ((row - GLOBAL * GLOBAL_LEN) * 1772) >> 16
    segment = jnp.where(row < GLOBAL * GLOBAL_LEN, jnp.where(row < GLOBAL_LEN, 0, 1), local + GLOBAL)
    return jnp.where(row < IMG_TOK, segment, 99)


def window_of(segment):
    return jnp.where(segment < 2, segment, jnp.where(segment < 7, 2, jnp.where(segment < 12, 3, 9)))


def dot(a, b):
    return jnp.dot(a, b, preferred_element_type=F32)


def dot_t(a, b):
    return lax.dot_general(a, b, (((1,), (1,)), ((), ())), preferred_element_type=F32)


def t_dot(a, b):
    return lax.dot_general(a, b, (((0,), (0,)), ((), ())), preferred_element_type=F32)


def standard(values):
    centre = values - jnp.mean(values, axis=-1, keepdims=True)
    inverse = lax.rsqrt(jnp.mean(centre * centre, axis=-1, keepdims=True) + NORM_EPS)
    return centre * inverse, inverse


def norm_back(normed, inverse, gain, incoming):
    scaled = incoming * gain
    return inverse * (
        scaled
        - jnp.mean(scaled, axis=-1, keepdims=True)
        - normed * jnp.mean(scaled * normed, axis=-1, keepdims=True)
    )


def gelu_pair(f):
    t = 1.0 / (1.0 + (0.3275911 * 0.7071067811865476) * jnp.abs(f))
    e = jnp.exp(-0.5 * f * f)
    poly = t * (
        0.5 * 0.254829592
        + t * (0.5 * -0.284496736 + t * (0.5 * 1.421413741 + t * (0.5 * -1.453152027 + t * (0.5 * 1.061405429))))
    )
    tail = poly * e
    below = jnp.where(f >= 0, 1.0 - tail, tail)
    return f * below, below + f * e * 0.3989422804014327


def column_sum(values):
    return jnp.sum(values, axis=0, keepdims=True)


def qkv_tile(i):
    return i if i < 5 else 19 + i - 5


def tall_tile(i):
    return 6 + i if i < 7 else (23 if i == 7 else 25 + i - 8)


def up_tile(i):
    return 13 + i if i < 6 else 32 + i - 6


def vec_tile(half):
    return 19 * half + 5


def runs(tiles):
    out = []
    for slot, tile in tiles:
        if out and out[-1][0] == slot and out[-1][1] + out[-1][2] == tile * TILE:
            out[-1][2] += TILE
        else:
            out.append([slot, tile * TILE, TILE])
    return out


def wide_tiles(name, block):
    return [(k, name(3 * block + i)) for k in range(SLOTS) for i in range(3)]


def tall_tiles(first, count):
    per = 15
    return [(t // per, tall_tile(t % per)) for t in range(first // TILE, (first + count) // TILE)]


def load_rows(ref, l, tiles, lanes=slice(0, D)):
    return jnp.concatenate(
        [ref[l, slot // 2, slot % 2, row : row + count, lanes] for slot, row, count in runs(tiles)], axis=0
    )


def store_rows(ref, l, tiles, value):
    done = 0
    for slot, row, count in runs(tiles):
        ref[l, slot // 2, slot % 2, row : row + count, :] = value[done : done + count]
        done += count


def load_qkv(w, l):
    return jnp.concatenate([load_rows(w, l, wide_tiles(qkv_tile, b)) for b in range(3)], axis=1)


def load_up(w, l, j):
    parts, at = [], j * CHUNK
    while at < (j + 1) * CHUNK:
        block, lane = divmod(at, D)
        take = min(D - lane, (j + 1) * CHUNK - at)
        parts.append(load_rows(w, l, wide_tiles(up_tile, block), slice(lane, lane + take)))
        at += take
    return jnp.concatenate(parts, axis=1)


def load_proj(w, l):
    return load_rows(w, l, tall_tiles(0, D))


def load_down(w, l, j):
    return load_rows(w, l, tall_tiles(D + j * CHUNK, CHUNK))


def row_block(i):
    return pl.ds(pl.multiple_of(i * BLOCK, BLOCK), BLOCK)


class Image:
    def __init__(self, s):
        self.s = s
        self.low = None

    def gains(self, l):
        s = self.s
        lane = lax.broadcasted_iota(jnp.int32, (TILE, 128), 1)
        tiles = [jnp.zeros((TILE, 128), F32) for _ in range(D // 128)]
        for slot in range(SLOTS):
            for half in range(2):
                row = vec_tile(half) * TILE
                part = s.w[l, slot // 2, slot % 2, row : row + TILE, 0:128].astype(F32)
                width = D // (2 * SLOTS)
                at = (2 * slot + half) * width
                index, shift = divmod(at, 128)
                moved = pltpu.roll(part, shift, 1) if shift else part
                if shift + width > 128:
                    tiles[index] = tiles[index] + jnp.where(lane >= shift, moved, 0.0)
                    tiles[index + 1] = tiles[index + 1] + jnp.where(lane < shift, moved, 0.0)
                else:
                    tiles[index] = tiles[index] + moved
        for index, tile in enumerate(tiles):
            s.vec[l, :, index * 128 : (index + 1) * 128] = tile
        for j in range(FF // D):
            s.bup[l, 0:1, j * D : (j + 1) * D] = s.vec[l, 8 + j : 9 + j, :]

    def spread_gains(self, l):
        s = self.s
        lane = lax.broadcasted_iota(jnp.int32, (TILE, 128), 1)
        width = D // (2 * SLOTS)
        for slot in range(SLOTS):
            for half in range(2):
                at = (2 * slot + half) * width
                index, shift = divmod(at, 128)
                tile = s.gvec[l, :, index * 128 : (index + 1) * 128]
                if shift + width > 128:
                    tile = jnp.where(lane >= shift, tile, s.gvec[l, :, (index + 1) * 128 : (index + 2) * 128])
                moved = pltpu.roll(tile, 128 - shift, 1) if shift else tile
                moved = jnp.where(lane < width, moved, 0.0).astype(BF16)
                row = vec_tile(half) * TILE
                s.g[l, slot // 2, slot % 2, row : row + TILE, :] = jnp.concatenate(
                    (moved, jnp.zeros((TILE, D - 128), BF16)), axis=1
                )

    def fill_bias(self):
        s = self.s

        def fill(w, _):
            start = window_start(w)
            key = row_segment(start + lax.broadcasted_iota(jnp.int32, (WINDOW, 1), 0))
            query = row_segment(start + lax.broadcasted_iota(jnp.int32, (1, WINDOW), 1))
            inside = (key == query) & (window_of(key) == w)
            s.bias[w] = jnp.where(inside, 0.0, -1e30).astype(F32)
            return 0

        lax.fori_loop(0, WINDOWS, fill, 0)

    def forward_first(self, l, u_ref):
        s = self.s

        def step(i, _):
            rows = row_block(i)
            normed, _unused = standard(u_ref[rows, :].astype(F32))
            a = (normed * s.vec[l, 0:1, :] + s.vec[l, 1:2, :]).astype(BF16)
            s.a[l, rows, :] = a
            part = dot(a, load_qkv(s.w, l))
            s.qkv[l, rows, 0:D] = (part[:, 0:D] + s.vec[l, 2:3, :]).astype(BF16)
            s.qkv[l, rows, D : 2 * D] = part[:, D : 2 * D].astype(BF16)
            s.qkv[l, rows, 2 * D :] = (part[:, 2 * D :] + s.vec[l, 3:4, :]).astype(BF16)
            return 0

        lax.fori_loop(0, BLOCKS, step, 0)
        s.o[l] = jnp.zeros((ROWS, D), BF16)

    def forward_attend(self, l, begin, end):
        s = self.s
        low = lax.broadcasted_iota(jnp.int32, (1, 128), 1) < HEAD_DIM

        def step(w, _):
            rows = pl.ds(window_start(w), WINDOW)
            bias = s.bias[w]
            for pair in range(HEADS // 2):
                base = pair * 128
                q = s.qkv[l, rows, base : base + 128]
                k = s.qkv[l, rows, D + base : D + base + 128]
                v = s.qkv[l, rows, 2 * D + base : 2 * D + base + 128]
                total = None
                for half in range(2):
                    keep = low if half == 0 else jnp.logical_not(low)
                    scores = dot_t(jnp.where(keep, k, jnp.zeros_like(k)), q) * (HEAD_DIM**-0.5) + bias
                    top = jnp.maximum(jnp.max(scores, axis=0, keepdims=True), -1e20)
                    weights = jnp.exp(scores - top)
                    summed = jnp.sum(weights, axis=0, keepdims=True)
                    weights = (weights * (1.0 / jnp.maximum(summed, 1e-20))).astype(BF16)
                    s.p[l, w, 2 * pair + half] = weights
                    part = t_dot(weights, jnp.where(keep, v, jnp.zeros_like(v)))
                    total = part if total is None else total + part
                old = s.o[l, rows, base : base + 128]
                s.o[l, rows, base : base + 128] = old + total.astype(BF16)
            return 0

        lax.fori_loop(begin, end, step, 0)

    def forward_second(self, l, u_ref, out_ref):
        s = self.s

        def step(i, _):
            rows = row_block(i)
            hidden = u_ref[rows, :].astype(F32) + dot(s.o[l, rows, :], load_proj(s.w, l)) + s.vec[l, 4:5, :]
            s.h[l, rows, :] = hidden
            normed, _unused = standard(hidden)
            c = (normed * s.vec[l, 5:6, :] + s.vec[l, 6:7, :]).astype(BF16)
            s.c[l, rows, :] = c
            total = hidden + s.vec[l, 7:8, :]
            for j in range(CHUNKS):
                cols = slice(j * CHUNK, (j + 1) * CHUNK)
                f = dot(c, load_up(s.w, l, j)) + s.bup[l, 0:1, cols]
                value, slope = gelu_pair(f)
                z = value.astype(BF16)
                s.z[l, rows, cols] = z
                s.slope[l, rows, cols] = slope.astype(BF16)
                total = total + dot(z, load_down(s.w, l, j))
            out_ref[rows, :] = total.astype(BF16)
            return 0

        lax.fori_loop(0, BLOCKS, step, 0)

    def backward_first(self, l, dy_ref):
        s = self.s
        s.gvec[l] = jnp.zeros_like(s.gvec[l])
        s.dbup[...] = jnp.zeros_like(s.dbup)

        def step(i, _):
            rows = row_block(i)
            dy = dy_ref[rows, :]
            dc = jnp.zeros((BLOCK, D), F32)
            for j in range(CHUNKS):
                cols = slice(j * CHUNK, (j + 1) * CHUNK)
                dz = dot_t(dy, load_down(s.w, l, j))
                df = (dz * s.slope[l, rows, cols].astype(F32)).astype(BF16)
                s.df[rows, cols] = df
                s.dbup[0:1, cols] += column_sum(df.astype(F32))
                dc = dc + dot_t(df, load_up(s.w, l, j))
            normed, inverse = standard(s.h[l, rows, :])
            top = dy.astype(F32)
            dh = top + norm_back(normed, inverse, s.vec[l, 5:6, :], dc)
            s.dh[rows, :] = dh
            dhb = dh.astype(BF16)
            s.dhb[rows, :] = dhb
            s.dout[rows, :] = dot_t(dhb, load_proj(s.w, l)).astype(BF16)
            s.gvec[l, 4:5, :] += column_sum(dhb.astype(F32))
            s.gvec[l, 5:6, :] += column_sum(dc * normed)
            s.gvec[l, 6:7, :] += column_sum(dc)
            s.gvec[l, 7:8, :] += column_sum(top)
            return 0

        lax.fori_loop(0, BLOCKS, step, 0)
        for j in range(FF // D):
            s.gvec[l, 8 + j : 9 + j, :] = s.dbup[0:1, j * D : (j + 1) * D]

    def grad_up(self, l):
        s = self.s
        for b in range(FF // D):
            value = t_dot(s.c[l], s.df[:, b * D : (b + 1) * D]).astype(BF16)
            store_rows(s.g, l, wide_tiles(up_tile, b), value)

    def grad_tall(self, l, dy_ref):
        s = self.s
        for b in range(FF // D):
            value = t_dot(s.z[l, :, b * D : (b + 1) * D], dy_ref[...]).astype(BF16)
            store_rows(s.g, l, tall_tiles(D + b * D, D), value)
        store_rows(s.g, l, tall_tiles(0, D), t_dot(s.o[l], s.dhb[...]).astype(BF16))

    def backward_attend(self, l, begin, end):
        s = self.s
        low = lax.broadcasted_iota(jnp.int32, (1, 128), 1) < HEAD_DIM

        def step(w, _):
            rows = pl.ds(window_start(w), WINDOW)
            for pair in range(HEADS // 2):
                base = pair * 128
                q = s.qkv[l, rows, base : base + 128]
                k = s.qkv[l, rows, D + base : D + base + 128]
                v = s.qkv[l, rows, 2 * D + base : 2 * D + base + 128]
                grad = s.dout[rows, base : base + 128]
                dq = dk = dv = None
                for half in range(2):
                    keep = low if half == 0 else jnp.logical_not(low)

                    def only(x, keep=keep):
                        return jnp.where(keep, x, jnp.zeros_like(x))

                    weights = s.p[l, w, 2 * pair + half]
                    grad_half = only(grad)
                    dv_part = dot(weights, grad_half)
                    dp = dot_t(v, grad_half)
                    wide_weights = weights.astype(F32)
                    product = dp * wide_weights
                    ds = (product - wide_weights * jnp.sum(product, axis=0, keepdims=True)).astype(BF16)
                    dk_part = dot(ds, only(q))
                    dq_part = t_dot(ds, only(k))
                    if half == 0:
                        dq, dk, dv = dq_part, dk_part, dv_part
                    else:
                        dq, dk, dv = dq + dq_part, dk + dk_part, dv + dv_part
                scale = HEAD_DIM**-0.5
                for offset, value in ((0, dq * scale), (D, dk * scale), (2 * D, dv)):
                    cols = slice(offset + base, offset + base + 128)
                    s.dqkv[rows, cols] = s.dqkv[rows, cols] + value.astype(BF16)
            return 0

        if begin == 0:
            s.dqkv[...] = jnp.zeros_like(s.dqkv)
        lax.fori_loop(begin, end, step, 0)

    def backward_last(self, l, u_ref, du_ref):
        s = self.s

        def step(i, _):
            rows = row_block(i)
            dqkv = s.dqkv[rows, :]
            da = dot_t(dqkv, load_qkv(s.w, l))
            normed, inverse = standard(u_ref[rows, :].astype(F32))
            du = s.dh[rows, :] + norm_back(normed, inverse, s.vec[l, 0:1, :], da)
            du_ref[rows, :] = du.astype(BF16)
            s.gvec[l, 0:1, :] += column_sum(da * normed)
            s.gvec[l, 1:2, :] += column_sum(da)
            s.gvec[l, 2:3, :] += column_sum(dqkv[:, 0:D].astype(F32))
            s.gvec[l, 3:4, :] += column_sum(dqkv[:, 2 * D : 3 * D].astype(F32))
            return 0

        lax.fori_loop(0, BLOCKS, step, 0)
        self.spread_gains(l)

    def grad_qkv(self, l):
        s = self.s
        for b in range(3):
            value = t_dot(s.a[l], s.dqkv[:, b * D : (b + 1) * D]).astype(BF16)
            store_rows(s.g, l, wide_tiles(qkv_tile, b), value)


COMPUTE = (
    ("w", (2, 4, 2, 2 * HALF, D), BF16),
    ("g", (2, 4, 2, 2 * HALF, D), BF16),
    ("vec", (2, TILE, D), F32),
    ("gvec", (2, TILE, D), F32),
    ("a", (2, ROWS, D), BF16),
    ("qkv", (2, ROWS, 3 * D), BF16),
    ("o", (2, ROWS, D), BF16),
    ("h", (2, ROWS, D), F32),
    ("c", (2, ROWS, D), BF16),
    ("z", (2, ROWS, FF), BF16),
    ("slope", (2, ROWS, FF), BF16),
    ("p", (2, WINDOWS, HEADS, WINDOW, WINDOW), BF16),
    ("bias", (WINDOWS, WINDOW, WINDOW), F32),
    ("bup", (2, 8, FF), F32),
    ("dbup", (8, FF), F32),
    ("df", (ROWS, FF), BF16),
    ("dh", (ROWS, D), F32),
    ("dhb", (ROWS, D), BF16),
    ("dout", (ROWS, D), BF16),
    ("dqkv", (ROWS, 3 * D), BF16),
)
LINKS = (
    ("near_wide", (24, 3 * D + FF), F32),
    ("near_tall", (120, D), F32),
    ("near_vec", (TILE, 128), F32),
    ("total", (2, HALF, D), F32),
    ("sum_x", (3, 7 * TILE, D), BF16),
    ("from_x", (3, 7 * TILE, D), BF16),
) + tuple(
    (f"{name}{l}{st}", (count, STAGES[st][1], D), BF16)
    for l in range(2)
    for st in range(3)
    for name, count in (("from_c", 8), ("from_y", 4), ("from_z", 3))
)


class Refs:
    pass


class Links:
    def __init__(self, s):
        self.s = s
        self.section = lax.axis_index("section")
        self.dp = lax.axis_index("dp")
        self.z, self.y, self.core = self.dp // 4, (self.dp // 2) % 2, self.dp % 2
        self.near = (self.section, self.dp + 1 - 2 * self.core)
        self.across = (1 - self.section, self.dp)
        self.beside = (self.section, self.dp + 2 - 4 * self.y)
        self.pending = []

    def level(self, steps):
        there = (self.z + steps) % 4
        return there, (self.section, self.dp + 4 * (there - self.z))

    def barrier(self):
        sem = pltpu.get_barrier_semaphore()
        others = [self.near, self.across, self.beside] + [self.level(i)[1] for i in (1, 2, 3)]
        for device in others:
            pl.semaphore_signal(sem, inc=1, device_id=device, device_id_type=MESH)
        pl.semaphore_wait(sem, len(others))

    def copy(self, src, dst, sems, index, device):
        return pltpu.make_async_remote_copy(
            src_ref=src,
            dst_ref=dst,
            send_sem=sems[0].at[index],
            recv_sem=sems[1].at[index],
            device_id=device,
            device_id_type=MESH,
        )

    def send(self, *args, when=None):
        made = self.copy(*args)
        if when is None:
            made.start()
        else:
            pl.when(when)(made.start)
        self.pending.append((made, when))

    def received(self, *args):
        self.copy(*args).wait_recv()

    def drain(self):
        for made, when in self.pending:
            if when is None:
                made.wait_send()
            else:
                pl.when(when)(made.wait_send)
        self.pending = []


    def near_start(self):
        s = self.s
        for index, (src, dst) in enumerate(
            ((s.wide_in, s.near_wide), (s.tall_in, s.near_tall), (s.vec_in, s.near_vec))
        ):
            self.send(src, dst, s.near_sems, index, self.near)

    def near_finish(self):
        s = self.s
        for index, (src, dst) in enumerate(
            ((s.wide_in, s.near_wide), (s.tall_in, s.near_tall), (s.vec_in, s.near_vec))
        ):
            self.received(src, dst, s.near_sems, index, self.near)
        first = self.core == 0

        def pair(own, near):
            return jnp.where(first, own, near), jnp.where(first, near, own)

        def put(tile, value):
            s.w[self.section, self.z, self.y, tile * TILE : (tile + 1) * TILE, :] = value

        rows = jnp.concatenate(pair(s.wide_in[...], s.near_wide[...]), axis=0).astype(BF16)
        for block in range(7):
            for i in range(3):
                tile = qkv_tile(3 * block + i) if block < 3 else up_tile(3 * (block - 3) + i)
                put(tile, rows[i * TILE : (i + 1) * TILE, block * D : (block + 1) * D])
        rows = jnp.concatenate(pair(s.tall_in[...], s.near_tall[...]), axis=0).astype(BF16)
        for i in range(15):
            put(tall_tile(i), rows[i * TILE : (i + 1) * TILE])
        for half, value in enumerate(pair(s.vec_in[...], s.near_vec[...])):
            put(vec_tile(half), jnp.concatenate((value, jnp.zeros((TILE, D - 128), F32)), axis=1).astype(BF16))

    def part(self, ref, l, z, y, stage, core):
        first, count = STAGES[stage]
        return ref.at[l, z, y, pl.ds(pl.multiple_of(core * HALF + first, TILE), count), :]

    def w_part(self, l, z, y, stage, core=None):
        return self.part(self.s.w, l, z, y, stage, self.core if core is None else core)

    def gather_across(self, l, stage):
        own = self.w_part(l, self.z, self.y, stage)
        self.send(own, own, self.s.w_sems, (l, stage, 0), self.across, when=self.section == l)

    def gather_begin(self, l, stage):
        s = self.s
        own = self.w_part(l, self.z, self.y, stage)

        @pl.when(self.section != l)
        def _():
            self.received(own, own, s.w_sems, (l, stage, 0), self.across)

        self.send(own, own, s.w_sems, (l, stage, 1), self.near, when=self.section != l)
        for i in (1, 2, 3):
            self.send(own, own, s.w_sems, (l, stage, 1 + i), self.level(i)[1])
        self.send(own, own, s.w_sems, (l, stage, 8), self.beside)

    def gather_z(self, l, stage):
        s = self.s
        for i in (1, 2, 3):
            came = self.w_part(l, self.level(4 - i)[0], self.y, stage)
            self.received(came, came, s.w_sems, (l, stage, 1 + i), self.level(i)[1])
            self.send(came, came, s.w_sems, (l, stage, 8 + i), self.beside)
            self.send(came, came, s.w_sems, (l, stage, 4 + i), self.near)

    def gather_y(self, l, stage):
        s = self.s
        for i in range(4):
            came = self.w_part(l, self.level(4 - i)[0], 1 - self.y, stage)
            self.received(came, came, s.w_sems, (l, stage, 8 + i), self.beside)
            self.send(came, came, s.w_sems, (l, stage, 12 + i), self.near)

    def gather_near(self, l, stage):
        s = self.s
        other = 1 - self.core
        own = self.w_part(l, self.z, self.y, stage, other)

        @pl.when(self.section != l)
        def _():
            self.received(own, own, s.w_sems, (l, stage, 1), self.near)

        for i in (1, 2, 3):
            came = self.w_part(l, self.level(4 - i)[0], self.y, stage, other)
            self.received(came, came, s.w_sems, (l, stage, 4 + i), self.near)
        for i in range(4):
            came = self.w_part(l, self.level(4 - i)[0], 1 - self.y, stage, other)
            self.received(came, came, s.w_sems, (l, stage, 12 + i), self.near)


    def rows_of(self, stage, core):
        first, count = STAGES[stage]
        return pl.ds(pl.multiple_of(core * HALF + first, TILE), count)

    def box(self, name, l, stage):
        return getattr(self.s, f"{name}{l}{stage}")

    def reduce_begin(self, l, stage):
        s = self.s
        for i in range(8):
            src = s.g.at[l, i // 2, i % 2, self.rows_of(stage, 1 - self.core), :]
            self.send(src, self.box("from_c", l, stage).at[i], s.c_sems, (l, stage, i), self.near)

    def reduce_near(self, l, stage):
        s = self.s
        box = self.box("from_c", l, stage)
        rows = self.rows_of(stage, self.core)
        for i in range(8):
            src = s.g.at[l, i // 2, i % 2, self.rows_of(stage, 1 - self.core), :]
            self.received(src, box.at[i], s.c_sems, (l, stage, i), self.near)

        def add(i, _):
            z, y = i // 2, i % 2
            s.g[l, z, y, rows, :] = (s.g[l, z, y, rows, :].astype(F32) + box[i].astype(F32)).astype(BF16)
            return 0

        lax.fori_loop(0, 8, add, 0)
        for i in range(4):
            self.send(
                s.g.at[l, i, 1 - self.y, rows, :], self.box("from_y", l, stage).at[i], s.g_sems, (l, stage, i), self.beside
            )

    def reduce_y(self, l, stage):
        s = self.s
        box = self.box("from_y", l, stage)
        rows = self.rows_of(stage, self.core)
        for i in range(4):
            self.received(s.g.at[l, i, 1 - self.y, rows, :], box.at[i], s.g_sems, (l, stage, i), self.beside)

        def add(i, _):
            s.g[l, i, self.y, rows, :] = (s.g[l, i, self.y, rows, :].astype(F32) + box[i].astype(F32)).astype(BF16)
            return 0

        lax.fori_loop(0, 4, add, 0)
        for i in (1, 2, 3):
            there, device = self.level(i)
            self.send(
                s.g.at[l, there, self.y, rows, :], self.box("from_z", l, stage).at[i - 1], s.g_sems, (l, stage, 3 + i), device
            )

    def reduce_z(self, l, stage):
        s = self.s
        box = self.box("from_z", l, stage)
        rows = self.rows_of(stage, self.core)
        count = STAGES[stage][1]
        for i in (1, 2, 3):
            there, device = self.level(i)
            self.received(s.g.at[l, there, self.y, rows, :], box.at[i - 1], s.g_sems, (l, stage, 3 + i), device)
        total = s.g[l, self.z, self.y, rows, :].astype(F32)
        for i in range(3):
            total = total + box[i].astype(F32)
        first = STAGES[stage][0]

        @pl.when(self.section == l)
        def _():
            s.total[self.core, first : first + count, :] = total

        @pl.when(self.section != l)
        def _():
            s.sum_x[stage, 0:count, :] = total.astype(BF16)

        self.send(
            s.sum_x.at[stage, 0:count, :],
            s.from_x.at[stage, 0:count, :],
            s.g_sems,
            (l, stage, 7),
            self.across,
            when=self.section != l,
        )

    def reduce_x(self, l, stage):
        s = self.s
        first, count = STAGES[stage]
        mine = s.total.at[self.core, first : first + count, :]

        @pl.when(self.section == l)
        def _():
            self.received(
                s.sum_x.at[stage, 0:count, :], s.from_x.at[stage, 0:count, :], s.g_sems, (l, stage, 7), self.across
            )
            mine[...] += s.from_x[stage, 0:count, :].astype(F32)

        self.send(mine, mine, s.g_sems, (l, stage, 8), self.near, when=self.section == l)

    def reduce_last(self, l, stage):
        s = self.s
        first, count = STAGES[stage]
        came = s.total.at[1 - self.core, first : first + count, :]

        @pl.when(self.section == l)
        def _():
            self.received(came, came, s.g_sems, (l, stage, 8), self.near)


def image_kernel(
    x, cot, wide_in, tall_in, vec_in, act, grads, far_act, far_grads, gwide, gtall, gvec_out, *scratch
):
    s = Refs()
    names = [name for name, _, _ in COMPUTE + LINKS] + ["near_sems", "w_sems", "c_sems", "g_sems", "o_sems"]
    flat = list(scratch)
    for name in names:
        if name.endswith("_sems"):
            setattr(s, name, (flat.pop(0), flat.pop(0)))
        else:
            setattr(s, name, flat.pop(0))
    s.wide_in, s.tall_in, s.vec_in = wide_in, tall_in, vec_in
    link, image = Links(s), Image(s)
    A, B, C = 0, 1, 2

    link.barrier()
    link.near_start()
    image.fill_bias()
    link.near_finish()
    for stage in (A, B, C):
        link.gather_across(0, stage)
        link.gather_across(1, stage)
    for stage in (A, B, C):
        link.gather_begin(0, stage)
    link.gather_z(0, A)
    link.gather_y(0, A)
    link.gather_z(0, B)
    link.gather_near(0, A)
    link.gather_begin(1, A)
    image.gains(0)
    image.forward_first(0, x)
    link.gather_y(0, B)
    image.forward_attend(0, 0, 2)
    link.gather_z(0, C)
    link.gather_begin(1, B)
    image.forward_attend(0, 2, WINDOWS)
    link.gather_y(0, C)
    link.gather_begin(1, C)
    link.gather_near(0, B)
    link.gather_near(0, C)
    link.gather_z(1, A)
    image.forward_second(0, x, act.at[0])
    out0 = (act.at[0], far_act, s.o_sems, 0, link.across)
    link.send(*out0, when=link.section == 1)
    link.gather_y(1, A)
    link.gather_z(1, B)
    link.gather_near(1, A)
    image.gains(1)
    image.forward_first(1, act.at[0])
    link.gather_y(1, B)
    image.forward_attend(1, 0, 2)
    link.gather_z(1, C)
    image.forward_attend(1, 2, WINDOWS)
    link.gather_y(1, C)
    link.gather_near(1, B)
    link.gather_near(1, C)
    image.forward_second(1, act.at[0], act.at[1])
    out1 = (act.at[1], far_act, s.o_sems, 0, link.across)
    link.send(*out1, when=link.section == 0)

    image.backward_first(1, cot)
    image.grad_up(1)
    link.reduce_begin(1, C)
    image.grad_tall(1, cot)
    link.reduce_near(1, C)
    link.reduce_begin(1, B)
    image.backward_attend(1, 0, 2)
    link.reduce_near(1, B)
    link.reduce_y(1, C)
    image.backward_attend(1, 2, WINDOWS)
    link.reduce_y(1, B)
    image.backward_last(1, act.at[0], grads.at[1])
    back1 = (grads.at[1], far_grads, s.o_sems, 1, link.across)
    link.send(*back1, when=link.section == 0)
    image.grad_qkv(1)
    link.reduce_begin(1, A)
    link.reduce_z(1, C)
    image.backward_first(0, grads.at[1])
    link.reduce_near(1, A)
    link.reduce_z(1, B)
    link.reduce_x(1, C)
    image.grad_up(0)
    link.reduce_begin(0, C)
    link.reduce_y(1, A)
    image.grad_tall(0, grads.at[1])
    link.reduce_near(0, C)
    link.reduce_begin(0, B)
    link.reduce_x(1, B)
    image.backward_attend(0, 0, 2)
    link.reduce_near(0, B)
    link.reduce_z(1, A)
    link.reduce_y(0, C)
    image.backward_attend(0, 2, WINDOWS)
    link.reduce_y(0, B)
    link.reduce_x(1, A)
    image.backward_last(0, x, grads.at[0])
    back0 = (grads.at[0], far_grads, s.o_sems, 1, link.across)
    link.send(*back0, when=link.section == 1)
    image.grad_qkv(0)
    link.reduce_begin(0, A)
    link.reduce_z(0, C)
    link.reduce_near(0, A)
    link.reduce_z(0, B)
    link.reduce_x(0, C)
    link.reduce_x(0, B)
    link.reduce_y(0, A)
    link.reduce_z(0, A)
    link.reduce_x(0, A)
    for l in range(2):
        for stage in (C, B, A):
            link.reduce_last(l, stage)

    first = link.core == 0
    for block in range(7):
        tiles = [
            qkv_tile(3 * block + i) if block < 3 else up_tile(3 * (block - 3) + i) for i in range(3)
        ]
        rows = jnp.concatenate(
            [s.total[t // 19, (t % 19) * TILE : (t % 19 + 1) * TILE, :] for t in tiles], axis=0
        )
        gwide[:, block * D : (block + 1) * D] = jnp.where(first, rows[0:24], rows[24:48])
    rows = jnp.concatenate(
        [
            s.total[tall_tile(i) // 19, (tall_tile(i) % 19) * TILE : (tall_tile(i) % 19 + 1) * TILE, :]
            for i in range(15)
        ],
        axis=0,
    )
    gtall[...] = jnp.where(first, rows[0:120], rows[120:240])
    at = (vec_tile(0) % 19) * TILE
    gvec_out[...] = jnp.where(first, s.total[0, at : at + TILE, 0:128], s.total[1, at : at + TILE, 0:128])

    link.received(*out0)
    link.received(*back0)
    link.drain()


def one_image(x, cot, wide, tall, vec):
    whole = pl.BlockSpec(memory_space=pltpu.VMEM)
    sems = [
        pltpu.SemaphoreType.DMA(shape)
        for shape in ((3,), (2, 3, 16), (2, 3, 8), (2, 3, 9), (2,))
        for _ in range(2)
    ]
    return pl.pallas_call(
        image_kernel,
        out_shape=(
            jax.ShapeDtypeStruct((2, ROWS, D), BF16),
            jax.ShapeDtypeStruct((2, ROWS, D), BF16),
            jax.ShapeDtypeStruct((ROWS, D), BF16),
            jax.ShapeDtypeStruct((ROWS, D), BF16),
            jax.ShapeDtypeStruct(wide.shape, F32),
            jax.ShapeDtypeStruct(tall.shape, F32),
            jax.ShapeDtypeStruct(vec.shape, F32),
        ),
        in_specs=[whole] * 5,
        out_specs=(whole,) * 7,
        scratch_shapes=[pltpu.VMEM(shape, dtype) for _, shape, dtype in COMPUTE + LINKS] + sems,
        compiler_params=pltpu.CompilerParams(
            vmem_limit_bytes=64 * 2**20, collective_id=0, has_side_effects=True
        ),
        cost_estimate=pl.CostEstimate(flops=18 * 10**9, bytes_accessed=20 * 10**6, transcendentals=10**7),
    )(x, cot, wide, tall, vec)


def adamw(weights, first, second, grads, rate, decay):
    first_new = BETA_ONE * first + (1.0 - BETA_ONE) * grads
    second_new = BETA_TWO * second + (1.0 - BETA_TWO) * grads * grads
    corrected = (
        first_new
        / (1.0 - BETA_ONE**STEP)
        / (jnp.sqrt(second_new / (1.0 - BETA_TWO**STEP)) + ADAM_EPS)
    )
    return (first_new, second_new, weights - rate * (corrected + decay * weights))


def plain_kernel(x, cot, w, act, grads, g, *scratch):
    s = Refs()
    s.w, s.g = w, g
    for (name, _, _), ref in zip(COMPUTE[2:], scratch):
        setattr(s, name, ref)
    image = Image(s)
    image.fill_bias()
    for l, u, out in ((0, x, act.at[0]), (1, act.at[0], act.at[1])):
        image.gains(l)
        image.forward_first(l, u)
        image.forward_attend(l, 0, WINDOWS)
        image.forward_second(l, u, out)
    for l, u, dy, du in ((1, act.at[0], cot, grads.at[1]), (0, x, grads.at[1], grads.at[0])):
        image.backward_first(l, dy)
        image.grad_up(l)
        image.grad_tall(l, dy)
        image.backward_attend(l, 0, WINDOWS)
        image.backward_last(l, u, du)
        image.grad_qkv(l)


def plain_image(x, cot, w):
    whole = pl.BlockSpec(memory_space=pltpu.VMEM)
    return pl.pallas_call(
        plain_kernel,
        out_shape=(
            jax.ShapeDtypeStruct((2, ROWS, D), BF16),
            jax.ShapeDtypeStruct((2, ROWS, D), BF16),
            jax.ShapeDtypeStruct(w.shape, BF16),
        ),
        in_specs=[whole] * 3,
        out_specs=(whole,) * 3,
        scratch_shapes=[pltpu.VMEM(shape, dtype) for _, shape, dtype in COMPUTE[2:]],
        compiler_params=pltpu.CompilerParams(vmem_limit_bytes=64 * 2**20),
    )(x, cot, w)


def tile_order():
    wide = [qkv_tile(i) for i in range(9)] + [up_tile(i) for i in range(12)]
    return wide + [tall_tile(i) for i in range(15)] + [vec_tile(half) for half in range(2)]


def any_mesh(
    inputs, cotangent, wide_weights, wide_first, wide_second, tall_weights, tall_first, tall_second,
    vectors, vector_first, vector_second,
):
    section = lax.axis_index("section")
    both = ("section", "dp")
    wide = lax.all_gather(wide_weights[0].astype(BF16), both, axis=0, tiled=True)
    tall = lax.all_gather(tall_weights[0].astype(BF16), both, axis=0, tiled=True)
    vec = lax.all_gather(lax.all_gather(vectors[0].astype(BF16), "dp", axis=1, tiled=True), "section", axis=0)
    vec_rows, width = vec.shape[1], D // (2 * SLOTS)
    order = tile_order()
    place = sorted(range(len(order)), key=order.__getitem__)
    wide = wide.reshape(2, SLOTS, 3, TILE, 7, D).transpose(0, 1, 4, 2, 3, 5).reshape(2, SLOTS, 21, TILE, D)
    tall = tall.reshape(2, SLOTS, 15, TILE, D)
    vec = vec.reshape(2, vec_rows, SLOTS, 2, width).transpose(0, 2, 3, 1, 4)
    vec = jnp.pad(vec, ((0, 0),) * 3 + ((0, TILE - vec_rows), (0, D - width)))
    tiles = jnp.concatenate((wide, tall, vec), axis=2)[:, :, jnp.array(place)]
    act, grads, g = plain_image(
        own_rows(inputs, section), own_rows(cotangent, section), tiles.reshape(2, SLOTS // 2, 2, 2 * HALF, D)
    )
    far_act, far_grads = (
        lax.ppermute(lax.dynamic_index_in_dim(array, 1 - section, keepdims=False), "section", [(0, 1), (1, 0)])
        for array in (act, grads)
    )
    g = g.reshape(2, SLOTS, len(order), TILE, D)[:, :, jnp.array(order)].astype(F32)
    wide = g[:, :, :21].reshape(2, SLOTS, 7, 3, TILE, D).transpose(0, 1, 3, 4, 2, 5).reshape(2, D, 7 * D)
    tall = g[:, :, 21:36].reshape(2, D + FF, D)
    vec = g[:, :, 36:, :vec_rows, :width].transpose(0, 3, 1, 2, 4).reshape(2, vec_rows, D)

    def reduced(array, dim):
        array = lax.psum_scatter(array, "section", scatter_dimension=0, tiled=False)
        return lax.psum_scatter(array, "dp", scatter_dimension=dim, tiled=True)

    return finish(
        section, act, grads, far_act, far_grads, reduced(wide, 0), reduced(tall, 0), reduced(vec, 1),
        wide_weights, wide_first, wide_second, tall_weights, tall_first, tall_second, vectors, vector_first, vector_second,
    )


def own_rows(array, section):
    return jnp.pad(lax.dynamic_slice_in_dim(array, section * IMG_TOK, IMG_TOK), ((0, ROWS - IMG_TOK), (0, 0)))


def finish(
    section, act, grads, far_act, far_grads, total_wide, total_tall, total_vec,
    wide_weights, wide_first, wide_second, tall_weights, tall_first, tall_second, vectors, vector_first, vector_second,
):
    def joined(array, other):
        mine = lax.dynamic_index_in_dim(array, section, keepdims=False)[:IMG_TOK]
        other = other[:IMG_TOK]
        return jnp.where(section == 0, jnp.concatenate((mine, other)), jnp.concatenate((other, mine)))

    wide_m, wide_s, wide_n = adamw(wide_weights[0], wide_first[0], wide_second[0], total_wide, RATE_MATRIX, DECAY)
    tall_m, tall_s, tall_n = adamw(tall_weights[0], tall_first[0], tall_second[0], total_tall, RATE_MATRIX, DECAY)
    vec_m, vec_s, vec_n = adamw(vectors[0], vector_first[0], vector_second[0], total_vec, RATE_VECTOR, 0.0)
    outs = (joined(act, far_act), joined(grads, far_grads), wide_m, wide_s, wide_n, tall_m, tall_s, tall_n, vec_m, vec_s, vec_n)
    return tuple(out[None] for out in outs)


def per_device(
    inputs, cotangent, wide_weights, wide_first, wide_second, tall_weights, tall_first, tall_second,
    vectors, vector_first, vector_second,
):
    section = lax.axis_index("section")
    rows, width = vectors.shape[1:]
    vec = jnp.pad(vectors[0], ((0, TILE - rows), (0, 128 - width)))
    act, grads, far_act, far_grads, total_wide, total_tall, total_vec = one_image(
        own_rows(inputs, section), own_rows(cotangent, section), wide_weights[0], tall_weights[0], vec
    )
    return finish(
        section, act, grads, far_act, far_grads, total_wide, total_tall, total_vec[:rows, :width],
        wide_weights, wide_first, wide_second, tall_weights, tall_first, tall_second, vectors, vector_first, vector_second,
    )


def solution(mesh):
    data = P("dp", None)
    matrix = P("section", "dp", None)
    vector = P("section", None, "dp")
    in_specs = (data, data) + (matrix,) * 6 + (vector,) * 3
    out_specs = (matrix,) * 8 + (vector,) * 3
    device_fn = per_device if mesh.shape["dp"] == 2 * SLOTS else any_mesh
    return jax.shard_map(device_fn, mesh=mesh, in_specs=in_specs, out_specs=out_specs, check_vma=False)
```

```python
import functools

import jax
import jax.numpy as jnp
from jax import lax
from jax.experimental import pallas as pl
from jax.experimental.pallas import tpu as pltpu
from jax.sharding import PartitionSpec as P

D = 384
HEADS = 6
HEAD_DIM = 64
FF = 1536
GLOBAL = 2
GLOBAL_LEN = 197
LOCAL = 10
LOCAL_LEN = 37
STEP = 5
IMG_TOK = GLOBAL * GLOBAL_LEN + LOCAL * LOCAL_LEN

NORM_EPS = 1e-06
BETA_ONE = 0.5
BETA_TWO = 0.5
ADAM_EPS = 1e-08
RATE_MATRIX = 0.05
RATE_VECTOR = 0.2
DECAY = 0.05
ERF_SCALE = 0.7071067811865476
DENSITY_SCALE = 0.3989422804014327

ROWS = 768
BLOCK = 768
BLOCKS = ROWS // BLOCK
WINDOW = 208
WINDOWS = 4
UNROLL = 2
CHUNK = 512
CHUNKS = FF // CHUNK
TILE = 16
SLOTS = 8
HALF = 19 * TILE
STAGES = ((0, 3 * TILE), (3 * TILE, 3 * TILE), (6 * TILE, 7 * TILE), (13 * TILE, 6 * TILE))
MESH = pl.DeviceIdType.MESH
F32 = jnp.float32
BF16 = jnp.bfloat16


def window_start(index):
    if isinstance(index, int):
        return min(index * 192, ROWS - WINDOW)
    return pl.multiple_of(jnp.minimum(index * 192, ROWS - WINDOW), 16)


def row_segment(row):
    local = ((row - GLOBAL * GLOBAL_LEN) * 1772) >> 16
    segment = jnp.where(row < GLOBAL * GLOBAL_LEN, jnp.where(row < GLOBAL_LEN, 0, 1), local + GLOBAL)
    return jnp.where(row < IMG_TOK, segment, 99)


def window_of(segment):
    return jnp.where(segment < 2, segment, jnp.where(segment < 7, 2, jnp.where(segment < 12, 3, 9)))


def dot(a, b):
    return jnp.dot(a, b, preferred_element_type=F32)


def dot_t(a, b):
    return lax.dot_general(a, b, (((1,), (1,)), ((), ())), preferred_element_type=F32)


def t_dot(a, b):
    return lax.dot_general(a, b, (((0,), (0,)), ((), ())), preferred_element_type=F32)


def standard(values):
    centre = values - jnp.mean(values, axis=-1, keepdims=True)
    inverse = lax.rsqrt(jnp.mean(centre * centre, axis=-1, keepdims=True) + NORM_EPS)
    return centre * inverse, inverse


def norm_back(normed, inverse, gain, incoming):
    scaled = incoming * gain
    return inverse * (
        scaled
        - jnp.mean(scaled, axis=-1, keepdims=True)
        - normed * jnp.mean(scaled * normed, axis=-1, keepdims=True)
    )


def gelu_pair(f):
    below = 0.5 + 0.5 * lax.erf(f * ERF_SCALE)
    return f * below, below + f * jnp.exp(-0.5 * f * f) * DENSITY_SCALE


def column_sum(values):
    return jnp.sum(values, axis=0, keepdims=True)


def qkv_tile(i):
    return i if i < 5 else 19 + i - 5


def tall_tile(i):
    return 6 + i if i < 7 else (23 if i == 7 else 25 + i - 8)


def up_tile(i):
    return 13 + i if i < 6 else 32 + i - 6


def vec_tile(half):
    return 19 * half + 5


def runs(tiles):
    out = []
    for slot, tile in tiles:
        if out and out[-1][0] == slot and out[-1][1] + out[-1][2] == tile * TILE:
            out[-1][2] += TILE
        else:
            out.append([slot, tile * TILE, TILE])
    return out


def wide_tiles(name, block):
    return [(k, name(3 * block + i)) for k in range(SLOTS) for i in range(3)]


def tall_tiles(first, count):
    per = 15
    return [(t // per, tall_tile(t % per)) for t in range(first // TILE, (first + count) // TILE)]


def load_rows(ref, l, tiles, lanes=slice(0, D)):
    return jnp.concatenate(
        [ref[l, slot // 2, slot % 2, row : row + count, lanes] for slot, row, count in runs(tiles)], axis=0
    )


def store_rows(ref, l, tiles, value):
    done = 0
    for slot, row, count in runs(tiles):
        ref[l, slot // 2, slot % 2, row : row + count, :] = value[done : done + count]
        done += count


def load_qkv(w, l):
    return jnp.concatenate([load_rows(w, l, wide_tiles(qkv_tile, b)) for b in range(3)], axis=1)


def load_up(w, l, j):
    parts, at = [], j * CHUNK
    while at < (j + 1) * CHUNK:
        block, lane = divmod(at, D)
        take = min(D - lane, (j + 1) * CHUNK - at)
        parts.append(load_rows(w, l, wide_tiles(up_tile, block), slice(lane, lane + take)))
        at += take
    return jnp.concatenate(parts, axis=1)


def load_proj(w, l):
    return load_rows(w, l, tall_tiles(0, D))


def load_down(w, l, j):
    return load_rows(w, l, tall_tiles(D + j * CHUNK, CHUNK))


def row_block(i):
    if isinstance(i, int):
        return pl.ds(i * BLOCK, BLOCK)
    return pl.ds(pl.multiple_of(i * BLOCK, BLOCK), BLOCK)


def steps(count, step, then=None):
    def body(i, carry):
        step(i, carry)
        for at, action in (then or {}).items():
            pl.when(i == at)(action)
        return 0

    if count == 1:
        step(0, 0)
        for action in (then or {}).values():
            action()
        return
    lax.fori_loop(0, count, body, 0)


def windows(window, then=None):
    def step(i, _):
        for j in range(UNROLL):
            window(i * UNROLL + j)

    grouped = {}
    for at, action in (then or {}).items():
        grouped.setdefault(at // UNROLL, []).append(action)
    if UNROLL == WINDOWS:
        for w in range(WINDOWS):
            window(w)
            if then and w in then:
                then[w]()
        return
    steps(WINDOWS // UNROLL, step, {at: lambda made=made: [action() for action in made] and None for at, made in grouped.items()})


class Image:
    def __init__(self, s):
        self.s = s
        self.low = None

    def gains(self, l):
        s = self.s
        lane = lax.broadcasted_iota(jnp.int32, (TILE, 128), 1)
        tiles = [jnp.zeros((TILE, 128), F32) for _ in range(D // 128)]
        for slot in range(SLOTS):
            for half in range(2):
                row = vec_tile(half) * TILE
                part = s.w[l, slot // 2, slot % 2, row : row + TILE, 0:128].astype(F32)
                width = D // (2 * SLOTS)
                at = (2 * slot + half) * width
                index, shift = divmod(at, 128)
                moved = pltpu.roll(part, shift, 1) if shift else part
                if shift + width > 128:
                    tiles[index] = tiles[index] + jnp.where(lane >= shift, moved, 0.0)
                    tiles[index + 1] = tiles[index + 1] + jnp.where(lane < shift, moved, 0.0)
                else:
                    tiles[index] = tiles[index] + moved
        for index, tile in enumerate(tiles):
            s.vec[l, :, index * 128 : (index + 1) * 128] = tile
        for j in range(FF // D):
            s.bup[l, 0:1, j * D : (j + 1) * D] = s.vec[l, 8 + j : 9 + j, :]

    def spread_gains(self, l):
        s = self.s
        lane = lax.broadcasted_iota(jnp.int32, (TILE, 128), 1)
        width = D // (2 * SLOTS)
        for slot in range(SLOTS):
            for half in range(2):
                at = (2 * slot + half) * width
                index, shift = divmod(at, 128)
                tile = s.gvec[l, :, index * 128 : (index + 1) * 128]
                if shift + width > 128:
                    tile = jnp.where(lane >= shift, tile, s.gvec[l, :, (index + 1) * 128 : (index + 2) * 128])
                moved = pltpu.roll(tile, 128 - shift, 1) if shift else tile
                moved = jnp.where(lane < width, moved, 0.0).astype(BF16)
                row = vec_tile(half) * TILE
                s.g[l, slot // 2, slot % 2, row : row + TILE, :] = jnp.concatenate(
                    (moved, jnp.zeros((TILE, D - 128), BF16)), axis=1
                )

    def window_bias(self, w):
        start = window_start(w)
        key = row_segment(start + lax.broadcasted_iota(jnp.int32, (WINDOW, 1), 0))
        query = row_segment(start + lax.broadcasted_iota(jnp.int32, (1, WINDOW), 1))
        inside = (key == query) & (window_of(key) == w)
        return jnp.where(inside, 0.0, -1e30).astype(F32)

    def forward_first(self, l, u_ref, then=None):
        s = self.s

        def step(i, _):
            rows = row_block(i)
            normed, _unused = standard(u_ref[rows, :].astype(F32))
            a = (normed * s.vec[l, 0:1, :] + s.vec[l, 1:2, :]).astype(BF16)
            s.a[l, rows, :] = a
            part = dot(a, load_qkv(s.w, l))
            s.qkv[l, rows, 0:D] = (part[:, 0:D] + s.vec[l, 2:3, :]).astype(BF16) * jnp.asarray(HEAD_DIM**-0.5, BF16)
            s.qkv[l, rows, D : 2 * D] = part[:, D : 2 * D].astype(BF16)
            s.qkv[l, rows, 2 * D :] = (part[:, 2 * D :] + s.vec[l, 3:4, :]).astype(BF16)
            return 0

        steps(BLOCKS, step, then)

    def forward_attend(self, l, then=None):
        s = self.s
        s.o[l] = jnp.zeros((ROWS, D), BF16)
        low = lax.broadcasted_iota(jnp.int32, (1, 128), 1) < HEAD_DIM

        def window(w):
            rows = pl.ds(window_start(w), WINDOW)
            bias = self.window_bias(w)
            for pair in range(HEADS // 2):
                base = pair * 128
                q = s.qkv[l, rows, base : base + 128]
                k = s.qkv[l, rows, D + base : D + base + 128]
                v = s.qkv[l, rows, 2 * D + base : 2 * D + base + 128]
                total = None
                for half in range(2):
                    keep = low if half == 0 else jnp.logical_not(low)
                    scores = dot_t(jnp.where(keep, k, jnp.zeros_like(k)), q) + bias
                    top = jnp.maximum(jnp.max(scores, axis=0, keepdims=True), -1e20)
                    weights = jnp.exp(scores - top)
                    summed = jnp.sum(weights, axis=0, keepdims=True)
                    weights = (weights * (1.0 / jnp.maximum(summed, 1e-20))).astype(BF16)
                    s.p[l, w, 2 * pair + half] = weights
                    part = t_dot(weights, jnp.where(keep, v, jnp.zeros_like(v)))
                    total = part if total is None else total + part
                old = s.o[l, rows, base : base + 128]
                s.o[l, rows, base : base + 128] = old + total.astype(BF16)

        windows(window, then)

    def forward_second(self, l, u_ref, out_ref, then=None):
        s = self.s

        def step(i, _):
            rows = row_block(i)
            hidden = u_ref[rows, :].astype(F32) + dot(s.o[l, rows, :], load_proj(s.w, l)) + s.vec[l, 4:5, :]
            s.h[l, rows, :] = hidden
            normed, _unused = standard(hidden)
            c = (normed * s.vec[l, 5:6, :] + s.vec[l, 6:7, :]).astype(BF16)
            s.c[l, rows, :] = c
            total = hidden + s.vec[l, 7:8, :]
            for j in range(CHUNKS):
                cols = slice(j * CHUNK, (j + 1) * CHUNK)
                f = dot(c, load_up(s.w, l, j)) + s.bup[l, 0:1, cols]
                value, slope = gelu_pair(f)
                z = value.astype(BF16)
                s.z[l, rows, cols] = z
                s.slope[l, rows, cols] = slope.astype(BF16)
                total = total + dot(z, load_down(s.w, l, j))
            out_ref[rows, :] = total.astype(BF16)
            return 0

        steps(BLOCKS, step, then)

    def backward_first(self, l, dy_ref, then=None):
        s = self.s
        s.gvec[l] = jnp.zeros_like(s.gvec[l])
        s.dbup[...] = jnp.zeros_like(s.dbup)

        def step(i, _):
            rows = row_block(i)
            dy = dy_ref[rows, :]
            dc = jnp.zeros((BLOCK, D), F32)
            for j in range(CHUNKS):
                cols = slice(j * CHUNK, (j + 1) * CHUNK)
                dz = dot_t(dy, load_down(s.w, l, j))
                df = (dz * s.slope[l, rows, cols].astype(F32)).astype(BF16)
                s.df[rows, cols] = df
                s.dbup[0:1, cols] += column_sum(df.astype(F32))
                dc = dc + dot_t(df, load_up(s.w, l, j))
            normed, inverse = standard(s.h[l, rows, :])
            top = dy.astype(F32)
            dh = top + norm_back(normed, inverse, s.vec[l, 5:6, :], dc)
            s.dh[rows, :] = dh
            dhb = dh.astype(BF16)
            s.dhb[rows, :] = dhb
            s.dout[rows, :] = dot_t(dhb, load_proj(s.w, l)).astype(BF16)
            s.gvec[l, 4:5, :] += column_sum(dhb.astype(F32))
            s.gvec[l, 5:6, :] += column_sum(dc * normed)
            s.gvec[l, 6:7, :] += column_sum(dc)
            s.gvec[l, 7:8, :] += column_sum(top)
            return 0

        steps(BLOCKS, step, then)
        for j in range(FF // D):
            s.gvec[l, 8 + j : 9 + j, :] = s.dbup[0:1, j * D : (j + 1) * D]

    def grad_up(self, l):
        s = self.s
        for b in range(0, FF // D, 2):
            value = t_dot(s.c[l], s.df[:, b * D : (b + 2) * D]).astype(BF16)
            store_rows(s.g, l, wide_tiles(up_tile, b), value[:, :D])
            store_rows(s.g, l, wide_tiles(up_tile, b + 1), value[:, D:])

    def grad_tall(self, l, dy_ref):
        s = self.s
        for j in range(FF // 512):
            value = t_dot(dy_ref[...], s.z[l, :, j * 512 : (j + 1) * 512])
            store_rows(s.g, l, tall_tiles(D + j * 512, 512), value.T.astype(BF16))
        store_rows(s.g, l, tall_tiles(0, D), t_dot(s.o[l], s.dhb[...]).astype(BF16))

    def backward_attend(self, l, then=None):
        s = self.s
        s.dqkv[...] = jnp.zeros_like(s.dqkv)
        low = lax.broadcasted_iota(jnp.int32, (1, 128), 1) < HEAD_DIM

        def window(w):
            rows = pl.ds(window_start(w), WINDOW)
            for pair in range(HEADS // 2):
                base = pair * 128
                q = s.qkv[l, rows, base : base + 128]
                k = s.qkv[l, rows, D + base : D + base + 128]
                v = s.qkv[l, rows, 2 * D + base : 2 * D + base + 128]
                grad = s.dout[rows, base : base + 128]
                dq = dk = dv = None
                for half in range(2):
                    keep = low if half == 0 else jnp.logical_not(low)

                    def only(x, keep=keep):
                        return jnp.where(keep, x, jnp.zeros_like(x))

                    weights = s.p[l, w, 2 * pair + half]
                    grad_half = only(grad)
                    dv_part = dot(weights, grad_half)
                    dp = dot_t(v, grad_half)
                    wide_weights = weights.astype(F32)
                    product = dp * wide_weights
                    ds = (product - wide_weights * jnp.sum(product, axis=0, keepdims=True)).astype(BF16)
                    dk_part = dot(ds, only(q))
                    dq_part = t_dot(only(k), ds)
                    if half == 0:
                        dq, dk, dv = dq_part, dk_part, dv_part
                    else:
                        dq, dk, dv = dq + dq_part, dk + dk_part, dv + dv_part
                for offset, value in ((0, (dq * HEAD_DIM**-0.5).T), (D, dk), (2 * D, dv)):
                    cols = slice(offset + base, offset + base + 128)
                    s.dqkv[rows, cols] = s.dqkv[rows, cols] + value.astype(BF16)

        windows(window, then)

    def backward_last(self, l, u_ref, du_ref, then=None):
        s = self.s

        def step(i, _):
            rows = row_block(i)
            dqkv = s.dqkv[rows, :]
            da = dot_t(dqkv, load_qkv(s.w, l))
            normed, inverse = standard(u_ref[rows, :].astype(F32))
            du = s.dh[rows, :] + norm_back(normed, inverse, s.vec[l, 0:1, :], da)
            du_ref[rows, :] = du.astype(BF16)
            s.gvec[l, 0:1, :] += column_sum(da * normed)
            s.gvec[l, 1:2, :] += column_sum(da)
            s.gvec[l, 2:3, :] += column_sum(dqkv[:, 0:D].astype(F32))
            s.gvec[l, 3:4, :] += column_sum(dqkv[:, 2 * D : 3 * D].astype(F32))
            return 0

        steps(BLOCKS, step, then)
        self.spread_gains(l)

    def grad_qkv(self, l):
        s = self.s
        value = t_dot(s.a[l], s.dqkv[...]).astype(BF16)
        for b in range(3):
            store_rows(s.g, l, wide_tiles(qkv_tile, b), value[:, b * D : (b + 1) * D])


COMPUTE = (
    ("w", (2, 4, 2, 2 * HALF, D), BF16),
    ("g", (2, 4, 2, 2 * HALF, D), BF16),
    ("vec", (2, TILE, D), F32),
    ("gvec", (2, TILE, D), F32),
    ("a", (2, ROWS, D), BF16),
    ("qkv", (2, ROWS, 3 * D), BF16),
    ("o", (2, ROWS, D), BF16),
    ("h", (2, ROWS, D), F32),
    ("c", (2, ROWS, D), BF16),
    ("z", (2, ROWS, FF), BF16),
    ("slope", (2, ROWS, FF), BF16),
    ("p", (2, WINDOWS, HEADS, WINDOW, WINDOW), BF16),
    ("bup", (2, 8, FF), F32),
    ("dbup", (8, FF), F32),
    ("df", (ROWS, FF), BF16),
    ("dh", (ROWS, D), F32),
    ("dhb", (ROWS, D), BF16),
    ("dout", (ROWS, D), BF16),
    ("dqkv", (ROWS, 3 * D), BF16),
)
LINKS = (
    ("x", (ROWS, D), BF16),
    ("cot", (ROWS, D), BF16),
    ("whole", (2 * IMG_TOK, D), BF16),
    ("act", (2, ROWS, D), BF16),
    ("grads", (2, ROWS, D), BF16),
    ("near_wide", (D // (2 * SLOTS), 3 * D + FF), F32),
    ("near_tall", ((D + FF) // (2 * SLOTS), D), F32),
    ("near_vec", (12, 1, D // (2 * SLOTS)), F32),
    ("total", (2, HALF, D), F32),
) + tuple(
    (f"{name}{st}", (count, STAGES[st][1], D), BF16)
    for st in range(len(STAGES))
    for name, count in (("sum_x", 1), ("from_x", 1), ("from_xy", 4), ("from_xz", 4))
) + tuple(
    (f"{name}{l}{st}", count + (STAGES[st][1], D), BF16)
    for l in range(2)
    for st in range(len(STAGES))
    for name, count in (("from_c", (4, 2)), ("from_y", (4,)), ("from_z", (3,)))
)


class Refs:
    pass


G0, G1, G2, G3, G4, R0, R1, R1X, R2, R2X, R3, R3X, R4 = range(13)
GAINS, FIRST, ATTEND, SECOND, BACK_FIRST, GRAD_UP, GRAD_TALL, BACK_ATTEND, LAST, GRAD_QKV = range(13, 23)
BY_X, BY_Y, BY_Z = range(3)
GATHER = (
    (((BY_Z, BY_X), (BY_X, BY_Y)), ((BY_X, BY_Y), (BY_X, BY_X)), ((BY_X, BY_X), (BY_X, BY_X)), ((BY_Z, BY_Y), (BY_Z, BY_Y))),
    (((BY_X, BY_X), (BY_X, BY_X)), ((BY_X, BY_Y), (BY_X, BY_Y)), ((BY_Z, BY_X), (BY_Z, BY_X)), ((BY_X, BY_Y), (BY_Z, BY_Y))),
)
REDUCE = (
    (((BY_Z, BY_Y), (BY_Z, BY_Y)), ((BY_X, BY_Y), (BY_X, BY_X)), ((BY_Z, BY_Y), (BY_Z, BY_Y)), ((BY_Z, BY_X), (BY_Z, BY_X))),
    (((BY_X, BY_X), (BY_Z, BY_X)), ((BY_X, BY_X), (BY_X, BY_X)), ((BY_Z, BY_X), (BY_Z, BY_Y)), ((BY_Z, BY_Y), (BY_Z, BY_Y))),
)
PLAN = (
    (G0, 0, 0, True),
    (G0, 0, 1, True),
    (G0, 0, 2, True),
    (G0, 0, 3, True),
    (G0, 1, 2, True),
    (G1, 0, 0, False),
    (G1, 0, 1, False),
    (G1, 1, 2, False),
    (G1, 0, 0, True),
    (G1, 0, 2, False),
    (G1, 0, 3, False),
    (G1, 0, 1, True),
    (G0, 1, 0, True),
    (G1, 1, 2, True),
    (G2, 0, 0, True),
    (G1, 1, 0, False),
    (G4, 0, 0, True),
    (G2, 0, 1, False),
    (G2, 0, 0, False),
    (G2, 0, 1, True),
    (G4, 0, 1, True),
    (G1, 0, 2, True),
    (G0, 1, 1, True),
    (G1, 1, 1, False),
    (G2, 1, 2, True),
    (G4, 1, 2, True),
    (G2, 0, 3, False),
    (G3, 0, 1, False),
    (G3, 0, 0, False),
    (G4, 0, 1, False),
    (G4, 0, 0, False),
    (G1, 1, 0, True),
    (G2, 0, 2, True),
    (G2, 0, 2, False),
    (G1, 0, 3, True),
    (G0, 1, 3, True),
    (GAINS, 0, ()),
    (FIRST, 0, ()),
    (G4, 0, 2, True),
    (ATTEND, 0, ((0, G2, 1, 0, False), (1, G1, 1, 1, True), (1, G3, 0, 3, False), (2, G1, 1, 3, False),)),
    (G2, 1, 0, True),
    (G4, 0, 3, False),
    (G2, 0, 3, True),
    (G4, 1, 0, True),
    (G4, 0, 3, True),
    (G2, 1, 1, False),
    (G3, 0, 2, False),
    (G2, 1, 2, False),
    (G3, 1, 2, False),
    (G4, 0, 2, False),
    (G1, 1, 3, True),
    (G2, 1, 1, True),
    (SECOND, 0, ()),
    (G4, 1, 2, False),
    (G4, 1, 1, True),
    (G3, 1, 0, False),
    (G3, 1, 1, False),
    (G2, 1, 3, False),
    (G4, 1, 0, False),
    (G4, 1, 1, False),
    (GAINS, 1, ()),
    (FIRST, 1, ()),
    (G2, 1, 3, True),
    (ATTEND, 1, ((2, G4, 1, 3, True),)),
    (G3, 1, 3, False),
    (G4, 1, 3, False),
    (SECOND, 1, ()),
    (BACK_FIRST, 1, ()),
    (GRAD_UP, 1, ()),
    (R0, 1, 3, None),
    (GRAD_TALL, 1, ()),
    (R0, 1, 2, None),
    (BACK_ATTEND, 1, ((0, R1, 1, 3, None), (1, R1, 1, 2, None),)),
    (LAST, 1, ()),
    (GRAD_QKV, 1, ()),
    (R0, 1, 0, None),
    (R0, 1, 1, None),
    (BACK_FIRST, 0, ()),
    (R2, 1, 3, True),
    (R1, 1, 0, None),
    (R2, 1, 3, False),
    (R1, 1, 1, None),
    (GRAD_UP, 0, ()),
    (R2, 1, 2, False),
    (R0, 0, 3, None),
    (GRAD_TALL, 0, ()),
    (R1X, 1, 2, True),
    (R3, 1, 0, False),
    (R0, 0, 2, None),
    (BACK_ATTEND, 0, ((0, R1, 0, 3, None), (1, R1, 0, 2, None), (2, R3, 1, 3, True),)),
    (R2, 1, 2, True),
    (LAST, 0, ()),
    (R3, 1, 3, False),
    (R1X, 0, 3, True),
    (GRAD_QKV, 0, ()),
    (R0, 0, 0, None),
    (R0, 0, 1, None),
    (R3, 0, 3, False),
    (R1, 0, 0, None),
    (R3, 1, 2, False),
    (R1, 0, 1, None),
    (R2, 0, 2, False),
    (R2, 0, 2, True),
    (R1X, 1, 0, True),
    (R2, 0, 0, False),
    (R2, 0, 1, False),
    (R3, 1, 2, True),
    (R2, 0, 3, True),
    (R2, 1, 0, True),
    (R2X, 1, 0, True),
    (R1X, 1, 1, True),
    (R3, 0, 2, True),
    (R2, 0, 0, True),
    (R3X, 1, 3, True),
    (R2, 1, 1, True),
    (R2X, 1, 1, True),
    (R3, 0, 2, False),
    (R1X, 0, 1, True),
    (R4, 1, 3, True),
    (R3X, 1, 2, True),
    (R4, 1, 2, True),
    (R3, 0, 3, True),
    (R3X, 0, 3, True),
    (R3, 0, 0, False),
    (R2, 0, 1, True),
    (R2X, 0, 1, True),
    (R3X, 0, 2, True),
    (R3, 0, 0, True),
    (R3X, 0, 0, True),
    (R3, 1, 0, True),
    (R3X, 1, 0, True),
    (R3, 0, 1, True),
    (R3, 1, 1, True),
    (R4, 1, 1, True),
    (R4, 1, 0, True),
    (R4, 0, 3, True),
    (R4, 0, 2, True),
    (R4, 0, 1, True),
    (R4, 0, 0, True),
)


class Links:
    def __init__(self, s):
        self.s = s
        self.section = lax.axis_index("section")
        self.dp = lax.axis_index("dp")
        self.z, self.y, self.core = self.dp // 4, (self.dp // 2) % 2, self.dp % 2
        self.near = (self.section, self.dp + 1 - 2 * self.core)
        self.across = (1 - self.section, self.dp)
        self.beside = (self.section, self.dp + 2 - 4 * self.y)
        self.pending = []

    def level(self, steps):
        there = (self.z + steps) % 4
        return there, (self.section, self.dp + 4 * (there - self.z))

    def barrier(self):
        sem = pltpu.get_barrier_semaphore()
        others = [self.near, self.across, self.beside] + [self.level(i)[1] for i in (1, 2, 3)]
        for device in others:
            pl.semaphore_signal(sem, inc=1, device_id=device, device_id_type=MESH)
        pl.semaphore_wait(sem, len(others))

    def copy(self, src, dst, sems, index, device):
        return pltpu.make_async_remote_copy(
            src_ref=src,
            dst_ref=dst,
            send_sem=sems[0].at[index],
            recv_sem=sems[1].at[index],
            device_id=device,
            device_id_type=MESH,
        )

    def send(self, make, when=None):
        self.pending.append((make, when))
        self.copy(*make()).start()

    def received(self, make):
        self.copy(*make()).wait_recv()

    def drain(self):
        for make, when in self.pending:
            if when is None:
                self.copy(*make()).wait_send()
            else:
                pl.when(when)(lambda make=make: self.copy(*make()).wait_send())


    def rows_of(self, stage, core):
        first, count = STAGES[stage]
        return pl.ds(pl.multiple_of(core * HALF + first, TILE), count)

    def w_part(self, l, z, y, stage, core):
        return self.s.w.at[l, z, y, self.rows_of(stage, core), :]

    def box(self, name, l, stage):
        return getattr(self.s, f"{name}{l}{stage}")


    def shard(self):
        s = self.s
        return ((s.wide_in.at[0], s.near_wide), (s.tall_in.at[0], s.near_tall), (s.vec_in, s.near_vec))

    def near_start(self):
        for index, (src, dst) in enumerate(self.shard()):
            self.send(lambda src=src, dst=dst, index=index: (src, dst, self.s.near_sems, index, self.near))

    def near_finish(self):
        s = self.s
        for index, (src, dst) in enumerate(self.shard()):
            self.received(lambda: (src, dst, s.near_sems, index, self.near))
        first = self.core == 0

        def pair(own, near):
            return jnp.where(first, own, near), jnp.where(first, near, own)

        def put(tile, value):
            s.w[self.section, self.z, self.y, tile * TILE : (tile + 1) * TILE, :] = value

        rows = jnp.concatenate(pair(s.wide_in[0], s.near_wide[...]), axis=0).astype(BF16)
        for block in range(7):
            for i in range(3):
                tile = qkv_tile(3 * block + i) if block < 3 else up_tile(3 * (block - 3) + i)
                put(tile, rows[i * TILE : (i + 1) * TILE, block * D : (block + 1) * D])
        rows = jnp.concatenate(pair(s.tall_in[0], s.near_tall[...]), axis=0).astype(BF16)
        for i in range(15):
            put(tall_tile(i), rows[i * TILE : (i + 1) * TILE])
        count, _, width = s.near_vec.shape
        s.padded[...] = jnp.zeros_like(s.padded)
        for i in range(count):
            for half, value in enumerate(pair(s.vec_in[i], s.near_vec[i])):
                s.padded[half, i : i + 1, 0:width] = value
        for half in range(2):
            put(vec_tile(half), s.padded[half].astype(BF16))

    def place(self, tag, l, stage, coming):
        s = self.s
        kind, i = tag[:-1], int(tag[-1])
        back = self.level(4 - i)[0] if i else self.z
        core = 1 - self.core if coming and kind[0] == "n" else self.core
        if kind == "z":
            slot, device, index = (back if coming else self.z, self.y), self.level(i)[1], 1 + i
        elif kind == "y":
            slot, device, index = (back, 1 - self.y if coming else self.y), self.beside, 8 + i
        elif kind == "x":
            slot, device, index = (self.z, self.y), self.across, 0
        elif kind == "n":
            slot, device, index = (self.z, self.y), self.near, 1
        else:
            slot = (back, self.y if kind[1] == "z" else 1 - self.y)
            device = self.across if kind[0] == "x" else self.near
            index = {"nz": 4, "ny": 12, "xz": 15, "xy": 19}[kind] + i
        part = self.w_part(l, slot[0], slot[1], stage, core)
        return part, part, s.w_sems, (l, stage, index), device

    def gather(self, name, l, stage, owner, zs, ys):
        three, four = (1, 2, 3), (0, 1, 2, 3)
        if name == G0:
            return [((), ("x0", "z1", "z2", "z3", "y0"))] if owner else []
        if name == G1:
            if owner:
                return [((f"z{i}",), (f"y{i}", f"nz{i}") + ((f"xz{i}",) if zs == BY_X else ())) for i in three]
            sends = ("n0",) + (("z1", "z2", "z3") if zs == BY_Z else ()) + (("y0",) if ys == BY_Y else ())
            return [(("x0",), sends)]
        if name == G2:
            if owner:
                return [((f"y{i}",), (f"ny{i}",) + ((f"xy{i}",) if ys == BY_X else ())) for i in four]
            source = "z" if zs == BY_Z else "xz"
            return [((f"{source}{i}",), (f"nz{i}",) + ((f"y{i}",) if ys == BY_Y else ())) for i in three]
        if name == G3:
            source = "y" if ys == BY_Y else "xy"
            return [] if owner else [((f"{source}{i}",), (f"ny{i}",)) for i in four]
        waits = tuple(f"nz{i}" for i in three) + tuple(f"ny{i}" for i in four)
        return [(waits + (() if owner else ("n0",)), ())]

    def condition(self, l, owner, core):
        when = self.section == l if owner else self.section != l
        return when if core is None else when & (self.core == core)

    def do(self, name, l, stage, side):
        config = (GATHER if name <= G4 else REDUCE)[l][stage]
        if name == R0:
            self.send(lambda: self.sum_copy("c", l, stage))
            return
        if name == R1:
            self.received(lambda: self.sum_copy("c", l, stage))
            self.add_near(l, stage)
        cores = (None,) if config[0] == config[1] else (0, 1)
        for owner in (True, False) if side is None else (side,):
            for core in cores:
                zs, ys = config[core or 0]
                when = self.conditions[l, owner, core]
                if name <= G4:
                    todo = self.gather(name, l, stage, owner, zs, ys)
                    make = self.place
                else:
                    todo = self.reduce(name, l, stage, owner, zs, ys)
                    make = None
                if not todo:
                    continue

                def act(todo=todo, when=when):
                    for entry in todo:
                        waits, sends = entry[0], entry[-1]
                        for tag in waits:
                            if make is None:
                                self.received(lambda: self.sum_copy(tag, l, stage))
                            else:
                                self.received(lambda: self.place(tag, l, stage, True))
                        if len(entry) == 3:
                            entry[1]()
                        for tag in sends:
                            if make is None:
                                self.send(lambda tag=tag: self.sum_copy(tag, l, stage), when)
                            else:
                                self.send(lambda tag=tag: self.place(tag, l, stage, False), when)

                pl.when(when)(act)


    def sum_copy(self, tag, l, stage):
        s = self.s
        rows = self.rows_of(stage, self.core)
        first, count = STAGES[stage]
        if tag == "c":
            src = s.g.at[l, :, :, self.rows_of(stage, 1 - self.core), :]
            return src, self.box("from_c", l, stage), s.g_sems, (l, stage, 0), self.near
        if tag == "Y":
            return s.g.at[l, :, 1 - self.y, rows, :], self.box("from_y", l, stage), s.g_sems, (l, stage, 1), self.beside
        if tag == "XY":
            return s.g.at[l, :, 1 - self.y, rows, :], self.box("from_xy", "", stage), s.g_sems, (l, stage, 5), self.across
        if tag == "XZ":
            return s.g.at[l, :, self.y, rows, :], self.box("from_xz", "", stage), s.g_sems, (l, stage, 6), self.across
        if tag == "X":
            return self.box("sum_x", "", stage), self.box("from_x", "", stage), s.g_sems, (l, stage, 7), self.across
        if tag == "T":
            mine = s.total.at[self.core, first : first + count, :]
            return mine, mine, s.g_sems, (l, stage, 8), self.near
        there, device = self.level(int(tag[1]))
        return (
            s.g.at[l, there, self.y, rows, :],
            self.box("from_z", l, stage).at[int(tag[1]) - 1],
            s.g_sems,
            (l, stage, 1 + int(tag[1])),
            device,
        )

    def add_near(self, l, stage):
        s = self.s
        rows, box = self.rows_of(stage, self.core), self.box("from_c", l, stage)

        def add(i, _):
            z, y = i // 2, i % 2
            s.g[l, z, y, rows, :] = (s.g[l, z, y, rows, :].astype(F32) + box[z, y].astype(F32)).astype(BF16)
            return 0

        lax.fori_loop(0, SLOTS, add, 0)

    def add_column(self, name, l, stage, y):
        s = self.s
        rows = self.rows_of(stage, self.core)

        def add(i, _):
            s.g[l, i, y, rows, :] = (s.g[l, i, y, rows, :].astype(F32) + name[i].astype(F32)).astype(BF16)
            return 0

        lax.fori_loop(0, 4, add, 0)

    def add_levels(self, l, stage):
        box = self.box("from_z", l, stage)
        total = self.s.g[l, self.z, self.y, self.rows_of(stage, self.core), :].astype(F32)
        for i in range(3):
            total = total + box[i].astype(F32)
        return total

    def reduce(self, name, l, stage, owner, zs, ys):
        s = self.s
        first, count = STAGES[stage]
        levels = ("Z1", "Z2", "Z3")
        down = levels if zs == BY_Z else ("XZ",)

        def column(name, y, layer):
            return lambda: self.add_column(self.box(name, layer, stage), l, stage, y)

        def keep():
            s.total[self.core, first : first + count, :] = self.add_levels(l, stage)

        def pass_on():
            self.box("sum_x", "", stage)[0] = self.add_levels(l, stage).astype(BF16)

        def last():
            s.total[self.core, first : first + count, :] += self.box("from_x", "", stage)[0].astype(F32)

        if name == R1:
            if ys == BY_Y:
                return [((), ("Y",))]
            return [] if owner else [((), ("XY",) + down)]
        if name == R1X:
            return [(("XY",), column("from_xy", 1 - self.y, ""), ("Y",))] if owner and ys == BY_X else []
        if name == R2:
            if owner:
                return [(("Y",), column("from_y", self.y, l), levels if zs == BY_Z else ())]
            return [(("Y",), column("from_y", self.y, l), down)] if ys == BY_Y else []
        if name == R2X:
            return [(("XZ",), column("from_xz", self.y, ""), levels)] if owner and zs == BY_X else []
        if name == R3:
            if owner:
                return [(levels, keep, ("T",) if zs == BY_X else ())]
            return [(levels, pass_on, ("X",))] if zs == BY_Z else []
        if name == R3X:
            return [(("X",), last, ("T",))] if owner and zs == BY_Z else []
        return [(("T",), ())] if owner else []


def take_rows(section, whole, out):
    edge = IMG_TOK // TILE * TILE

    @pl.when(section == 0)
    def _():
        out[0:edge, :] = whole[0:edge, :]
        row = lax.broadcasted_iota(jnp.int32, (ROWS - edge, D), 0)
        out[edge:ROWS, :] = jnp.where(row < IMG_TOK - edge, whole[edge:ROWS, :].astype(F32), 0.0).astype(BF16)

    @pl.when(section == 1)
    def _():
        rows = whole[edge : 2 * IMG_TOK, :].astype(F32)
        rows = jnp.concatenate((rows[IMG_TOK - edge :], jnp.zeros((ROWS - IMG_TOK, D), F32)), axis=0)
        out[...] = rows.astype(BF16)


def image_kernel(
    inputs, cotangent, wide_in, tall_in, vec_in, own_act, own_grads, far_act, far_grads, total_out, *scratch
):
    s = Refs()
    names = [name for name, _, _ in COMPUTE + LINKS] + ["padded", "near_sems", "w_sems", "g_sems", "o_sems", "local_sems"]
    flat = list(scratch)
    for name in names:
        if name in ("near_sems", "w_sems", "g_sems", "o_sems"):
            setattr(s, name, (flat.pop(0), flat.pop(0)))
        else:
            setattr(s, name, flat.pop(0))
    s.wide_in, s.tall_in, s.vec_in = wide_in, tall_in, vec_in
    link, image = Links(s), Image(s)
    section = link.section
    link.conditions = {
        (l, owner, core): link.condition(l, owner, core)
        for l in range(2)
        for owner in (True, False)
        for core in (None, 0, 1)
    }

    def bring(array, index):
        return pltpu.make_async_copy(array, s.whole, s.local_sems.at[index])

    def keep(array, out, index):
        return pltpu.make_async_copy(array.at[section], out, s.local_sems.at[index])

    def thirds(array, out, l, which, i):
        rows = slice(i * BLOCK, (i + 1) * BLOCK)
        return lambda: (array.at[l, rows, :], out.at[rows, :], s.o_sems, (which, i), link.across)

    def share(array, out, l, which):
        def after(i):
            def action():
                when = link.conditions[l, False, None]
                pl.when(when)(lambda: link.send(thirds(array, out, l, which, i), when))

            return action

        return after

    def compute(name, l, then):
        u = s.x if l == 0 else s.act.at[0]
        dy = s.cot if l == 1 else s.grads.at[1]
        if name == GAINS:
            image.gains(l)
        elif name == FIRST:
            image.forward_first(l, u, then)
        elif name == ATTEND:
            image.forward_attend(l, then)
        elif name == SECOND:
            image.forward_second(l, u, s.act.at[l], then)
        elif name == BACK_FIRST:
            image.backward_first(l, dy, then)
        elif name == GRAD_UP:
            image.grad_up(l)
        elif name == GRAD_TALL:
            image.grad_tall(l, dy)
        elif name == BACK_ATTEND:
            image.backward_attend(l, then)
        elif name == LAST:
            image.backward_last(l, u, s.grads.at[l], then)
        elif name == GRAD_QKV:
            image.grad_qkv(l)

    bring(inputs, 0).start()
    link.barrier()
    link.near_start()
    bring(inputs, 0).wait()
    take_rows(section, s.whole, s.x)
    bring(cotangent, 1).start()
    link.near_finish()
    fresh = True
    for entry in PLAN:
        if entry[0] < GAINS:
            link.do(*entry)
            continue
        if entry[0] == FIRST and fresh:
            bring(cotangent, 1).wait()
            take_rows(section, s.whole, s.cot)
            fresh = False
        name, l, hooks = entry
        then = {}
        after = None
        if name == SECOND:
            after = share(s.act, far_act, l, 0)
        if name == LAST:
            after = share(s.grads, far_grads, l, 1)
        for i in range(WINDOWS):
            actions = ([after(i)] if after and i < BLOCKS else []) + [functools.partial(link.do, *hook[1:]) for hook in hooks if hook[0] == i]
            if actions:
                then[i] = lambda actions=actions: [action() for action in actions] and None
        compute(name, l, then)
        if entry[:2] == (SECOND, 1):
            keep(s.act, own_act, 2).start()
    keep(s.grads, own_grads, 3).start()
    put = pltpu.make_async_copy(s.total, total_out, s.local_sems.at[4])
    put.start()
    for which, array, out in ((0, s.act, far_act), (1, s.grads, far_grads)):
        for i in range(BLOCKS):
            link.received(thirds(array, out, 0, which, i))
    link.drain()
    keep(s.act, own_act, 2).wait()
    keep(s.grads, own_grads, 3).wait()
    put.wait()


def one_image(inputs, cotangent, wide, tall, vec):
    whole = pl.BlockSpec(memory_space=pltpu.VMEM)
    anywhere = pl.BlockSpec(memory_space=pl.ANY)
    sems = [
        pltpu.SemaphoreType.DMA(shape)
        for shape in ((3,), (2, len(STAGES), 23), (2, len(STAGES), 9), (2, 3))
        for _ in range(2)
    ] + [pltpu.SemaphoreType.DMA((5,))]
    rows = jax.ShapeDtypeStruct((ROWS, D), BF16)
    return pl.pallas_call(
        image_kernel,
        out_shape=[rows, rows, rows, rows, jax.ShapeDtypeStruct((2, HALF, D), F32)],
        in_specs=[anywhere] * 2 + [whole] * 3,
        out_specs=[anywhere] * 5,
        scratch_shapes=[pltpu.VMEM(shape, dtype) for _, shape, dtype in COMPUTE + LINKS]
        + [pltpu.VMEM((2, TILE, D), F32)]
        + sems,
        compiler_params=pltpu.CompilerParams(
            vmem_limit_bytes=64 * 2**20, collective_id=0, has_side_effects=True
        ),
        cost_estimate=pl.CostEstimate(flops=18 * 10**9, bytes_accessed=20 * 10**6, transcendentals=10**7),
    )(inputs, cotangent, wide, tall, vec)


def plain_kernel(x, cot, w, act, grads, g, *scratch):
    s = Refs()
    s.w, s.g = w, g
    for (name, _, _), ref in zip(COMPUTE[2:], scratch):
        setattr(s, name, ref)
    image = Image(s)
    for l, u, out in ((0, x, act.at[0]), (1, act.at[0], act.at[1])):
        image.gains(l)
        image.forward_first(l, u)
        image.forward_attend(l)
        image.forward_second(l, u, out)
    for l, u, dy, du in ((1, act.at[0], cot, grads.at[1]), (0, x, grads.at[1], grads.at[0])):
        image.backward_first(l, dy)
        image.grad_up(l)
        image.grad_tall(l, dy)
        image.backward_attend(l)
        image.backward_last(l, u, du)
        image.grad_qkv(l)


def plain_image(x, cot, w):
    whole = pl.BlockSpec(memory_space=pltpu.VMEM)
    return pl.pallas_call(
        plain_kernel,
        out_shape=(
            jax.ShapeDtypeStruct((2, ROWS, D), BF16),
            jax.ShapeDtypeStruct((2, ROWS, D), BF16),
            jax.ShapeDtypeStruct(w.shape, BF16),
        ),
        in_specs=[whole] * 3,
        out_specs=(whole,) * 3,
        scratch_shapes=[pltpu.VMEM(shape, dtype) for _, shape, dtype in COMPUTE[2:]],
        compiler_params=pltpu.CompilerParams(vmem_limit_bytes=64 * 2**20),
    )(x, cot, w)


def tile_order():
    wide = [qkv_tile(i) for i in range(9)] + [up_tile(i) for i in range(12)]
    return wide + [tall_tile(i) for i in range(15)] + [vec_tile(half) for half in range(2)]


def any_mesh(
    inputs, cotangent, wide_weights, wide_first, wide_second, tall_weights, tall_first, tall_second,
    vectors, vector_first, vector_second,
):
    section = lax.axis_index("section")
    both = ("section", "dp")
    wide = lax.all_gather(wide_weights[0].astype(BF16), both, axis=0, tiled=True)
    tall = lax.all_gather(tall_weights[0].astype(BF16), both, axis=0, tiled=True)
    vec = lax.all_gather(lax.all_gather(vectors[0].astype(BF16), "dp", axis=1, tiled=True), "section", axis=0)
    vec_rows, width = vec.shape[1], D // (2 * SLOTS)
    order = tile_order()
    place = sorted(range(len(order)), key=order.__getitem__)
    wide = wide.reshape(2, SLOTS, 3, TILE, 7, D).transpose(0, 1, 4, 2, 3, 5).reshape(2, SLOTS, 21, TILE, D)
    tall = tall.reshape(2, SLOTS, 15, TILE, D)
    vec = vec.reshape(2, vec_rows, SLOTS, 2, width).transpose(0, 2, 3, 1, 4)
    vec = jnp.pad(vec, ((0, 0),) * 3 + ((0, TILE - vec_rows), (0, D - width)))
    tiles = jnp.concatenate((wide, tall, vec), axis=2)[:, :, jnp.array(place)]
    act, grads, g = plain_image(
        own_rows(inputs, section), own_rows(cotangent, section), tiles.reshape(2, SLOTS // 2, 2, 2 * HALF, D)
    )
    far_act, far_grads = (
        lax.ppermute(lax.dynamic_index_in_dim(array, 1 - section, keepdims=False), "section", [(0, 1), (1, 0)])
        for array in (act, grads)
    )
    g = g.reshape(2, SLOTS, len(order), TILE, D)[:, :, jnp.array(order)].astype(F32)
    wide = g[:, :, :21].reshape(2, SLOTS, 7, 3, TILE, D).transpose(0, 1, 3, 4, 2, 5).reshape(2, D, 7 * D)
    tall = g[:, :, 21:36].reshape(2, D + FF, D)
    vec = g[:, :, 36:, :vec_rows, :width].transpose(0, 3, 1, 2, 4).reshape(2, vec_rows, D)

    def reduced(array, dim):
        array = lax.psum_scatter(array, "section", scatter_dimension=0, tiled=False)
        return lax.psum_scatter(array, "dp", scatter_dimension=dim, tiled=True)

    return finish(
        section, act, grads, far_act, far_grads, reduced(wide, 0), reduced(tall, 0), reduced(vec, 1),
        wide_weights, wide_first, wide_second, tall_weights, tall_first, tall_second, vectors, vector_first, vector_second,
    )


def adamw(weights, first, second, grads, rate, decay):
    first_new = BETA_ONE * first + (1.0 - BETA_ONE) * grads
    second_new = BETA_TWO * second + (1.0 - BETA_TWO) * grads * grads
    corrected = (
        first_new
        / (1.0 - BETA_ONE**STEP)
        / (jnp.sqrt(second_new / (1.0 - BETA_TWO**STEP)) + ADAM_EPS)
    )
    return (first_new, second_new, weights - rate * (corrected + decay * weights))


def own_rows(array, section):
    return jnp.pad(lax.dynamic_slice_in_dim(array, section * IMG_TOK, IMG_TOK), ((0, ROWS - IMG_TOK), (0, 0)))


def finish(
    section, act, grads, far_act, far_grads, total_wide, total_tall, total_vec,
    wide_weights, wide_first, wide_second, tall_weights, tall_first, tall_second, vectors, vector_first, vector_second,
):
    def joined(array, other):
        mine = lax.dynamic_index_in_dim(array, section, keepdims=False)[:IMG_TOK]
        other = other[:IMG_TOK]
        return jnp.where(section == 0, jnp.concatenate((mine, other)), jnp.concatenate((other, mine)))

    wide_m, wide_s, wide_n = adamw(wide_weights[0], wide_first[0], wide_second[0], total_wide, RATE_MATRIX, DECAY)
    tall_m, tall_s, tall_n = adamw(tall_weights[0], tall_first[0], tall_second[0], total_tall, RATE_MATRIX, DECAY)
    vec_m, vec_s, vec_n = adamw(vectors[0], vector_first[0], vector_second[0], total_vec, RATE_VECTOR, 0.0)
    outs = (joined(act, far_act), joined(grads, far_grads), wide_m, wide_s, wide_n, tall_m, tall_s, tall_n, vec_m, vec_s, vec_n)
    return tuple(out[None] for out in outs)


OWN_ROWS = ("own_act", "own_grads", "far_act", "far_grads", "total")
MASTERS = ("wide_w", "wide_m", "wide_s", "tall_w", "tall_m", "tall_s", "vec_w", "vec_m", "vec_s")
RESULTS = ("act", "grads", "wide_m1", "wide_s1", "wide_w1", "tall_m1", "tall_s1", "tall_w1", "vec_m1", "vec_s1", "vec_w1")


def finish_kernel(*refs):
    names = OWN_ROWS + MASTERS
    given, results = refs[: len(names)], refs[len(names) : len(names) + len(RESULTS)]
    held = refs[len(names) + len(RESULTS) : -2]
    came, left = refs[-2:]
    section = lax.axis_index("section")
    first = lax.axis_index("dp") % 2 == 0
    s = Refs()
    copies = {}
    for index, (name, src, dst) in enumerate(zip(names, given, held)):
        setattr(s, name, dst)
        copies[name] = pltpu.make_async_copy(src, dst, came.at[index])
    for index, (name, src, dst) in enumerate(zip(RESULTS, held[len(names) :], results)):
        setattr(s, name, src)
        copies[name] = pltpu.make_async_copy(src, dst, left.at[index])
    for name in names:
        copies[name].start()

    def fetch(*wanted):
        for name in wanted:
            copies[name].wait()

    def put(*done):
        for name in done:
            copies[name].start()

    edge = IMG_TOK // TILE * TILE

    def join(low, high, out):
        out[0, 0:edge, :] = low[0:edge, :]
        rows = jnp.concatenate((low[edge:IMG_TOK, :].astype(F32), high[0:IMG_TOK, :].astype(F32)), axis=0)
        out[0, edge : 2 * IMG_TOK, :] = rows.astype(BF16)

    for own, far, out in (("own_act", "far_act", "act"), ("own_grads", "far_grads", "grads")):
        fetch(own, far)
        pl.when(section == 0)(lambda: join(getattr(s, own), getattr(s, far), getattr(s, out)))
        pl.when(section == 1)(lambda: join(getattr(s, far), getattr(s, own), getattr(s, out)))
        put(out)

    def tile(i):
        return s.total[i // 19, (i % 19) * TILE : (i % 19 + 1) * TILE, :]

    def own_half(rows):
        half = rows.shape[0] // 2
        return jnp.where(first, rows[:half], rows[half:])

    fetch("total", "wide_w", "wide_m", "wide_s")
    for block in range(7):
        tiles = [qkv_tile(3 * block + i) if block < 3 else up_tile(3 * (block - 3) + i) for i in range(3)]
        g = own_half(jnp.concatenate([tile(i) for i in tiles], axis=0))
        cols = slice(block * D, (block + 1) * D)
        s.wide_m1[0, :, cols], s.wide_s1[0, :, cols], s.wide_w1[0, :, cols] = adamw(
            s.wide_w[0, :, cols], s.wide_m[0, :, cols], s.wide_s[0, :, cols], g, RATE_MATRIX, DECAY
        )
    put("wide_m1", "wide_s1", "wide_w1")
    fetch("tall_w", "tall_m", "tall_s")
    g = own_half(jnp.concatenate([tile(tall_tile(i)) for i in range(15)], axis=0))
    s.tall_m1[0], s.tall_s1[0], s.tall_w1[0] = adamw(s.tall_w[0], s.tall_m[0], s.tall_s[0], g, RATE_MATRIX, DECAY)
    put("tall_m1", "tall_s1", "tall_w1")
    fetch("vec_w", "vec_m", "vec_s")
    count, _, width = s.vec_w.shape
    g = jnp.where(first, tile(vec_tile(0)), tile(vec_tile(1)))[0:count, 0:width]
    for i in range(count):
        s.vec_m1[i], s.vec_s1[i], s.vec_w1[i] = adamw(
            s.vec_w[i], s.vec_m[i], s.vec_s[i], g[i : i + 1], RATE_VECTOR, 0.0
        )
    put("vec_m1", "vec_s1", "vec_w1")
    for name in RESULTS:
        copies[name].wait()


def per_device(
    inputs, cotangent, wide_weights, wide_first, wide_second, tall_weights, tall_first, tall_second,
    vectors, vector_first, vector_second,
):
    vectors, vector_first, vector_second = (
        jnp.transpose(array, (1, 0, 2)) for array in (vectors, vector_first, vector_second)
    )
    sums = one_image(inputs, cotangent, wide_weights, tall_weights, vectors)
    given = list(sums) + [
        wide_weights, wide_first, wide_second, tall_weights, tall_first, tall_second, vectors, vector_first, vector_second,
    ]
    anywhere = pl.BlockSpec(memory_space=pl.ANY)
    rows = jax.ShapeDtypeStruct((1,) + inputs.shape, BF16)
    outs = [rows, rows] + [
        jax.ShapeDtypeStruct(array.shape, F32) for array in (wide_weights,) * 3 + (tall_weights,) * 3 + (vectors,) * 3
    ]
    results = pl.pallas_call(
        finish_kernel,
        out_shape=outs,
        in_specs=[anywhere] * len(given),
        out_specs=[anywhere] * len(outs),
        scratch_shapes=[pltpu.VMEM(array.shape, array.dtype) for array in given + outs]
        + [pltpu.SemaphoreType.DMA((len(given),)), pltpu.SemaphoreType.DMA((len(outs),))],
        compiler_params=pltpu.CompilerParams(vmem_limit_bytes=64 * 2**20),
        cost_estimate=pl.CostEstimate(flops=10**7, bytes_accessed=10**7, transcendentals=10**6),
    )(*given)
    return tuple(results[:8]) + tuple(jnp.transpose(array, (1, 0, 2)) for array in results[8:])


def solution(mesh):
    data = P("dp", None)
    matrix = P("section", "dp", None)
    vector = P("section", None, "dp")
    in_specs = (data, data) + (matrix,) * 6 + (vector,) * 3
    out_specs = (matrix,) * 8 + (vector,) * 3
    device_fn = per_device if mesh.shape["dp"] == 2 * SLOTS else any_mesh
    return jax.shard_map(device_fn, mesh=mesh, in_specs=in_specs, out_specs=out_specs, check_vma=False)
```

```python
import functools

import jax
import jax.numpy as jnp
from jax import lax
from jax.experimental import pallas as pl
from jax.experimental.pallas import tpu as pltpu
from jax.sharding import PartitionSpec as P

D = 384
HEADS = 6
HEAD_DIM = 64
FF = 1536
GLOBAL = 2
GLOBAL_LEN = 197
LOCAL = 10
LOCAL_LEN = 37
STEP = 5
IMG_TOK = GLOBAL * GLOBAL_LEN + LOCAL * LOCAL_LEN

NORM_EPS = 1e-06
BETA_ONE = 0.5
BETA_TWO = 0.5
ADAM_EPS = 1e-08
RATE_MATRIX = 0.05
RATE_VECTOR = 0.2
DECAY = 0.05
ERF_SCALE = 0.7071067811865476
DENSITY_SCALE = 0.3989422804014327

ROWS = 768
BLOCK = 768
BLOCKS = ROWS // BLOCK
WINDOW = 208
WINDOWS = 4
UNROLL = 2
CHUNK = 512
CHUNKS = FF // CHUNK
TILE = 16
SLOTS = 8
HALF = 19 * TILE
STAGES = ((0, 3 * TILE), (3 * TILE, 3 * TILE), (6 * TILE, 7 * TILE), (13 * TILE, 6 * TILE))
MESH = pl.DeviceIdType.MESH
F32 = jnp.float32
BF16 = jnp.bfloat16


def window_start(index):
    if isinstance(index, int):
        return min(index * 192, ROWS - WINDOW)
    return pl.multiple_of(jnp.minimum(index * 192, ROWS - WINDOW), 16)


def row_segment(row):
    local = ((row - GLOBAL * GLOBAL_LEN) * 1772) >> 16
    segment = jnp.where(row < GLOBAL * GLOBAL_LEN, jnp.where(row < GLOBAL_LEN, 0, 1), local + GLOBAL)
    return jnp.where(row < IMG_TOK, segment, 99)


def window_of(segment):
    return jnp.where(segment < 2, segment, jnp.where(segment < 7, 2, jnp.where(segment < 12, 3, 9)))


def dot(a, b):
    return jnp.dot(a, b, preferred_element_type=F32)


def dot_t(a, b):
    return lax.dot_general(a, b, (((1,), (1,)), ((), ())), preferred_element_type=F32)


def t_dot(a, b):
    return lax.dot_general(a, b, (((0,), (0,)), ((), ())), preferred_element_type=F32)


def standard(values):
    centre = values - jnp.mean(values, axis=-1, keepdims=True)
    inverse = lax.rsqrt(jnp.mean(centre * centre, axis=-1, keepdims=True) + NORM_EPS)
    return centre * inverse, inverse


def norm_back(normed, inverse, gain, incoming):
    scaled = incoming * gain
    return inverse * (
        scaled
        - jnp.mean(scaled, axis=-1, keepdims=True)
        - normed * jnp.mean(scaled * normed, axis=-1, keepdims=True)
    )


def gelu_pair(f):
    below = 0.5 + 0.5 * lax.erf(f * ERF_SCALE)
    return f * below, below + f * jnp.exp(-0.5 * f * f) * DENSITY_SCALE


def column_sum(values):
    return jnp.sum(values, axis=0, keepdims=True)


def qkv_tile(i):
    return i if i < 5 else 19 + i - 5


def tall_tile(i):
    return 6 + i if i < 7 else (23 if i == 7 else 25 + i - 8)


def up_tile(i):
    return 13 + i if i < 6 else 32 + i - 6


def vec_tile(half):
    return 19 * half + 5


def runs(tiles):
    out = []
    for slot, tile in tiles:
        if out and out[-1][0] == slot and out[-1][1] + out[-1][2] == tile * TILE:
            out[-1][2] += TILE
        else:
            out.append([slot, tile * TILE, TILE])
    return out


def wide_tiles(name, block):
    return [(k, name(3 * block + i)) for k in range(SLOTS) for i in range(3)]


def tall_tiles(first, count):
    per = 15
    return [(t // per, tall_tile(t % per)) for t in range(first // TILE, (first + count) // TILE)]


def load_rows(ref, l, tiles, lanes=slice(0, D)):
    return jnp.concatenate(
        [ref[l, slot // 2, slot % 2, row : row + count, lanes] for slot, row, count in runs(tiles)], axis=0
    )


def store_rows(ref, l, tiles, value):
    done = 0
    for slot, row, count in runs(tiles):
        ref[l, slot // 2, slot % 2, row : row + count, :] = value[done : done + count]
        done += count


def load_qkv(w, l):
    return jnp.concatenate([load_rows(w, l, wide_tiles(qkv_tile, b)) for b in range(3)], axis=1)


def load_up(w, l, j):
    parts, at = [], j * CHUNK
    while at < (j + 1) * CHUNK:
        block, lane = divmod(at, D)
        take = min(D - lane, (j + 1) * CHUNK - at)
        parts.append(load_rows(w, l, wide_tiles(up_tile, block), slice(lane, lane + take)))
        at += take
    return jnp.concatenate(parts, axis=1)


def load_proj(w, l):
    return load_rows(w, l, tall_tiles(0, D))


def load_down(w, l, j):
    return load_rows(w, l, tall_tiles(D + j * CHUNK, CHUNK))


def row_block(i):
    if isinstance(i, int):
        return pl.ds(i * BLOCK, BLOCK)
    return pl.ds(pl.multiple_of(i * BLOCK, BLOCK), BLOCK)


def steps(count, step, then=None):
    def body(i, carry):
        step(i, carry)
        for at, action in (then or {}).items():
            pl.when(i == at)(action)
        return 0

    if count == 1:
        step(0, 0)
        for action in (then or {}).values():
            action()
        return
    lax.fori_loop(0, count, body, 0)


def windows(window, then=None):
    def step(i, _):
        for j in range(UNROLL):
            window(i * UNROLL + j)

    steps(WINDOWS // UNROLL, step, then)


class Image:
    def __init__(self, s):
        self.s = s
        self.low = None

    def gains(self, l):
        s = self.s
        lane = lax.broadcasted_iota(jnp.int32, (TILE, 128), 1)
        tiles = [jnp.zeros((TILE, 128), F32) for _ in range(D // 128)]
        for slot in range(SLOTS):
            for half in range(2):
                row = vec_tile(half) * TILE
                part = s.w[l, slot // 2, slot % 2, row : row + TILE, 0:128].astype(F32)
                width = D // (2 * SLOTS)
                at = (2 * slot + half) * width
                index, shift = divmod(at, 128)
                moved = pltpu.roll(part, shift, 1) if shift else part
                if shift + width > 128:
                    tiles[index] = tiles[index] + jnp.where(lane >= shift, moved, 0.0)
                    tiles[index + 1] = tiles[index + 1] + jnp.where(lane < shift, moved, 0.0)
                else:
                    tiles[index] = tiles[index] + moved
        for index, tile in enumerate(tiles):
            s.vec[l, :, index * 128 : (index + 1) * 128] = tile
        for j in range(FF // D):
            s.bup[l, 0:1, j * D : (j + 1) * D] = s.vec[l, 8 + j : 9 + j, :]

    def spread_gains(self, l):
        s = self.s
        lane = lax.broadcasted_iota(jnp.int32, (TILE, 128), 1)
        width = D // (2 * SLOTS)
        for slot in range(SLOTS):
            for half in range(2):
                at = (2 * slot + half) * width
                index, shift = divmod(at, 128)
                tile = s.gvec[l, :, index * 128 : (index + 1) * 128]
                if shift + width > 128:
                    tile = jnp.where(lane >= shift, tile, s.gvec[l, :, (index + 1) * 128 : (index + 2) * 128])
                moved = pltpu.roll(tile, 128 - shift, 1) if shift else tile
                moved = jnp.where(lane < width, moved, 0.0).astype(BF16)
                row = vec_tile(half) * TILE
                s.g[l, slot // 2, slot % 2, row : row + TILE, :] = jnp.concatenate(
                    (moved, jnp.zeros((TILE, D - 128), BF16)), axis=1
                )

    def window_bias(self, w):
        start = window_start(w)
        key = row_segment(start + lax.broadcasted_iota(jnp.int32, (WINDOW, 1), 0))
        query = row_segment(start + lax.broadcasted_iota(jnp.int32, (1, WINDOW), 1))
        inside = (key == query) & (window_of(key) == w)
        return jnp.where(inside, 0.0, -1e30).astype(F32)

    def forward_first(self, l, u_ref, then=None):
        s = self.s

        def step(i, _):
            rows = row_block(i)
            normed, _unused = standard(u_ref[rows, :].astype(F32))
            a = (normed * s.vec[l, 0:1, :] + s.vec[l, 1:2, :]).astype(BF16)
            s.a[l, rows, :] = a
            part = dot(a, load_qkv(s.w, l))
            s.qkv[l, rows, 0:D] = (part[:, 0:D] + s.vec[l, 2:3, :]).astype(BF16) * jnp.asarray(HEAD_DIM**-0.5, BF16)
            s.qkv[l, rows, D : 2 * D] = part[:, D : 2 * D].astype(BF16)
            s.qkv[l, rows, 2 * D :] = (part[:, 2 * D :] + s.vec[l, 3:4, :]).astype(BF16)
            return 0

        steps(BLOCKS, step, then)

    def forward_attend(self, l, then=None):
        s = self.s
        s.o[l] = jnp.zeros((ROWS, D), BF16)
        low = lax.broadcasted_iota(jnp.int32, (1, 128), 1) < HEAD_DIM

        def window(w):
            rows = pl.ds(window_start(w), WINDOW)
            bias = self.window_bias(w)
            for pair in range(HEADS // 2):
                base = pair * 128
                q = s.qkv[l, rows, base : base + 128]
                k = s.qkv[l, rows, D + base : D + base + 128]
                v = s.qkv[l, rows, 2 * D + base : 2 * D + base + 128]
                total = None
                for half in range(2):
                    keep = low if half == 0 else jnp.logical_not(low)
                    scores = dot_t(jnp.where(keep, k, jnp.zeros_like(k)), q) + bias
                    top = jnp.maximum(jnp.max(scores, axis=0, keepdims=True), -1e20)
                    weights = jnp.exp(scores - top)
                    summed = jnp.sum(weights, axis=0, keepdims=True)
                    weights = (weights * (1.0 / jnp.maximum(summed, 1e-20))).astype(BF16)
                    s.p[l, w, 2 * pair + half] = weights
                    part = t_dot(weights, jnp.where(keep, v, jnp.zeros_like(v)))
                    total = part if total is None else total + part
                old = s.o[l, rows, base : base + 128]
                s.o[l, rows, base : base + 128] = old + total.astype(BF16)

        windows(window, then)

    def forward_second(self, l, u_ref, out_ref, then=None):
        s = self.s

        def step(i, _):
            rows = row_block(i)
            hidden = u_ref[rows, :].astype(F32) + dot(s.o[l, rows, :], load_proj(s.w, l)) + s.vec[l, 4:5, :]
            s.h[l, rows, :] = hidden
            normed, _unused = standard(hidden)
            c = (normed * s.vec[l, 5:6, :] + s.vec[l, 6:7, :]).astype(BF16)
            s.c[l, rows, :] = c
            total = hidden + s.vec[l, 7:8, :]
            for j in range(CHUNKS):
                cols = slice(j * CHUNK, (j + 1) * CHUNK)
                f = dot(c, load_up(s.w, l, j)) + s.bup[l, 0:1, cols]
                value, slope = gelu_pair(f)
                z = value.astype(BF16)
                s.z[l, rows, cols] = z
                s.slope[l, rows, cols] = slope.astype(BF16)
                total = total + dot(z, load_down(s.w, l, j))
            out_ref[rows, :] = total.astype(BF16)
            return 0

        steps(BLOCKS, step, then)

    def backward_first(self, l, dy_ref, then=None):
        s = self.s
        s.gvec[l] = jnp.zeros_like(s.gvec[l])
        s.dbup[...] = jnp.zeros_like(s.dbup)

        def step(i, _):
            rows = row_block(i)
            dy = dy_ref[rows, :]
            dc = jnp.zeros((BLOCK, D), F32)
            for j in range(CHUNKS):
                cols = slice(j * CHUNK, (j + 1) * CHUNK)
                dz = dot_t(dy, load_down(s.w, l, j))
                df = (dz * s.slope[l, rows, cols].astype(F32)).astype(BF16)
                s.df[rows, cols] = df
                s.dbup[0:1, cols] += column_sum(df.astype(F32))
                dc = dc + dot_t(df, load_up(s.w, l, j))
            normed, inverse = standard(s.h[l, rows, :])
            top = dy.astype(F32)
            dh = top + norm_back(normed, inverse, s.vec[l, 5:6, :], dc)
            s.dh[rows, :] = dh
            dhb = dh.astype(BF16)
            s.dhb[rows, :] = dhb
            s.dout[rows, :] = dot_t(dhb, load_proj(s.w, l)).astype(BF16)
            s.gvec[l, 4:5, :] += column_sum(dhb.astype(F32))
            s.gvec[l, 5:6, :] += column_sum(dc * normed)
            s.gvec[l, 6:7, :] += column_sum(dc)
            s.gvec[l, 7:8, :] += column_sum(top)
            return 0

        steps(BLOCKS, step, then)
        for j in range(FF // D):
            s.gvec[l, 8 + j : 9 + j, :] = s.dbup[0:1, j * D : (j + 1) * D]

    def grad_up(self, l):
        s = self.s
        for b in range(0, FF // D, 2):
            value = t_dot(s.c[l], s.df[:, b * D : (b + 2) * D]).astype(BF16)
            store_rows(s.g, l, wide_tiles(up_tile, b), value[:, :D])
            store_rows(s.g, l, wide_tiles(up_tile, b + 1), value[:, D:])

    def grad_tall(self, l, dy_ref):
        s = self.s
        for j in range(FF // 512):
            value = t_dot(dy_ref[...], s.z[l, :, j * 512 : (j + 1) * 512])
            store_rows(s.g, l, tall_tiles(D + j * 512, 512), value.T.astype(BF16))
        store_rows(s.g, l, tall_tiles(0, D), t_dot(s.o[l], s.dhb[...]).astype(BF16))

    def backward_attend(self, l, then=None):
        s = self.s
        s.dqkv[...] = jnp.zeros_like(s.dqkv)
        low = lax.broadcasted_iota(jnp.int32, (1, 128), 1) < HEAD_DIM

        def window(w):
            rows = pl.ds(window_start(w), WINDOW)
            for pair in range(HEADS // 2):
                base = pair * 128
                q = s.qkv[l, rows, base : base + 128]
                k = s.qkv[l, rows, D + base : D + base + 128]
                v = s.qkv[l, rows, 2 * D + base : 2 * D + base + 128]
                grad = s.dout[rows, base : base + 128]
                dq = dk = dv = None
                for half in range(2):
                    keep = low if half == 0 else jnp.logical_not(low)

                    def only(x, keep=keep):
                        return jnp.where(keep, x, jnp.zeros_like(x))

                    weights = s.p[l, w, 2 * pair + half]
                    grad_half = only(grad)
                    dv_part = dot(weights, grad_half)
                    dp = dot_t(v, grad_half)
                    wide_weights = weights.astype(F32)
                    product = dp * wide_weights
                    ds = (product - wide_weights * jnp.sum(product, axis=0, keepdims=True)).astype(BF16)
                    dk_part = dot(ds, only(q))
                    dq_part = t_dot(only(k), ds)
                    if half == 0:
                        dq, dk, dv = dq_part, dk_part, dv_part
                    else:
                        dq, dk, dv = dq + dq_part, dk + dk_part, dv + dv_part
                for offset, value in ((0, (dq * HEAD_DIM**-0.5).T), (D, dk), (2 * D, dv)):
                    cols = slice(offset + base, offset + base + 128)
                    s.dqkv[rows, cols] = s.dqkv[rows, cols] + value.astype(BF16)

        windows(window, then)

    def backward_last(self, l, u_ref, du_ref, then=None):
        s = self.s

        def step(i, _):
            rows = row_block(i)
            dqkv = s.dqkv[rows, :]
            da = dot_t(dqkv, load_qkv(s.w, l))
            normed, inverse = standard(u_ref[rows, :].astype(F32))
            du = s.dh[rows, :] + norm_back(normed, inverse, s.vec[l, 0:1, :], da)
            du_ref[rows, :] = du.astype(BF16)
            s.gvec[l, 0:1, :] += column_sum(da * normed)
            s.gvec[l, 1:2, :] += column_sum(da)
            s.gvec[l, 2:3, :] += column_sum(dqkv[:, 0:D].astype(F32))
            s.gvec[l, 3:4, :] += column_sum(dqkv[:, 2 * D : 3 * D].astype(F32))
            return 0

        steps(BLOCKS, step, then)
        self.spread_gains(l)

    def grad_qkv(self, l):
        s = self.s
        value = t_dot(s.a[l], s.dqkv[...]).astype(BF16)
        for b in range(3):
            store_rows(s.g, l, wide_tiles(qkv_tile, b), value[:, b * D : (b + 1) * D])


COMPUTE = (
    ("w", (2, 4, 2, 2 * HALF, D), BF16),
    ("g", (2, 4, 2, 2 * HALF, D), BF16),
    ("vec", (2, TILE, D), F32),
    ("gvec", (2, TILE, D), F32),
    ("a", (2, ROWS, D), BF16),
    ("qkv", (2, ROWS, 3 * D), BF16),
    ("o", (2, ROWS, D), BF16),
    ("h", (2, ROWS, D), F32),
    ("c", (2, ROWS, D), BF16),
    ("z", (2, ROWS, FF), BF16),
    ("slope", (2, ROWS, FF), BF16),
    ("p", (2, WINDOWS, HEADS, WINDOW, WINDOW), BF16),
    ("bup", (2, 8, FF), F32),
    ("dbup", (8, FF), F32),
    ("df", (ROWS, FF), BF16),
    ("dh", (ROWS, D), F32),
    ("dhb", (ROWS, D), BF16),
    ("dout", (ROWS, D), BF16),
    ("dqkv", (ROWS, 3 * D), BF16),
)
LINKS = (
    ("x", (ROWS, D), BF16),
    ("cot", (ROWS, D), BF16),
    ("act", (2 * ROWS, D), BF16),
    ("grads", (2 * ROWS, D), BF16),
    ("near_wide", (D // (2 * SLOTS), 3 * D + FF), F32),
    ("near_tall", ((D + FF) // (2 * SLOTS), D), F32),
    ("near_vec", (12, 1, D // (2 * SLOTS)), F32),
    ("total", (2, HALF, D), F32),
) + tuple(
    (f"{name}{st}", (count, STAGES[st][1], D), BF16)
    for st in range(len(STAGES))
    for name, count in (("sum_x", 1), ("from_x", 1), ("from_xy", 4), ("from_xz", 4))
) + tuple(
    (f"{name}{l}{st}", count + (STAGES[st][1], D), BF16)
    for l in range(2)
    for st in range(len(STAGES))
    for name, count in (("from_c", (4, 2)), ("from_y", (4,)), ("from_z", (3,)))
)


class Refs:
    pass


G0, G1, G2, G3, G4, R0, R1, R1X, R2, R2X, R3, R3X, R4, SHARE = range(14)
GAINS, FIRST, ATTEND, SECOND, BACK_FIRST, GRAD_UP, GRAD_TALL, BACK_ATTEND, LAST, GRAD_QKV = range(14, 24)
BY_X, BY_Y, BY_Z = range(3)
GATHER = (
    (((BY_X, BY_Y), (BY_X, BY_Y)), ((BY_X, BY_X), (BY_X, BY_Y)), ((BY_X, BY_X), (BY_X, BY_X)), ((BY_Z, BY_Y), (BY_Z, BY_Y))),
    (((BY_Z, BY_X), (BY_Z, BY_Y)), ((BY_X, BY_Y), (BY_Z, BY_X)), ((BY_Z, BY_Y), (BY_X, BY_Y)), ((BY_X, BY_X), (BY_X, BY_X))),
)
REDUCE = (
    (((BY_Z, BY_Y), (BY_Z, BY_Y)), ((BY_X, BY_Y), (BY_X, BY_Y)), ((BY_Z, BY_Y), (BY_Z, BY_Y)), ((BY_Z, BY_X), (BY_Z, BY_Y))),
    (((BY_X, BY_X), (BY_X, BY_X)), ((BY_X, BY_X), (BY_X, BY_X)), ((BY_Z, BY_Y), (BY_Z, BY_Y)), ((BY_Z, BY_Y), (BY_Z, BY_Y))),
)
PLAN = (
    (G0, 0, 0, True),
    (G0, 0, 1, True),
    (G0, 0, 2, True),
    (G0, 0, 3, True),
    (G0, 1, 1, True),
    (G0, 1, 3, True),
    (G1, 0, 0, False),
    (G1, 1, 1, False),
    (G1, 0, 1, False),
    (G1, 1, 3, False),
    (G1, 0, 0, True),
    (G1, 1, 1, True),
    (G1, 0, 2, False),
    (G1, 0, 3, False),
    (G1, 0, 1, True),
    (G2, 1, 1, True),
    (G2, 0, 0, False),
    (G4, 1, 1, True),
    (G2, 0, 0, True),
    (G4, 0, 0, True),
    (G1, 1, 3, True),
    (G2, 0, 1, False),
    (G2, 0, 1, True),
    (G3, 0, 0, False),
    (G4, 0, 1, True),
    (G4, 0, 0, False),
    (G1, 0, 2, True),
    (G0, 1, 0, True),
    (G2, 1, 3, False),
    (G2, 1, 3, True),
    (G1, 1, 0, False),
    (G2, 0, 3, False),
    (G4, 1, 3, True),
    (G3, 0, 1, False),
    (G4, 0, 1, False),
    (G1, 1, 0, True),
    (G2, 0, 2, True),
    (G2, 0, 2, False),
    (G1, 0, 3, True),
    (G0, 1, 2, True),
    (GAINS, 0, ()),
    (FIRST, 0, ()),
    (G4, 0, 2, True),
    (G2, 1, 1, False),
    (ATTEND, 0, ((0, G3, 1, 3, False),)),
    (G3, 0, 3, False),
    (G1, 1, 2, False),
    (G2, 1, 0, False),
    (G4, 1, 3, False),
    (G2, 0, 3, True),
    (G2, 1, 0, True),
    (G4, 0, 3, False),
    (G4, 1, 0, True),
    (G3, 1, 1, False),
    (G3, 0, 2, False),
    (G4, 0, 3, True),
    (G4, 1, 1, False),
    (G1, 1, 2, True),
    (G4, 0, 2, False),
    (SECOND, 0, ()),
    (G3, 1, 0, False),
    (SHARE, 0, 0, 0),
    (G2, 1, 2, False),
    (G4, 1, 0, False),
    (GAINS, 1, ()),
    (FIRST, 1, ()),
    (ATTEND, 1, ((0, G2, 1, 2, True),)),
    (G4, 1, 2, True),
    (G3, 1, 2, False),
    (G4, 1, 2, False),
    (SECOND, 1, ()),
    (SHARE, 0, 0, 1),
    (SHARE, 1, 0, 0),
    (BACK_FIRST, 1, ()),
    (GRAD_UP, 1, ()),
    (R0, 1, 3, None),
    (GRAD_TALL, 1, ()),
    (SHARE, 1, 0, 1),
    (R0, 1, 2, None),
    (BACK_ATTEND, 1, ((0, R1, 1, 3, None),)),
    (R1, 1, 2, None),
    (LAST, 1, ()),
    (SHARE, 1, 1, 0),
    (GRAD_QKV, 1, ()),
    (R0, 1, 0, None),
    (R0, 1, 1, None),
    (BACK_FIRST, 0, ()),
    (R2, 1, 3, True),
    (R1, 1, 0, None),
    (R1, 1, 1, None),
    (R2, 1, 3, False),
    (GRAD_UP, 0, ()),
    (R0, 0, 3, None),
    (GRAD_TALL, 0, ()),
    (R0, 0, 2, None),
    (BACK_ATTEND, 0, ((0, R1, 0, 3, None), (0, R2, 1, 2, False),)),
    (R2, 1, 2, True),
    (R3, 1, 3, True),
    (R1, 0, 2, None),
    (R1X, 0, 3, True),
    (R3, 1, 3, False),
    (GRAD_QKV, 0, ()),
    (R0, 0, 0, None),
    (LAST, 0, ()),
    (R2, 0, 3, False),
    (R1X, 1, 0, True),
    (SHARE, 0, 1, 0),
    (R0, 0, 1, None),
    (R1, 0, 0, None),
    (R1, 0, 1, None),
    (R1X, 1, 1, True),
    (SHARE, 0, 1, 1),
    (R3, 1, 2, True),
    (R2, 0, 2, False),
    (R3, 1, 2, False),
    (R3X, 1, 3, True),
    (R2, 0, 2, True),
    (SHARE, 1, 1, 1),
    (R3, 0, 3, False),
    (R2, 1, 0, True),
    (R2X, 1, 0, True),
    (R4, 1, 3, True),
    (R3X, 1, 2, True),
    (R4, 1, 2, True),
    (R2, 0, 3, True),
    (R2, 0, 0, False),
    (R3, 0, 2, True),
    (R2, 0, 0, True),
    (R2, 0, 1, False),
    (R3, 0, 2, False),
    (R2, 0, 1, True),
    (R2, 1, 1, True),
    (R2X, 1, 1, True),
    (R2X, 0, 1, True),
    (R3, 1, 0, True),
    (R3, 0, 3, True),
    (R3X, 0, 3, True),
    (R3X, 0, 2, True),
    (R3, 0, 0, False),
    (R3, 0, 0, True),
    (R3X, 0, 0, True),
    (R3, 1, 1, True),
    (R4, 1, 1, True),
    (R4, 1, 0, True),
    (R4, 0, 3, True),
    (R4, 0, 2, True),
    (R3, 0, 1, True),
    (R4, 0, 1, True),
    (R4, 0, 0, True),
)


PIECES = 2


class Links:
    def __init__(self, s):
        self.s = s
        self.section = lax.axis_index("section")
        self.dp = lax.axis_index("dp")
        self.z, self.y, self.core = self.dp // 4, (self.dp // 2) % 2, self.dp % 2
        self.near = (self.section, self.dp + 1 - 2 * self.core)
        self.across = (1 - self.section, self.dp)
        self.beside = (self.section, self.dp + 2 - 4 * self.y)
        self.pending = []
        sides = {(l, owner): self.section == l if owner else self.section != l for l in range(2) for owner in (True, False)}
        self.conditions = {}
        for (l, owner), side in sides.items():
            for core in (None, 0, 1):
                role = side if core is None else side & (self.core == core)
                self.conditions[l, owner, core] = role

    def level(self, steps):
        there = (self.z + steps) % 4
        return there, (self.section, self.dp + 4 * (there - self.z))

    def greet(self):
        others = [self.level(i)[1] for i in (2, 3, 1)] + [self.across, self.beside, self.near]
        for device in others:
            pl.semaphore_signal(pltpu.get_barrier_semaphore(), inc=1, device_id=device, device_id_type=MESH)

    def meet(self):
        pl.semaphore_wait(pltpu.get_barrier_semaphore(), 6)

    def copy(self, src, dst, sems, index, device):
        return pltpu.make_async_remote_copy(
            src_ref=src,
            dst_ref=dst,
            send_sem=sems[0].at[index],
            recv_sem=sems[1].at[index],
            device_id=device,
            device_id_type=MESH,
        )

    def send(self, make, when=None):
        self.pending.append((make, when))
        self.copy(*make()).start()

    def received(self, make):
        self.copy(*make()).wait_recv()

    def drain(self, count=None):
        groups = {}
        for make, when in self.pending[:count]:
            groups.setdefault(id(when), (when, []))[1].append(make)
        self.pending = self.pending[len(self.pending) if count is None else count :]
        for when, makes in groups.values():

            def wait(makes=makes):
                for make in makes:
                    self.copy(*make()).wait_send()

            wait() if when is None else pl.when(when)(wait)


    def rows_of(self, stage, core):
        first, count = STAGES[stage]
        return pl.ds(pl.multiple_of(core * HALF + first, TILE), count)

    def w_part(self, l, z, y, stage, core):
        return self.s.w.at[l, z, y, self.rows_of(stage, core), :]

    def box(self, name, l, stage):
        return getattr(self.s, f"{name}{l}{stage}")


    def shard(self):
        s = self.s
        return ((s.wide_in.at[0], s.near_wide), (s.tall_in.at[0], s.near_tall), (s.vec_in, s.near_vec))

    def near_start(self):
        for index, (src, dst) in enumerate(self.shard()):
            self.send(lambda src=src, dst=dst, index=index: (src, dst, self.s.near_sems, index, self.near))

    def near_finish(self):
        s = self.s
        for index, (src, dst) in enumerate(self.shard()):
            self.received(lambda: (src, dst, s.near_sems, index, self.near))
        first = self.core == 0

        def pair(own, near):
            return jnp.where(first, own, near), jnp.where(first, near, own)

        def put(tile, value):
            s.w[self.section, self.z, self.y, tile * TILE : (tile + 1) * TILE, :] = value

        rows = jnp.concatenate(pair(s.wide_in[0], s.near_wide[...]), axis=0).astype(BF16)
        for block in range(7):
            for i in range(3):
                tile = qkv_tile(3 * block + i) if block < 3 else up_tile(3 * (block - 3) + i)
                put(tile, rows[i * TILE : (i + 1) * TILE, block * D : (block + 1) * D])
        rows = jnp.concatenate(pair(s.tall_in[0], s.near_tall[...]), axis=0).astype(BF16)
        for i in range(15):
            put(tall_tile(i), rows[i * TILE : (i + 1) * TILE])
        count, _, width = s.near_vec.shape
        s.padded[...] = jnp.zeros_like(s.padded)
        for i in range(count):
            for half, value in enumerate(pair(s.vec_in[i], s.near_vec[i])):
                s.padded[half, i : i + 1, 0:width] = value
        for half in range(2):
            put(vec_tile(half), s.padded[half].astype(BF16))

    def place(self, tag, l, stage, coming):
        s = self.s
        kind, i = tag[:-1], int(tag[-1])
        back = self.level(4 - i)[0] if i else self.z
        core = 1 - self.core if coming and kind[0] == "n" else self.core
        if kind == "z":
            slot, device, index = (back if coming else self.z, self.y), self.level(i)[1], 1 + i
        elif kind == "y":
            slot, device, index = (back, 1 - self.y if coming else self.y), self.beside, 8 + i
        elif kind == "x":
            slot, device, index = (self.z, self.y), self.across, 0
        elif kind == "n":
            slot, device, index = (self.z, self.y), self.near, 1
        else:
            slot = (back, self.y if kind[1] == "z" else 1 - self.y)
            device = self.across if kind[0] == "x" else self.near
            index = {"nz": 4, "ny": 12, "xz": 15, "xy": 19}[kind] + i
        part = self.w_part(l, slot[0], slot[1], stage, core)
        return part, part, s.w_sems, (l, stage, index), device

    def gather(self, *role):
        return [(waits, None, sends) for waits, sends in self.gather_copies(*role)]

    def gather_copies(self, name, l, stage, owner, zs, ys):
        three, four = (1, 2, 3), (0, 1, 2, 3)
        if name == G0:
            return [((), ("x0", "z1", "z2", "z3", "y0"))] if owner else []
        if name == G1:
            if owner:
                return [
                    ((f"z{i}",), (f"y{i}", f"nz{i}") + ((f"xz{i}",) if zs == BY_X else ()))
                    for i in three
                ]
            sends = ("n0",) + (("z1", "z2", "z3") if zs == BY_Z else ()) + (("y0",) if ys == BY_Y else ())
            return [(("x0",), sends)]
        if name == G2:
            if owner:
                return [((f"y{i}",), (f"ny{i}",) + ((f"xy{i}",) if ys == BY_X else ())) for i in four]
            source = "z" if zs == BY_Z else "xz"
            return [
                ((f"{source}{i}",), (f"nz{i}",) + ((f"y{i}",) if ys == BY_Y else ()))
                for i in three
            ]
        if name == G3:
            source = "y" if ys == BY_Y else "xy"
            return [] if owner else [((f"{source}{i}",), (f"ny{i}",)) for i in four]
        waits = tuple(f"nz{i}" for i in three) + tuple(f"ny{i}" for i in four)
        return [(waits + (() if owner else ("n0",)), ())]

    def do(self, name, l, stage, side):
        if name == SHARE:
            self.share(l, stage, side)
            return
        config = (GATHER if name <= G4 else REDUCE)[l][stage]
        make = self.place if name <= G4 else self.sum_copy
        if name == R0:
            self.send(lambda: self.sum_copy("c", l, stage, False))
            return
        if name == R1:
            self.received(lambda: self.sum_copy("c", l, stage, True))
            self.add_near(l, stage)
        cores = (None,) if config[0] == config[1] else (0, 1)
        for owner in (True, False) if side is None else (side,):
            for core in cores:
                zs, ys = config[core or 0]
                role = (l, owner, core)
                todo = (self.gather if name <= G4 else self.reduce)(name, l, stage, owner, zs, ys)
                if not todo:
                    continue

                def act(todo=todo, role=role):
                    for waits, work, sends in todo:
                        for tag in waits:
                            self.received(lambda: make(tag, l, stage, True))
                        if work is not None:
                            work()
                        for tag in sends:
                            self.send(lambda tag=tag: make(tag, l, stage, False), self.conditions[role])

                pl.when(self.conditions[role])(act)

    def rows_shared(self, l, which, i):
        s = self.s
        array, out = ((s.act, s.far_act), (s.grads, s.far_grads))[which]
        count = ROWS // PIECES
        first = l * ROWS + i * count
        return array.at[first : first + count, :], out.at[i * count : (i + 1) * count, :], s.o_sems, (which, i), self.across

    def share(self, l, which, i):
        when = self.conditions[l, False, None]
        pl.when(when)(lambda: self.send(lambda: self.rows_shared(l, which, i), when))


    def sum_copy(self, tag, l, stage, coming):
        s = self.s
        rows = self.rows_of(stage, self.core)
        first, count = STAGES[stage]
        if tag == "c":
            src = s.g.at[l, :, :, self.rows_of(stage, 1 - self.core), :]
            return src, self.box("from_c", l, stage), s.g_sems, (l, stage, 0), self.near
        if tag == "Y":
            return s.g.at[l, :, 1 - self.y, rows, :], self.box("from_y", l, stage), s.g_sems, (l, stage, 1), self.beside
        if tag == "XY":
            return s.g.at[l, :, 1 - self.y, rows, :], self.box("from_xy", "", stage), s.g_sems, (l, stage, 5), self.across
        if tag == "XZ":
            return s.g.at[l, :, self.y, rows, :], self.box("from_xz", "", stage), s.g_sems, (l, stage, 6), self.across
        if tag == "X":
            return self.box("sum_x", "", stage), self.box("from_x", "", stage), s.g_sems, (l, stage, 7), self.across
        if tag == "T":
            mine = s.total.at[self.core, first : first + count, :]
            return mine, mine, s.g_sems, (l, stage, 8), self.near
        box = self.box("from_z", l, stage)
        there, device = self.level(int(tag[1]))
        return s.g.at[l, there, self.y, rows, :], box.at[int(tag[1]) - 1], s.g_sems, (l, stage, 1 + int(tag[1])), device

    def add_near(self, l, stage):
        s = self.s
        rows, box = self.rows_of(stage, self.core), self.box("from_c", l, stage)

        def add(i, _):
            z, y = i // 2, i % 2
            s.g[l, z, y, rows, :] = (s.g[l, z, y, rows, :].astype(F32) + box[z, y].astype(F32)).astype(BF16)
            return 0

        lax.fori_loop(0, SLOTS, add, 0)

    def add_column(self, name, l, stage, y):
        s = self.s
        rows = self.rows_of(stage, self.core)

        def add(i, _):
            s.g[l, i, y, rows, :] = (s.g[l, i, y, rows, :].astype(F32) + name[i].astype(F32)).astype(BF16)
            return 0

        lax.fori_loop(0, 4, add, 0)

    def add_levels(self, l, stage):
        box = self.box("from_z", l, stage)
        total = self.s.g[l, self.z, self.y, self.rows_of(stage, self.core), :].astype(F32)
        for i in range(3):
            total = total + box[i].astype(F32)
        return total

    def reduce(self, name, l, stage, owner, zs, ys):
        s = self.s
        first, count = STAGES[stage]
        levels = ("Z1", "Z2", "Z3")
        down = levels if zs == BY_Z else ("XZ",)

        def column(name, y, layer):
            return lambda: self.add_column(self.box(name, layer, stage), l, stage, y)

        def keep():
            s.total[self.core, first : first + count, :] = self.add_levels(l, stage)

        def hand_on():
            self.box("sum_x", "", stage)[0] = self.add_levels(l, stage).astype(BF16)

        def last():
            s.total[self.core, first : first + count, :] += self.box("from_x", "", stage)[0].astype(F32)

        if name == R1:
            if ys == BY_Y:
                return [((), None, ("Y",))]
            return [] if owner else [((), None, ("XY",) + down)]
        if name == R1X:
            return [(("XY",), column("from_xy", 1 - self.y, ""), ("Y",))] if owner and ys == BY_X else []
        if name == R2:
            if owner:
                return [(("Y",), column("from_y", self.y, l), levels if zs == BY_Z else ())]
            return [(("Y",), column("from_y", self.y, l), down)] if ys == BY_Y else []
        if name == R2X:
            return [(("XZ",), column("from_xz", self.y, ""), levels)] if owner and zs == BY_X else []
        if name == R3:
            if owner:
                return [(levels, keep, ("T",) if zs == BY_X else ())]
            return [(levels, hand_on, ("X",))] if zs == BY_Z else []
        if name == R3X:
            return [(("X",), last, ("T",))] if owner and zs == BY_Z else []
        return [(("T",), None, ())] if owner else []


def take_rows(section, whole, out):
    edge = IMG_TOK // TILE * TILE

    @pl.when(section == 0)
    def _():
        out[0:edge, :] = whole[0:edge, :]
        row = lax.broadcasted_iota(jnp.int32, (ROWS - edge, D), 0)
        out[edge:ROWS, :] = jnp.where(row < IMG_TOK - edge, whole[edge:ROWS, :].astype(F32), 0.0).astype(BF16)

    @pl.when(section == 1)
    def _():
        rows = whole[edge : 2 * IMG_TOK, :].astype(F32)
        rows = jnp.concatenate((rows[IMG_TOK - edge :], jnp.zeros((ROWS - IMG_TOK, D), F32)), axis=0)
        out[...] = rows.astype(BF16)


def image_kernel(
    inputs, cotangent, wide_in, tall_in, vec_in, own_act, own_grads, far_act, far_grads, total_out, *scratch
):
    s = Refs()
    names = [name for name, _, _ in COMPUTE + LINKS] + ["padded", "wide_in", "tall_in", "vec_in", "near_sems", "w_sems", "g_sems", "o_sems", "local_sems"]
    flat = list(scratch)
    for name in names:
        if name in ("near_sems", "w_sems", "g_sems", "o_sems"):
            setattr(s, name, (flat.pop(0), flat.pop(0)))
        else:
            setattr(s, name, flat.pop(0))
    s.far_act, s.far_grads = far_act, far_grads
    link, image = Links(s), Image(s)
    section = link.section
    def bring(array, index):
        return pltpu.make_async_copy(array, s.act.at[0 : 2 * IMG_TOK, :], s.local_sems.at[index])

    def keep(array, out, index):
        rows = pl.ds(pl.multiple_of(section * ROWS, ROWS), ROWS)
        return pltpu.make_async_copy(array.at[rows, :], out, s.local_sems.at[index])

    def compute(name, l, then):
        u = s.x if l == 0 else s.act.at[0:ROWS, :]
        dy = s.cot if l == 1 else s.grads.at[ROWS:, :]
        mine = slice(l * ROWS, (l + 1) * ROWS)
        if name == GAINS:
            image.gains(l)
        elif name == FIRST:
            image.forward_first(l, u, then)
        elif name == ATTEND:
            image.forward_attend(l, then)
        elif name == SECOND:
            image.forward_second(l, u, s.act.at[mine, :], then)
        elif name == BACK_FIRST:
            image.backward_first(l, dy, then)
        elif name == GRAD_UP:
            image.grad_up(l)
        elif name == GRAD_TALL:
            image.grad_tall(l, dy)
        elif name == BACK_ATTEND:
            image.backward_attend(l, then)
        elif name == LAST:
            image.backward_last(l, u, s.grads.at[mine, :], then)
        elif name == GRAD_QKV:
            image.grad_qkv(l)

    link.greet()
    shards = [
        pltpu.make_async_copy(array, held, s.local_sems.at[5 + i])
        for i, (array, held) in enumerate(((wide_in, s.wide_in), (tall_in, s.tall_in), (vec_in, s.vec_in)))
    ]
    for shard in shards:
        shard.start()
    bring(inputs, 0).start()
    for shard in shards:
        shard.wait()
    bring(inputs, 0).wait()
    take_rows(section, s.act, s.x)
    bring(cotangent, 1).start()
    link.meet()
    link.near_start()
    link.near_finish()
    fresh = True
    last = max(i for i, entry in enumerate(PLAN) if entry[0] >= GAINS)
    for position, entry in enumerate(PLAN):
        if entry[0] < GAINS:
            link.do(*entry)
            continue
        if entry[0] == FIRST and fresh:
            bring(cotangent, 1).wait()
            take_rows(section, s.act, s.cot)
            fresh = False
        name, l, hooks = entry
        then = {}
        for i in range(WINDOWS):
            actions = [functools.partial(link.do, *hook[1:]) for hook in hooks if hook[0] == i]
            if actions:
                then[i] = lambda actions=actions: [action() for action in actions] and None
        compute(name, l, then)
        if entry[:2] == (SECOND, 1):
            keep(s.act, own_act, 2).start()
            gathered = len(link.pending)
        if position == last:
            link.drain(gathered)
            keep(s.grads, own_grads, 3).start()
    put = pltpu.make_async_copy(s.total, total_out, s.local_sems.at[4])
    put.start()
    for which in range(2):
        for i in range(PIECES):
            link.received(lambda: link.rows_shared(0, which, i))
    link.drain()
    keep(s.act, own_act, 2).wait()
    keep(s.grads, own_grads, 3).wait()
    put.wait()


def one_image(inputs, cotangent, wide, tall, vec):
    anywhere = pl.BlockSpec(memory_space=pl.ANY)
    sems = [
        pltpu.SemaphoreType.DMA(shape)
        for shape in ((3,), (2, len(STAGES), 23), (2, len(STAGES), 9), (2, PIECES))
        for _ in range(2)
    ] + [pltpu.SemaphoreType.DMA((8,))]
    rows = jax.ShapeDtypeStruct((ROWS, D), BF16)
    return pl.pallas_call(
        image_kernel,
        out_shape=[rows, rows, rows, rows, jax.ShapeDtypeStruct((2, HALF, D), F32)],
        in_specs=[anywhere] * 5,
        out_specs=[anywhere] * 5,
        scratch_shapes=[pltpu.VMEM(shape, dtype) for _, shape, dtype in COMPUTE + LINKS]
        + [pltpu.VMEM((2, TILE, D), F32)]
        + [pltpu.VMEM(array.shape, F32) for array in (wide, tall, vec)]
        + sems,
        compiler_params=pltpu.CompilerParams(
            vmem_limit_bytes=64 * 2**20, collective_id=0, has_side_effects=True
        ),
        cost_estimate=pl.CostEstimate(flops=18 * 10**9, bytes_accessed=20 * 10**6, transcendentals=10**7),
    )(inputs, cotangent, wide, tall, vec)


def plain_kernel(x, cot, w, act, grads, g, *scratch):
    s = Refs()
    s.w, s.g = w, g
    for (name, _, _), ref in zip(COMPUTE[2:], scratch):
        setattr(s, name, ref)
    image = Image(s)
    for l, u, out in ((0, x, act.at[0]), (1, act.at[0], act.at[1])):
        image.gains(l)
        image.forward_first(l, u)
        image.forward_attend(l)
        image.forward_second(l, u, out)
    for l, u, dy, du in ((1, act.at[0], cot, grads.at[1]), (0, x, grads.at[1], grads.at[0])):
        image.backward_first(l, dy)
        image.grad_up(l)
        image.grad_tall(l, dy)
        image.backward_attend(l)
        image.backward_last(l, u, du)
        image.grad_qkv(l)


def plain_image(x, cot, w):
    whole = pl.BlockSpec(memory_space=pltpu.VMEM)
    return pl.pallas_call(
        plain_kernel,
        out_shape=(
            jax.ShapeDtypeStruct((2, ROWS, D), BF16),
            jax.ShapeDtypeStruct((2, ROWS, D), BF16),
            jax.ShapeDtypeStruct(w.shape, BF16),
        ),
        in_specs=[whole] * 3,
        out_specs=(whole,) * 3,
        scratch_shapes=[pltpu.VMEM(shape, dtype) for _, shape, dtype in COMPUTE[2:]],
        compiler_params=pltpu.CompilerParams(vmem_limit_bytes=64 * 2**20),
    )(x, cot, w)


def tile_order():
    wide = [qkv_tile(i) for i in range(9)] + [up_tile(i) for i in range(12)]
    return wide + [tall_tile(i) for i in range(15)] + [vec_tile(half) for half in range(2)]


def any_mesh(
    inputs, cotangent, wide_weights, wide_first, wide_second, tall_weights, tall_first, tall_second,
    vectors, vector_first, vector_second,
):
    section = lax.axis_index("section")
    both = ("section", "dp")
    wide = lax.all_gather(wide_weights[0].astype(BF16), both, axis=0, tiled=True)
    tall = lax.all_gather(tall_weights[0].astype(BF16), both, axis=0, tiled=True)
    vec = lax.all_gather(lax.all_gather(vectors[0].astype(BF16), "dp", axis=1, tiled=True), "section", axis=0)
    vec_rows, width = vec.shape[1], D // (2 * SLOTS)
    order = tile_order()
    place = sorted(range(len(order)), key=order.__getitem__)
    wide = wide.reshape(2, SLOTS, 3, TILE, 7, D).transpose(0, 1, 4, 2, 3, 5).reshape(2, SLOTS, 21, TILE, D)
    tall = tall.reshape(2, SLOTS, 15, TILE, D)
    vec = vec.reshape(2, vec_rows, SLOTS, 2, width).transpose(0, 2, 3, 1, 4)
    vec = jnp.pad(vec, ((0, 0),) * 3 + ((0, TILE - vec_rows), (0, D - width)))
    tiles = jnp.concatenate((wide, tall, vec), axis=2)[:, :, jnp.array(place)]
    act, grads, g = plain_image(
        own_rows(inputs, section), own_rows(cotangent, section), tiles.reshape(2, SLOTS // 2, 2, 2 * HALF, D)
    )
    far_act, far_grads = (
        lax.ppermute(lax.dynamic_index_in_dim(array, 1 - section, keepdims=False), "section", [(0, 1), (1, 0)])
        for array in (act, grads)
    )
    g = g.reshape(2, SLOTS, len(order), TILE, D)[:, :, jnp.array(order)].astype(F32)
    wide = g[:, :, :21].reshape(2, SLOTS, 7, 3, TILE, D).transpose(0, 1, 3, 4, 2, 5).reshape(2, D, 7 * D)
    tall = g[:, :, 21:36].reshape(2, D + FF, D)
    vec = g[:, :, 36:, :vec_rows, :width].transpose(0, 3, 1, 2, 4).reshape(2, vec_rows, D)

    def reduced(array, dim):
        array = lax.psum_scatter(array, "section", scatter_dimension=0, tiled=False)
        return lax.psum_scatter(array, "dp", scatter_dimension=dim, tiled=True)

    return finish(
        section, act, grads, far_act, far_grads, reduced(wide, 0), reduced(tall, 0), reduced(vec, 1),
        wide_weights, wide_first, wide_second, tall_weights, tall_first, tall_second, vectors, vector_first, vector_second,
    )


def adamw(weights, first, second, grads, rate, decay):
    first_new = BETA_ONE * first + (1.0 - BETA_ONE) * grads
    second_new = BETA_TWO * second + (1.0 - BETA_TWO) * grads * grads
    corrected = (
        first_new
        / (1.0 - BETA_ONE**STEP)
        / (jnp.sqrt(second_new / (1.0 - BETA_TWO**STEP)) + ADAM_EPS)
    )
    return (first_new, second_new, weights - rate * (corrected + decay * weights))


def own_rows(array, section):
    return jnp.pad(lax.dynamic_slice_in_dim(array, section * IMG_TOK, IMG_TOK), ((0, ROWS - IMG_TOK), (0, 0)))


def finish(
    section, act, grads, far_act, far_grads, total_wide, total_tall, total_vec,
    wide_weights, wide_first, wide_second, tall_weights, tall_first, tall_second, vectors, vector_first, vector_second,
):
    def joined(array, other):
        mine = lax.dynamic_index_in_dim(array, section, keepdims=False)[:IMG_TOK]
        other = other[:IMG_TOK]
        return jnp.where(section == 0, jnp.concatenate((mine, other)), jnp.concatenate((other, mine)))

    wide_m, wide_s, wide_n = adamw(wide_weights[0], wide_first[0], wide_second[0], total_wide, RATE_MATRIX, DECAY)
    tall_m, tall_s, tall_n = adamw(tall_weights[0], tall_first[0], tall_second[0], total_tall, RATE_MATRIX, DECAY)
    vec_m, vec_s, vec_n = adamw(vectors[0], vector_first[0], vector_second[0], total_vec, RATE_VECTOR, 0.0)
    outs = (joined(act, far_act), joined(grads, far_grads), wide_m, wide_s, wide_n, tall_m, tall_s, tall_n, vec_m, vec_s, vec_n)
    return tuple(out[None] for out in outs)


OWN_ROWS = ("own_act", "own_grads", "far_act", "far_grads", "total")
MASTERS = ("wide_w", "wide_m", "wide_s", "tall_w", "tall_m", "tall_s", "vec_w", "vec_m", "vec_s")
RESULTS = ("act", "grads", "wide_m1", "wide_s1", "wide_w1", "tall_m1", "tall_s1", "tall_w1", "vec_m1", "vec_s1", "vec_w1")


def finish_kernel(*refs):
    names = OWN_ROWS + MASTERS
    given, results = refs[: len(names)], refs[len(names) : len(names) + len(RESULTS)]
    held = refs[len(names) + len(RESULTS) : -2]
    came, left = refs[-2:]
    section = lax.axis_index("section")
    first = lax.axis_index("dp") % 2 == 0
    s = Refs()
    copies = {}
    for index, (name, src, dst) in enumerate(zip(names, given, held)):
        setattr(s, name, dst)
        copies[name] = pltpu.make_async_copy(src, dst, came.at[index])
    for index, (name, src, dst) in enumerate(zip(RESULTS, held[len(names) :], results)):
        setattr(s, name, src)
        copies[name] = pltpu.make_async_copy(src, dst, left.at[index])
    for name in names:
        copies[name].start()

    def fetch(*wanted):
        for name in wanted:
            copies[name].wait()

    def put(*done):
        for name in done:
            copies[name].start()

    edge = IMG_TOK // TILE * TILE

    def join(low, high, out):
        out[0, 0:edge, :] = low[0:edge, :]
        rows = jnp.concatenate((low[edge:IMG_TOK, :].astype(F32), high[0:IMG_TOK, :].astype(F32)), axis=0)
        out[0, edge : 2 * IMG_TOK, :] = rows.astype(BF16)

    for own, far, out in (("own_act", "far_act", "act"), ("own_grads", "far_grads", "grads")):
        fetch(own, far)
        pl.when(section == 0)(lambda: join(getattr(s, own), getattr(s, far), getattr(s, out)))
        pl.when(section == 1)(lambda: join(getattr(s, far), getattr(s, own), getattr(s, out)))
        put(out)

    def tile(i):
        return s.total[i // 19, (i % 19) * TILE : (i % 19 + 1) * TILE, :]

    def own_half(rows):
        half = rows.shape[0] // 2
        return jnp.where(first, rows[:half], rows[half:])

    fetch("total", "wide_w", "wide_m", "wide_s")
    for block in range(7):
        tiles = [qkv_tile(3 * block + i) if block < 3 else up_tile(3 * (block - 3) + i) for i in range(3)]
        g = own_half(jnp.concatenate([tile(i) for i in tiles], axis=0))
        cols = slice(block * D, (block + 1) * D)
        s.wide_m1[0, :, cols], s.wide_s1[0, :, cols], s.wide_w1[0, :, cols] = adamw(
            s.wide_w[0, :, cols], s.wide_m[0, :, cols], s.wide_s[0, :, cols], g, RATE_MATRIX, DECAY
        )
    put("wide_m1", "wide_s1", "wide_w1")
    fetch("tall_w", "tall_m", "tall_s")
    g = own_half(jnp.concatenate([tile(tall_tile(i)) for i in range(15)], axis=0))
    s.tall_m1[0], s.tall_s1[0], s.tall_w1[0] = adamw(s.tall_w[0], s.tall_m[0], s.tall_s[0], g, RATE_MATRIX, DECAY)
    put("tall_m1", "tall_s1", "tall_w1")
    fetch("vec_w", "vec_m", "vec_s")
    count, _, width = s.vec_w.shape
    g = jnp.where(first, tile(vec_tile(0)), tile(vec_tile(1)))[0:count, 0:width]
    for i in range(count):
        s.vec_m1[i], s.vec_s1[i], s.vec_w1[i] = adamw(
            s.vec_w[i], s.vec_m[i], s.vec_s[i], g[i : i + 1], RATE_VECTOR, 0.0
        )
    put("vec_m1", "vec_s1", "vec_w1")
    for name in RESULTS:
        copies[name].wait()


def per_device(
    inputs, cotangent, wide_weights, wide_first, wide_second, tall_weights, tall_first, tall_second,
    vectors, vector_first, vector_second,
):
    vectors, vector_first, vector_second = (
        jnp.transpose(array, (1, 0, 2)) for array in (vectors, vector_first, vector_second)
    )
    sums = one_image(inputs, cotangent, wide_weights, tall_weights, vectors)
    given = list(sums) + [
        wide_weights, wide_first, wide_second, tall_weights, tall_first, tall_second, vectors, vector_first, vector_second,
    ]
    anywhere = pl.BlockSpec(memory_space=pl.ANY)
    rows = jax.ShapeDtypeStruct((1,) + inputs.shape, BF16)
    outs = [rows, rows] + [
        jax.ShapeDtypeStruct(array.shape, F32) for array in (wide_weights,) * 3 + (tall_weights,) * 3 + (vectors,) * 3
    ]
    results = pl.pallas_call(
        finish_kernel,
        out_shape=outs,
        in_specs=[anywhere] * len(given),
        out_specs=[anywhere] * len(outs),
        scratch_shapes=[pltpu.VMEM(array.shape, array.dtype) for array in given + outs]
        + [pltpu.SemaphoreType.DMA((len(given),)), pltpu.SemaphoreType.DMA((len(outs),))],
        compiler_params=pltpu.CompilerParams(vmem_limit_bytes=64 * 2**20),
        cost_estimate=pl.CostEstimate(flops=10**7, bytes_accessed=10**7, transcendentals=10**6),
    )(*given)
    return tuple(results[:8]) + tuple(jnp.transpose(array, (1, 0, 2)) for array in results[8:])


def solution(mesh):
    data = P("dp", None)
    matrix = P("section", "dp", None)
    vector = P("section", None, "dp")
    in_specs = (data, data) + (matrix,) * 6 + (vector,) * 3
    out_specs = (matrix,) * 8 + (vector,) * 3
    device_fn = per_device if mesh.shape["dp"] == 2 * SLOTS else any_mesh
    return jax.shard_map(device_fn, mesh=mesh, in_specs=in_specs, out_specs=out_specs, check_vma=False)
```

```python
import functools

import jax
import jax.numpy as jnp
from jax import lax
from jax.experimental import pallas as pl
from jax.experimental.pallas import tpu as pltpu
from jax.sharding import PartitionSpec as P

D = 384
HEADS = 6
HEAD_DIM = 64
FF = 1536
GLOBAL = 2
GLOBAL_LEN = 197
LOCAL = 10
LOCAL_LEN = 37
STEP = 5
IMG_TOK = GLOBAL * GLOBAL_LEN + LOCAL * LOCAL_LEN

NORM_EPS = 1e-06
BETA_ONE = 0.5
BETA_TWO = 0.5
ADAM_EPS = 1e-08
RATE_MATRIX = 0.05
RATE_VECTOR = 0.2
DECAY = 0.05
ERF_SCALE = 0.7071067811865476
DENSITY_SCALE = 0.3989422804014327

ROWS = 768
BLOCK = 768
BLOCKS = ROWS // BLOCK
WINDOW = 208
WINDOWS = 4
UNROLL = 2
CHUNK = 512
CHUNKS = FF // CHUNK
TILE = 16
SLOTS = 8
HALF = 19 * TILE
STAGES = ((0, 3 * TILE), (3 * TILE, 3 * TILE), (6 * TILE, 7 * TILE), (13 * TILE, 6 * TILE))
MESH = pl.DeviceIdType.MESH
F32 = jnp.float32
BF16 = jnp.bfloat16


def window_start(index):
    if isinstance(index, int):
        return min(index * 192, ROWS - WINDOW)
    return pl.multiple_of(jnp.minimum(index * 192, ROWS - WINDOW), 16)


def row_segment(row):
    local = ((row - GLOBAL * GLOBAL_LEN) * 1772) >> 16
    segment = jnp.where(row < GLOBAL * GLOBAL_LEN, jnp.where(row < GLOBAL_LEN, 0, 1), local + GLOBAL)
    return jnp.where(row < IMG_TOK, segment, 99)


def window_of(segment):
    return jnp.where(segment < 2, segment, jnp.where(segment < 7, 2, jnp.where(segment < 12, 3, 9)))


def dot(a, b):
    return jnp.dot(a, b, preferred_element_type=F32)


def dot_t(a, b):
    return lax.dot_general(a, b, (((1,), (1,)), ((), ())), preferred_element_type=F32)


def t_dot(a, b):
    return lax.dot_general(a, b, (((0,), (0,)), ((), ())), preferred_element_type=F32)


def standard(values):
    centre = values - jnp.mean(values, axis=-1, keepdims=True)
    inverse = lax.rsqrt(jnp.mean(centre * centre, axis=-1, keepdims=True) + NORM_EPS)
    return centre * inverse, inverse


def norm_back(normed, inverse, gain, incoming):
    scaled = incoming * gain
    return inverse * (
        scaled
        - jnp.mean(scaled, axis=-1, keepdims=True)
        - normed * jnp.mean(scaled * normed, axis=-1, keepdims=True)
    )


def gelu_pair(f):
    below = 0.5 + 0.5 * lax.erf(f * ERF_SCALE)
    return f * below, below + f * jnp.exp(-0.5 * f * f) * DENSITY_SCALE


def column_sum(values):
    return jnp.sum(values, axis=0, keepdims=True)


def qkv_tile(i):
    return i if i < 5 else 19 + i - 5


def tall_tile(i):
    return 6 + i if i < 7 else (23 if i == 7 else 25 + i - 8)


def up_tile(i):
    return 13 + i if i < 6 else 32 + i - 6


def vec_tile(half):
    return 19 * half + 5


def runs(tiles):
    out = []
    for slot, tile in tiles:
        if out and out[-1][0] == slot and out[-1][1] + out[-1][2] == tile * TILE:
            out[-1][2] += TILE
        else:
            out.append([slot, tile * TILE, TILE])
    return out


def wide_tiles(name, block):
    return [(k, name(3 * block + i)) for k in range(SLOTS) for i in range(3)]


def tall_tiles(first, count):
    per = 15
    return [(t // per, tall_tile(t % per)) for t in range(first // TILE, (first + count) // TILE)]


def load_rows(ref, l, tiles, lanes=slice(0, D)):
    return jnp.concatenate(
        [ref[l, slot // 2, slot % 2, row : row + count, lanes] for slot, row, count in runs(tiles)], axis=0
    )


def store_rows(ref, l, tiles, value):
    done = 0
    for slot, row, count in runs(tiles):
        ref[l, slot // 2, slot % 2, row : row + count, :] = value[done : done + count]
        done += count


def load_qkv(w, l):
    return jnp.concatenate([load_rows(w, l, wide_tiles(qkv_tile, b)) for b in range(3)], axis=1)


def load_up(w, l, j):
    parts, at = [], j * CHUNK
    while at < (j + 1) * CHUNK:
        block, lane = divmod(at, D)
        take = min(D - lane, (j + 1) * CHUNK - at)
        parts.append(load_rows(w, l, wide_tiles(up_tile, block), slice(lane, lane + take)))
        at += take
    return jnp.concatenate(parts, axis=1)


def load_proj(w, l):
    return load_rows(w, l, tall_tiles(0, D))


def load_down(w, l, j):
    return load_rows(w, l, tall_tiles(D + j * CHUNK, CHUNK))


def row_block(i):
    if isinstance(i, int):
        return pl.ds(i * BLOCK, BLOCK)
    return pl.ds(pl.multiple_of(i * BLOCK, BLOCK), BLOCK)


def steps(count, step, then=None):
    def body(i, carry):
        step(i, carry)
        for at, action in (then or {}).items():
            pl.when(i == at)(action)
        return 0

    if count == 1:
        step(0, 0)
        for action in (then or {}).values():
            action()
        return
    lax.fori_loop(0, count, body, 0)


def windows(window, then=None):
    def step(i, _):
        for j in range(UNROLL):
            window(i * UNROLL + j)

    steps(WINDOWS // UNROLL, step, then)


class Image:
    def __init__(self, s):
        self.s = s
        self.low = None

    def gains(self, l):
        s = self.s
        lane = lax.broadcasted_iota(jnp.int32, (TILE, 128), 1)
        tiles = [jnp.zeros((TILE, 128), F32) for _ in range(D // 128)]
        for slot in range(SLOTS):
            for half in range(2):
                row = vec_tile(half) * TILE
                part = s.w[l, slot // 2, slot % 2, row : row + TILE, 0:128].astype(F32)
                width = D // (2 * SLOTS)
                at = (2 * slot + half) * width
                index, shift = divmod(at, 128)
                moved = pltpu.roll(part, shift, 1) if shift else part
                if shift + width > 128:
                    tiles[index] = tiles[index] + jnp.where(lane >= shift, moved, 0.0)
                    tiles[index + 1] = tiles[index + 1] + jnp.where(lane < shift, moved, 0.0)
                else:
                    tiles[index] = tiles[index] + moved
        for index, tile in enumerate(tiles):
            s.vec[l, :, index * 128 : (index + 1) * 128] = tile
        for j in range(FF // D):
            s.bup[l, 0:1, j * D : (j + 1) * D] = s.vec[l, 8 + j : 9 + j, :]

    def spread_gains(self, l):
        s = self.s
        lane = lax.broadcasted_iota(jnp.int32, (TILE, 128), 1)
        width = D // (2 * SLOTS)
        for slot in range(SLOTS):
            for half in range(2):
                at = (2 * slot + half) * width
                index, shift = divmod(at, 128)
                tile = s.gvec[l, :, index * 128 : (index + 1) * 128]
                if shift + width > 128:
                    tile = jnp.where(lane >= shift, tile, s.gvec[l, :, (index + 1) * 128 : (index + 2) * 128])
                moved = pltpu.roll(tile, 128 - shift, 1) if shift else tile
                moved = jnp.where(lane < width, moved, 0.0).astype(BF16)
                row = vec_tile(half) * TILE
                s.g[l, slot // 2, slot % 2, row : row + TILE, :] = jnp.concatenate(
                    (moved, jnp.zeros((TILE, D - 128), BF16)), axis=1
                )

    def window_bias(self, w):
        start = window_start(w)
        key = row_segment(start + lax.broadcasted_iota(jnp.int32, (WINDOW, 1), 0))
        query = row_segment(start + lax.broadcasted_iota(jnp.int32, (1, WINDOW), 1))
        inside = (key == query) & (window_of(key) == w)
        return jnp.where(inside, 0.0, -1e30).astype(F32)

    def forward_first(self, l, u_ref, then=None):
        s = self.s

        def step(i, _):
            rows = row_block(i)
            normed, _unused = standard(u_ref[rows, :].astype(F32))
            a = (normed * s.vec[l, 0:1, :] + s.vec[l, 1:2, :]).astype(BF16)
            s.a[l, rows, :] = a
            part = dot(a, load_qkv(s.w, l))
            s.qkv[l, rows, 0:D] = (part[:, 0:D] + s.vec[l, 2:3, :]).astype(BF16) * jnp.asarray(HEAD_DIM**-0.5, BF16)
            s.qkv[l, rows, D : 2 * D] = part[:, D : 2 * D].astype(BF16)
            s.qkv[l, rows, 2 * D :] = (part[:, 2 * D :] + s.vec[l, 3:4, :]).astype(BF16)
            return 0

        steps(BLOCKS, step, then)

    def forward_attend(self, l, then=None):
        s = self.s
        s.o[l] = jnp.zeros((ROWS, D), BF16)
        low = lax.broadcasted_iota(jnp.int32, (1, 128), 1) < HEAD_DIM

        def window(w):
            rows = pl.ds(window_start(w), WINDOW)
            bias = self.window_bias(w)
            for pair in range(HEADS // 2):
                base = pair * 128
                q = s.qkv[l, rows, base : base + 128]
                k = s.qkv[l, rows, D + base : D + base + 128]
                v = s.qkv[l, rows, 2 * D + base : 2 * D + base + 128]
                total = None
                for half in range(2):
                    keep = low if half == 0 else jnp.logical_not(low)
                    scores = dot_t(jnp.where(keep, k, jnp.zeros_like(k)), q) + bias
                    top = jnp.maximum(jnp.max(scores, axis=0, keepdims=True), -1e20)
                    weights = jnp.exp(scores - top)
                    summed = jnp.sum(weights, axis=0, keepdims=True)
                    weights = (weights * (1.0 / jnp.maximum(summed, 1e-20))).astype(BF16)
                    s.p[l, w, 2 * pair + half] = weights
                    part = t_dot(weights, jnp.where(keep, v, jnp.zeros_like(v)))
                    total = part if total is None else total + part
                old = s.o[l, rows, base : base + 128]
                s.o[l, rows, base : base + 128] = old + total.astype(BF16)

        windows(window, then)

    def forward_second(self, l, u_ref, out_ref, then=None):
        s = self.s

        def step(i, _):
            rows = row_block(i)
            hidden = u_ref[rows, :].astype(F32) + dot(s.o[l, rows, :], load_proj(s.w, l)) + s.vec[l, 4:5, :]
            s.h[l, rows, :] = hidden
            normed, _unused = standard(hidden)
            c = (normed * s.vec[l, 5:6, :] + s.vec[l, 6:7, :]).astype(BF16)
            s.c[l, rows, :] = c
            total = hidden + s.vec[l, 7:8, :]
            for j in range(CHUNKS):
                cols = slice(j * CHUNK, (j + 1) * CHUNK)
                f = dot(c, load_up(s.w, l, j)) + s.bup[l, 0:1, cols]
                value, slope = gelu_pair(f)
                z = value.astype(BF16)
                s.z[l, rows, cols] = z
                s.slope[l, rows, cols] = slope.astype(BF16)
                total = total + dot(z, load_down(s.w, l, j))
            out_ref[rows, :] = total.astype(BF16)
            return 0

        steps(BLOCKS, step, then)

    def backward_first(self, l, dy_ref, then=None):
        s = self.s
        s.gvec[l] = jnp.zeros_like(s.gvec[l])
        s.dbup[...] = jnp.zeros_like(s.dbup)

        def step(i, _):
            rows = row_block(i)
            dy = dy_ref[rows, :]
            dc = jnp.zeros((BLOCK, D), F32)
            for j in range(CHUNKS):
                cols = slice(j * CHUNK, (j + 1) * CHUNK)
                dz = dot_t(dy, load_down(s.w, l, j))
                df = (dz * s.slope[l, rows, cols].astype(F32)).astype(BF16)
                s.df[rows, cols] = df
                s.dbup[0:1, cols] += column_sum(df.astype(F32))
                dc = dc + dot_t(df, load_up(s.w, l, j))
            normed, inverse = standard(s.h[l, rows, :])
            top = dy.astype(F32)
            dh = top + norm_back(normed, inverse, s.vec[l, 5:6, :], dc)
            s.dh[rows, :] = dh
            dhb = dh.astype(BF16)
            s.dhb[rows, :] = dhb
            s.dout[rows, :] = dot_t(dhb, load_proj(s.w, l)).astype(BF16)
            s.gvec[l, 4:5, :] += column_sum(dhb.astype(F32))
            s.gvec[l, 5:6, :] += column_sum(dc * normed)
            s.gvec[l, 6:7, :] += column_sum(dc)
            s.gvec[l, 7:8, :] += column_sum(top)
            return 0

        steps(BLOCKS, step, then)
        for j in range(FF // D):
            s.gvec[l, 8 + j : 9 + j, :] = s.dbup[0:1, j * D : (j + 1) * D]

    def grad_up(self, l):
        s = self.s
        for b in range(0, FF // D, 2):
            value = t_dot(s.c[l], s.df[:, b * D : (b + 2) * D]).astype(BF16)
            store_rows(s.g, l, wide_tiles(up_tile, b), value[:, :D])
            store_rows(s.g, l, wide_tiles(up_tile, b + 1), value[:, D:])

    def grad_tall(self, l, dy_ref):
        s = self.s
        for j in range(FF // 512):
            value = t_dot(dy_ref[...], s.z[l, :, j * 512 : (j + 1) * 512])
            store_rows(s.g, l, tall_tiles(D + j * 512, 512), value.T.astype(BF16))
        store_rows(s.g, l, tall_tiles(0, D), t_dot(s.o[l], s.dhb[...]).astype(BF16))

    def backward_attend(self, l, then=None):
        s = self.s
        s.dqkv[...] = jnp.zeros_like(s.dqkv)
        low = lax.broadcasted_iota(jnp.int32, (1, 128), 1) < HEAD_DIM

        def window(w):
            rows = pl.ds(window_start(w), WINDOW)
            for pair in range(HEADS // 2):
                base = pair * 128
                q = s.qkv[l, rows, base : base + 128]
                k = s.qkv[l, rows, D + base : D + base + 128]
                v = s.qkv[l, rows, 2 * D + base : 2 * D + base + 128]
                grad = s.dout[rows, base : base + 128]
                dq = dk = dv = None
                for half in range(2):
                    keep = low if half == 0 else jnp.logical_not(low)

                    def only(x, keep=keep):
                        return jnp.where(keep, x, jnp.zeros_like(x))

                    weights = s.p[l, w, 2 * pair + half]
                    grad_half = only(grad)
                    dv_part = dot(weights, grad_half)
                    dp = dot_t(v, grad_half)
                    wide_weights = weights.astype(F32)
                    product = dp * wide_weights
                    ds = (product - wide_weights * jnp.sum(product, axis=0, keepdims=True)).astype(BF16)
                    dk_part = dot(ds, only(q))
                    dq_part = t_dot(only(k), ds)
                    if half == 0:
                        dq, dk, dv = dq_part, dk_part, dv_part
                    else:
                        dq, dk, dv = dq + dq_part, dk + dk_part, dv + dv_part
                for offset, value in ((0, (dq * HEAD_DIM**-0.5).T), (D, dk), (2 * D, dv)):
                    cols = slice(offset + base, offset + base + 128)
                    s.dqkv[rows, cols] = s.dqkv[rows, cols] + value.astype(BF16)

        windows(window, then)

    def backward_last(self, l, u_ref, du_ref, then=None):
        s = self.s

        def step(i, _):
            rows = row_block(i)
            dqkv = s.dqkv[rows, :]
            da = dot_t(dqkv, load_qkv(s.w, l))
            normed, inverse = standard(u_ref[rows, :].astype(F32))
            du = s.dh[rows, :] + norm_back(normed, inverse, s.vec[l, 0:1, :], da)
            du_ref[rows, :] = du.astype(BF16)
            s.gvec[l, 0:1, :] += column_sum(da * normed)
            s.gvec[l, 1:2, :] += column_sum(da)
            s.gvec[l, 2:3, :] += column_sum(dqkv[:, 0:D].astype(F32))
            s.gvec[l, 3:4, :] += column_sum(dqkv[:, 2 * D : 3 * D].astype(F32))
            return 0

        steps(BLOCKS, step, then)
        self.spread_gains(l)

    def grad_qkv(self, l):
        s = self.s
        value = t_dot(s.a[l], s.dqkv[...]).astype(BF16)
        for b in range(3):
            store_rows(s.g, l, wide_tiles(qkv_tile, b), value[:, b * D : (b + 1) * D])


COMPUTE = (
    ("w", (2, 4, 2, 2 * HALF, D), BF16),
    ("g", (2, 4, 2, 2 * HALF, D), BF16),
    ("vec", (2, TILE, D), F32),
    ("gvec", (2, TILE, D), F32),
    ("a", (2, ROWS, D), BF16),
    ("qkv", (2, ROWS, 3 * D), BF16),
    ("o", (2, ROWS, D), BF16),
    ("h", (2, ROWS, D), F32),
    ("c", (2, ROWS, D), BF16),
    ("z", (2, ROWS, FF), BF16),
    ("slope", (2, ROWS, FF), BF16),
    ("p", (2, WINDOWS, HEADS, WINDOW, WINDOW), BF16),
    ("bup", (2, 8, FF), F32),
    ("dbup", (8, FF), F32),
    ("df", (ROWS, FF), BF16),
    ("dh", (ROWS, D), F32),
    ("dhb", (ROWS, D), BF16),
    ("dout", (ROWS, D), BF16),
    ("dqkv", (ROWS, 3 * D), BF16),
)
LINKS = (
    ("x", (ROWS, D), BF16),
    ("cot", (ROWS, D), BF16),
    ("act", (2 * ROWS, D), BF16),
    ("grads", (2 * ROWS, D), BF16),
    ("near_wide", (D // (2 * SLOTS), 3 * D + FF), F32),
    ("near_tall", ((D + FF) // (2 * SLOTS), D), F32),
    ("near_vec", (12, 1, D // (2 * SLOTS)), F32),
    ("total", (2, HALF, D), F32),
) + tuple(
    (f"{name}{st}", (count, STAGES[st][1], D), BF16)
    for st in range(len(STAGES))
    for name, count in (("sum_x", 1), ("from_x", 1), ("from_xy", 4), ("from_xz", 4))
) + tuple(
    (f"{name}{l}{st}", count + (STAGES[st][1], D), BF16)
    for l in range(2)
    for st in range(len(STAGES))
    for name, count in (("from_c", (4, 2)), ("from_y", (4,)), ("from_z", (3,)))
)


class Refs:
    pass


G0, G1, G2, G3, G4, R0, R1, R1X, R2, R2X, R3, R3X, R4, SHARE = range(14)
GAINS, FIRST, ATTEND, SECOND, BACK_FIRST, GRAD_UP, GRAD_TALL, BACK_ATTEND, LAST, GRAD_QKV = range(14, 24)
BY_X, BY_Y, BY_Z = range(3)
GATHER = (
    (((BY_X, BY_Y), (BY_X, BY_Y)), ((BY_X, BY_X), (BY_X, BY_Y)), ((BY_X, BY_X), (BY_X, BY_X)), ((BY_Z, BY_Y), (BY_Z, BY_Y))),
    (((BY_Z, BY_X), (BY_Z, BY_Y)), ((BY_X, BY_Y), (BY_Z, BY_X)), ((BY_Z, BY_Y), (BY_X, BY_Y)), ((BY_X, BY_X), (BY_X, BY_X))),
)
REDUCE = (
    (((BY_Z, BY_Y), (BY_Z, BY_Y)), ((BY_X, BY_Y), (BY_X, BY_Y)), ((BY_Z, BY_Y), (BY_Z, BY_Y)), ((BY_Z, BY_X), (BY_Z, BY_Y))),
    (((BY_X, BY_X), (BY_X, BY_X)), ((BY_Z, BY_X), (BY_X, BY_X)), ((BY_Z, BY_Y), (BY_Z, BY_Y)), ((BY_Z, BY_Y), (BY_Z, BY_Y))),
)
PLAN = (
    (G0, 0, 0, True),
    (G0, 0, 1, True),
    (G0, 0, 2, True),
    (G0, 0, 3, True),
    (G0, 1, 1, True),
    (G0, 1, 3, True),
    (G1, 0, 0, False),
    (G1, 1, 1, False),
    (G1, 0, 1, False),
    (G1, 1, 3, False),
    (G1, 0, 0, True),
    (G1, 1, 1, True),
    (G1, 0, 2, False),
    (G1, 0, 3, False),
    (G1, 0, 1, True),
    (G2, 1, 1, True),
    (G2, 0, 0, False),
    (G4, 1, 1, True),
    (G2, 0, 0, True),
    (G4, 0, 0, True),
    (G1, 1, 3, True),
    (G2, 0, 1, False),
    (G2, 0, 1, True),
    (G3, 0, 0, False),
    (G4, 0, 1, True),
    (G4, 0, 0, False),
    (G1, 0, 2, True),
    (G0, 1, 0, True),
    (G2, 1, 3, False),
    (G2, 1, 3, True),
    (G1, 1, 0, False),
    (G2, 0, 3, False),
    (G4, 1, 3, True),
    (G3, 0, 1, False),
    (G4, 0, 1, False),
    (G1, 1, 0, True),
    (G2, 0, 2, True),
    (G2, 0, 2, False),
    (G1, 0, 3, True),
    (G0, 1, 2, True),
    (GAINS, 0, ()),
    (FIRST, 0, ()),
    (G4, 0, 2, True),
    (G2, 1, 1, False),
    (ATTEND, 0, ((0, G3, 1, 3, False),)),
    (G3, 0, 3, False),
    (G1, 1, 2, False),
    (G2, 1, 0, False),
    (G4, 1, 3, False),
    (G2, 0, 3, True),
    (G2, 1, 0, True),
    (G4, 0, 3, False),
    (G4, 1, 0, True),
    (G3, 1, 1, False),
    (G3, 0, 2, False),
    (G4, 0, 3, True),
    (G4, 1, 1, False),
    (G1, 1, 2, True),
    (G4, 0, 2, False),
    (SECOND, 0, ()),
    (G3, 1, 0, False),
    (SHARE, 0, 0, 0),
    (G2, 1, 2, False),
    (G4, 1, 0, False),
    (GAINS, 1, ()),
    (FIRST, 1, ()),
    (ATTEND, 1, ((0, G2, 1, 2, True),)),
    (G4, 1, 2, True),
    (G3, 1, 2, False),
    (G4, 1, 2, False),
    (SECOND, 1, ()),
    (SHARE, 0, 0, 1),
    (SHARE, 1, 0, 0),
    (BACK_FIRST, 1, ()),
    (GRAD_UP, 1, ()),
    (R0, 1, 3, None),
    (GRAD_TALL, 1, ()),
    (SHARE, 1, 0, 1),
    (R0, 1, 2, None),
    (BACK_ATTEND, 1, ((0, R1, 1, 3, None),)),
    (R1, 1, 2, None),
    (LAST, 1, ()),
    (SHARE, 1, 1, 0),
    (GRAD_QKV, 1, ()),
    (R0, 1, 0, None),
    (R0, 1, 1, None),
    (BACK_FIRST, 0, ()),
    (R2, 1, 3, True),
    (R1, 1, 0, None),
    (R1, 1, 1, None),
    (R2, 1, 3, False),
    (GRAD_UP, 0, ()),
    (R0, 0, 3, None),
    (GRAD_TALL, 0, ()),
    (R0, 0, 2, None),
    (BACK_ATTEND, 0, ((0, R1, 0, 3, None), (0, R3, 1, 1, False), (0, R2, 1, 2, False),)),
    (R2, 1, 2, True),
    (R3, 1, 3, True),
    (R1, 0, 2, None),
    (R1X, 0, 3, True),
    (GRAD_QKV, 0, ()),
    (R3, 1, 3, False),
    (R0, 0, 0, None),
    (LAST, 0, ()),
    (R2, 0, 3, False),
    (R1X, 1, 0, True),
    (SHARE, 0, 1, 0),
    (R0, 0, 1, None),
    (R1, 0, 0, None),
    (R1, 0, 1, None),
    (SHARE, 1, 1, 1),
    (R1X, 1, 1, True),
    (SHARE, 0, 1, 1),
    (R3, 1, 2, True),
    (R2, 0, 2, False),
    (R3X, 1, 3, True),
    (R4, 1, 3, True),
    (R3, 1, 2, False),
    (R2, 0, 2, True),
    (R3, 0, 3, False),
    (R2, 1, 0, True),
    (R2X, 1, 0, True),
    (R2, 0, 3, True),
    (R2, 0, 0, False),
    (R2, 0, 0, True),
    (R3X, 1, 2, True),
    (R2, 0, 1, False),
    (R3, 0, 2, True),
    (R3, 0, 2, False),
    (R4, 1, 2, True),
    (R2, 0, 1, True),
    (R2, 1, 1, True),
    (R2X, 1, 1, True),
    (R3, 1, 0, True),
    (R2X, 0, 1, True),
    (R3X, 0, 2, True),
    (R3, 0, 3, True),
    (R3X, 0, 3, True),
    (R3, 0, 0, False),
    (R3, 0, 0, True),
    (R3X, 0, 0, True),
    (R3, 1, 1, True),
    (R3X, 1, 1, True),
    (R4, 1, 1, True),
    (R4, 1, 0, True),
    (R4, 0, 3, True),
    (R4, 0, 2, True),
    (R3, 0, 1, True),
    (R4, 0, 1, True),
    (R4, 0, 0, True),
)


PIECES = 2


class Links:
    def __init__(self, s):
        self.s = s
        self.section = lax.axis_index("section")
        self.dp = lax.axis_index("dp")
        self.z, self.y, self.core = self.dp // 4, (self.dp // 2) % 2, self.dp % 2
        self.near = (self.section, self.dp + 1 - 2 * self.core)
        self.across = (1 - self.section, self.dp)
        self.beside = (self.section, self.dp + 2 - 4 * self.y)
        self.pending = []
        sides = {(l, owner): self.section == l if owner else self.section != l for l in range(2) for owner in (True, False)}
        self.conditions = {}
        for (l, owner), side in sides.items():
            for core in (None, 0, 1):
                role = side if core is None else side & (self.core == core)
                self.conditions[l, owner, core] = role

    def level(self, steps):
        there = (self.z + steps) % 4
        return there, (self.section, self.dp + 4 * (there - self.z))

    def greet(self):
        others = [self.level(i)[1] for i in (2, 3, 1)] + [self.across, self.beside, self.near]
        for device in others:
            pl.semaphore_signal(pltpu.get_barrier_semaphore(), inc=1, device_id=device, device_id_type=MESH)

    def meet(self):
        pl.semaphore_wait(pltpu.get_barrier_semaphore(), 6)

    def copy(self, src, dst, sems, index, device):
        return pltpu.make_async_remote_copy(
            src_ref=src,
            dst_ref=dst,
            send_sem=sems[0].at[index],
            recv_sem=sems[1].at[index],
            device_id=device,
            device_id_type=MESH,
        )

    def send(self, make, when=None):
        self.pending.append((make, when))
        self.copy(*make()).start()

    def received(self, make):
        self.copy(*make()).wait_recv()

    def drain(self, count=None):
        groups = {}
        for make, when in self.pending[:count]:
            groups.setdefault(id(when), (when, []))[1].append(make)
        self.pending = self.pending[len(self.pending) if count is None else count :]
        for when, makes in groups.values():

            def wait(makes=makes):
                for make in makes:
                    self.copy(*make()).wait_send()

            wait() if when is None else pl.when(when)(wait)


    def rows_of(self, stage, core):
        first, count = STAGES[stage]
        return pl.ds(pl.multiple_of(core * HALF + first, TILE), count)

    def w_part(self, l, z, y, stage, core):
        return self.s.w.at[l, z, y, self.rows_of(stage, core), :]

    def box(self, name, l, stage):
        return getattr(self.s, f"{name}{l}{stage}")


    def shard(self):
        s = self.s
        return ((s.wide_in.at[0], s.near_wide), (s.tall_in.at[0], s.near_tall), (s.vec_in, s.near_vec))

    def near_start(self):
        for index, (src, dst) in enumerate(self.shard()):
            self.send(lambda src=src, dst=dst, index=index: (src, dst, self.s.near_sems, index, self.near))

    def near_finish(self):
        s = self.s
        for index, (src, dst) in enumerate(self.shard()):
            self.received(lambda: (src, dst, s.near_sems, index, self.near))
        first = self.core == 0

        def pair(own, near):
            return jnp.where(first, own, near), jnp.where(first, near, own)

        def put(tile, value):
            s.w[self.section, self.z, self.y, tile * TILE : (tile + 1) * TILE, :] = value

        rows = jnp.concatenate(pair(s.wide_in[0], s.near_wide[...]), axis=0).astype(BF16)
        for block in range(7):
            for i in range(3):
                tile = qkv_tile(3 * block + i) if block < 3 else up_tile(3 * (block - 3) + i)
                put(tile, rows[i * TILE : (i + 1) * TILE, block * D : (block + 1) * D])
        rows = jnp.concatenate(pair(s.tall_in[0], s.near_tall[...]), axis=0).astype(BF16)
        for i in range(15):
            put(tall_tile(i), rows[i * TILE : (i + 1) * TILE])
        count, _, width = s.near_vec.shape
        s.padded[...] = jnp.zeros_like(s.padded)
        for i in range(count):
            for half, value in enumerate(pair(s.vec_in[i], s.near_vec[i])):
                s.padded[half, i : i + 1, 0:width] = value
        for half in range(2):
            put(vec_tile(half), s.padded[half].astype(BF16))

    def place(self, tag, l, stage, coming):
        s = self.s
        kind, i = tag[:-1], int(tag[-1])
        back = self.level(4 - i)[0] if i else self.z
        core = 1 - self.core if coming and kind[0] == "n" else self.core
        if kind == "z":
            slot, device, index = (back if coming else self.z, self.y), self.level(i)[1], 1 + i
        elif kind == "y":
            slot, device, index = (back, 1 - self.y if coming else self.y), self.beside, 8 + i
        elif kind == "x":
            slot, device, index = (self.z, self.y), self.across, 0
        elif kind == "n":
            slot, device, index = (self.z, self.y), self.near, 1
        else:
            slot = (back, self.y if kind[1] == "z" else 1 - self.y)
            device = self.across if kind[0] == "x" else self.near
            index = {"nz": 4, "ny": 12, "xz": 15, "xy": 19}[kind] + i
        part = self.w_part(l, slot[0], slot[1], stage, core)
        return part, part, s.w_sems, (l, stage, index), device

    def gather(self, *role):
        return [(waits, None, sends) for waits, sends in self.gather_copies(*role)]

    def gather_copies(self, name, l, stage, owner, zs, ys):
        three, four = (1, 2, 3), (0, 1, 2, 3)
        if name == G0:
            return [((), ("x0", "z1", "z2", "z3", "y0"))] if owner else []
        if name == G1:
            if owner:
                return [
                    ((f"z{i}",), (f"y{i}", f"nz{i}") + ((f"xz{i}",) if zs == BY_X else ()))
                    for i in three
                ]
            sends = ("n0",) + (("z1", "z2", "z3") if zs == BY_Z else ()) + (("y0",) if ys == BY_Y else ())
            return [(("x0",), sends)]
        if name == G2:
            if owner:
                return [((f"y{i}",), (f"ny{i}",) + ((f"xy{i}",) if ys == BY_X else ())) for i in four]
            source = "z" if zs == BY_Z else "xz"
            return [
                ((f"{source}{i}",), (f"nz{i}",) + ((f"y{i}",) if ys == BY_Y else ()))
                for i in three
            ]
        if name == G3:
            source = "y" if ys == BY_Y else "xy"
            return [] if owner else [((f"{source}{i}",), (f"ny{i}",)) for i in four]
        waits = tuple(f"nz{i}" for i in three) + tuple(f"ny{i}" for i in four)
        return [(waits + (() if owner else ("n0",)), ())]

    def do(self, name, l, stage, side):
        if name == SHARE:
            self.share(l, stage, side)
            return
        config = (GATHER if name <= G4 else REDUCE)[l][stage]
        make = self.place if name <= G4 else self.sum_copy
        if name == R0:
            self.send(lambda: self.sum_copy("c", l, stage, False))
            return
        if name == R1:
            self.received(lambda: self.sum_copy("c", l, stage, True))
            self.add_near(l, stage)
        cores = (None,) if config[0] == config[1] else (0, 1)
        for owner in (True, False) if side is None else (side,):
            for core in cores:
                zs, ys = config[core or 0]
                role = (l, owner, core)
                todo = (self.gather if name <= G4 else self.reduce)(name, l, stage, owner, zs, ys)
                if not todo:
                    continue

                def act(todo=todo, role=role):
                    for waits, work, sends in todo:
                        for tag in waits:
                            self.received(lambda: make(tag, l, stage, True))
                        if work is not None:
                            work()
                        for tag in sends:
                            self.send(lambda tag=tag: make(tag, l, stage, False), self.conditions[role])

                pl.when(self.conditions[role])(act)

    def rows_shared(self, l, which, i):
        s = self.s
        array, out = ((s.act, s.far_act), (s.grads, s.far_grads))[which]
        count = ROWS // PIECES
        first = l * ROWS + i * count
        return array.at[first : first + count, :], out.at[i * count : (i + 1) * count, :], s.o_sems, (which, i), self.across

    def share(self, l, which, i):
        when = self.conditions[l, False, None]
        pl.when(when)(lambda: self.send(lambda: self.rows_shared(l, which, i), when))


    def sum_copy(self, tag, l, stage, coming):
        s = self.s
        rows = self.rows_of(stage, self.core)
        first, count = STAGES[stage]
        if tag == "c":
            src = s.g.at[l, :, :, self.rows_of(stage, 1 - self.core), :]
            return src, self.box("from_c", l, stage), s.g_sems, (l, stage, 0), self.near
        if tag == "Y":
            return s.g.at[l, :, 1 - self.y, rows, :], self.box("from_y", l, stage), s.g_sems, (l, stage, 1), self.beside
        if tag == "XY":
            return s.g.at[l, :, 1 - self.y, rows, :], self.box("from_xy", "", stage), s.g_sems, (l, stage, 5), self.across
        if tag == "XZ":
            return s.g.at[l, :, self.y, rows, :], self.box("from_xz", "", stage), s.g_sems, (l, stage, 6), self.across
        if tag == "X":
            return self.box("sum_x", "", stage), self.box("from_x", "", stage), s.g_sems, (l, stage, 7), self.across
        if tag == "T":
            mine = s.total.at[self.core, first : first + count, :]
            return mine, mine, s.g_sems, (l, stage, 8), self.near
        box = self.box("from_z", l, stage)
        there, device = self.level(int(tag[1]))
        return s.g.at[l, there, self.y, rows, :], box.at[int(tag[1]) - 1], s.g_sems, (l, stage, 1 + int(tag[1])), device

    def add_near(self, l, stage):
        s = self.s
        rows, box = self.rows_of(stage, self.core), self.box("from_c", l, stage)

        def add(i, _):
            z, y = i // 2, i % 2
            s.g[l, z, y, rows, :] = (s.g[l, z, y, rows, :].astype(F32) + box[z, y].astype(F32)).astype(BF16)
            return 0

        lax.fori_loop(0, SLOTS, add, 0)

    def add_column(self, name, l, stage, y):
        s = self.s
        rows = self.rows_of(stage, self.core)

        def add(i, _):
            s.g[l, i, y, rows, :] = (s.g[l, i, y, rows, :].astype(F32) + name[i].astype(F32)).astype(BF16)
            return 0

        lax.fori_loop(0, 4, add, 0)

    def add_levels(self, l, stage):
        box = self.box("from_z", l, stage)
        total = self.s.g[l, self.z, self.y, self.rows_of(stage, self.core), :].astype(F32)
        for i in range(3):
            total = total + box[i].astype(F32)
        return total

    def reduce(self, name, l, stage, owner, zs, ys):
        s = self.s
        first, count = STAGES[stage]
        levels = ("Z1", "Z2", "Z3")
        down = levels if zs == BY_Z else ("XZ",)

        def column(name, y, layer):
            return lambda: self.add_column(self.box(name, layer, stage), l, stage, y)

        def keep():
            s.total[self.core, first : first + count, :] = self.add_levels(l, stage)

        def hand_on():
            self.box("sum_x", "", stage)[0] = self.add_levels(l, stage).astype(BF16)

        def last():
            s.total[self.core, first : first + count, :] += self.box("from_x", "", stage)[0].astype(F32)

        if name == R1:
            if ys == BY_Y:
                return [((), None, ("Y",))]
            return [] if owner else [((), None, ("XY",) + down)]
        if name == R1X:
            return [(("XY",), column("from_xy", 1 - self.y, ""), ("Y",))] if owner and ys == BY_X else []
        if name == R2:
            if owner:
                return [(("Y",), column("from_y", self.y, l), levels if zs == BY_Z else ())]
            return [(("Y",), column("from_y", self.y, l), down)] if ys == BY_Y else []
        if name == R2X:
            return [(("XZ",), column("from_xz", self.y, ""), levels)] if owner and zs == BY_X else []
        if name == R3:
            if owner:
                return [(levels, keep, ("T",) if zs == BY_X else ())]
            return [(levels, hand_on, ("X",))] if zs == BY_Z else []
        if name == R3X:
            return [(("X",), last, ("T",))] if owner and zs == BY_Z else []
        return [(("T",), None, ())] if owner else []


def take_rows(section, whole, out):
    edge = IMG_TOK // TILE * TILE

    @pl.when(section == 0)
    def _():
        out[0:edge, :] = whole[0:edge, :]
        row = lax.broadcasted_iota(jnp.int32, (ROWS - edge, D), 0)
        out[edge:ROWS, :] = jnp.where(row < IMG_TOK - edge, whole[edge:ROWS, :].astype(F32), 0.0).astype(BF16)

    @pl.when(section == 1)
    def _():
        rows = whole[edge : 2 * IMG_TOK, :].astype(F32)
        rows = jnp.concatenate((rows[IMG_TOK - edge :], jnp.zeros((ROWS - IMG_TOK, D), F32)), axis=0)
        out[...] = rows.astype(BF16)


def image_kernel(
    inputs, cotangent, wide_in, tall_in, vec_in, own_act, own_grads, far_act, far_grads, total_out, *scratch
):
    s = Refs()
    names = [name for name, _, _ in COMPUTE + LINKS] + ["padded", "wide_in", "tall_in", "vec_in", "near_sems", "w_sems", "g_sems", "o_sems", "local_sems"]
    flat = list(scratch)
    for name in names:
        if name in ("near_sems", "w_sems", "g_sems", "o_sems"):
            setattr(s, name, (flat.pop(0), flat.pop(0)))
        else:
            setattr(s, name, flat.pop(0))
    s.far_act, s.far_grads = far_act, far_grads
    link, image = Links(s), Image(s)
    section = link.section
    def bring(array, index):
        return pltpu.make_async_copy(array, s.act.at[0 : 2 * IMG_TOK, :], s.local_sems.at[index])

    def keep(array, out, index):
        rows = pl.ds(pl.multiple_of(section * ROWS, ROWS), ROWS)
        return pltpu.make_async_copy(array.at[rows, :], out, s.local_sems.at[index])

    def compute(name, l, then):
        u = s.x if l == 0 else s.act.at[0:ROWS, :]
        dy = s.cot if l == 1 else s.grads.at[ROWS:, :]
        mine = slice(l * ROWS, (l + 1) * ROWS)
        if name == GAINS:
            image.gains(l)
        elif name == FIRST:
            image.forward_first(l, u, then)
        elif name == ATTEND:
            image.forward_attend(l, then)
        elif name == SECOND:
            image.forward_second(l, u, s.act.at[mine, :], then)
        elif name == BACK_FIRST:
            image.backward_first(l, dy, then)
        elif name == GRAD_UP:
            image.grad_up(l)
        elif name == GRAD_TALL:
            image.grad_tall(l, dy)
        elif name == BACK_ATTEND:
            image.backward_attend(l, then)
        elif name == LAST:
            image.backward_last(l, u, s.grads.at[mine, :], then)
        elif name == GRAD_QKV:
            image.grad_qkv(l)

    link.greet()
    shards = [
        pltpu.make_async_copy(array, held, s.local_sems.at[5 + i])
        for i, (array, held) in enumerate(((wide_in, s.wide_in), (tall_in, s.tall_in), (vec_in, s.vec_in)))
    ]
    for shard in shards:
        shard.start()
    bring(inputs, 0).start()
    for shard in shards:
        shard.wait()
    bring(inputs, 0).wait()
    take_rows(section, s.act, s.x)
    bring(cotangent, 1).start()
    link.meet()
    link.near_start()
    link.near_finish()
    fresh = True
    last = max(i for i, entry in enumerate(PLAN) if entry[0] >= GAINS)
    for position, entry in enumerate(PLAN):
        if entry[0] < GAINS:
            link.do(*entry)
            continue
        if entry[0] == FIRST and fresh:
            bring(cotangent, 1).wait()
            take_rows(section, s.act, s.cot)
            fresh = False
        name, l, hooks = entry
        then = {}
        for i in range(WINDOWS):
            actions = [functools.partial(link.do, *hook[1:]) for hook in hooks if hook[0] == i]
            if actions:
                then[i] = lambda actions=actions: [action() for action in actions] and None
        compute(name, l, then)
        if entry[:2] == (SECOND, 1):
            keep(s.act, own_act, 2).start()
            gathered = len(link.pending)
        if position == last:
            link.drain(gathered)
            keep(s.grads, own_grads, 3).start()
    put = pltpu.make_async_copy(s.total, total_out, s.local_sems.at[4])
    put.start()
    for which in range(2):
        for i in range(PIECES):
            link.received(lambda: link.rows_shared(0, which, i))
    link.drain()
    keep(s.act, own_act, 2).wait()
    keep(s.grads, own_grads, 3).wait()
    put.wait()


def one_image(inputs, cotangent, wide, tall, vec):
    anywhere = pl.BlockSpec(memory_space=pl.ANY)
    sems = [
        pltpu.SemaphoreType.DMA(shape)
        for shape in ((3,), (2, len(STAGES), 23), (2, len(STAGES), 9), (2, PIECES))
        for _ in range(2)
    ] + [pltpu.SemaphoreType.DMA((8,))]
    rows = jax.ShapeDtypeStruct((ROWS, D), BF16)
    return pl.pallas_call(
        image_kernel,
        out_shape=[rows, rows, rows, rows, jax.ShapeDtypeStruct((2, HALF, D), F32)],
        in_specs=[anywhere] * 5,
        out_specs=[anywhere] * 5,
        scratch_shapes=[pltpu.VMEM(shape, dtype) for _, shape, dtype in COMPUTE + LINKS]
        + [pltpu.VMEM((2, TILE, D), F32)]
        + [pltpu.VMEM(array.shape, F32) for array in (wide, tall, vec)]
        + sems,
        compiler_params=pltpu.CompilerParams(
            vmem_limit_bytes=64 * 2**20, collective_id=0, has_side_effects=True
        ),
        cost_estimate=pl.CostEstimate(flops=18 * 10**9, bytes_accessed=20 * 10**6, transcendentals=10**7),
    )(inputs, cotangent, wide, tall, vec)


def plain_kernel(x, cot, w, act, grads, g, *scratch):
    s = Refs()
    s.w, s.g = w, g
    for (name, _, _), ref in zip(COMPUTE[2:], scratch):
        setattr(s, name, ref)
    image = Image(s)
    for l, u, out in ((0, x, act.at[0]), (1, act.at[0], act.at[1])):
        image.gains(l)
        image.forward_first(l, u)
        image.forward_attend(l)
        image.forward_second(l, u, out)
    for l, u, dy, du in ((1, act.at[0], cot, grads.at[1]), (0, x, grads.at[1], grads.at[0])):
        image.backward_first(l, dy)
        image.grad_up(l)
        image.grad_tall(l, dy)
        image.backward_attend(l)
        image.backward_last(l, u, du)
        image.grad_qkv(l)


def plain_image(x, cot, w):
    whole = pl.BlockSpec(memory_space=pltpu.VMEM)
    return pl.pallas_call(
        plain_kernel,
        out_shape=(
            jax.ShapeDtypeStruct((2, ROWS, D), BF16),
            jax.ShapeDtypeStruct((2, ROWS, D), BF16),
            jax.ShapeDtypeStruct(w.shape, BF16),
        ),
        in_specs=[whole] * 3,
        out_specs=(whole,) * 3,
        scratch_shapes=[pltpu.VMEM(shape, dtype) for _, shape, dtype in COMPUTE[2:]],
        compiler_params=pltpu.CompilerParams(vmem_limit_bytes=64 * 2**20),
    )(x, cot, w)


def tile_order():
    wide = [qkv_tile(i) for i in range(9)] + [up_tile(i) for i in range(12)]
    return wide + [tall_tile(i) for i in range(15)] + [vec_tile(half) for half in range(2)]


def any_mesh(
    inputs, cotangent, wide_weights, wide_first, wide_second, tall_weights, tall_first, tall_second,
    vectors, vector_first, vector_second,
):
    section = lax.axis_index("section")
    both = ("section", "dp")
    wide = lax.all_gather(wide_weights[0].astype(BF16), both, axis=0, tiled=True)
    tall = lax.all_gather(tall_weights[0].astype(BF16), both, axis=0, tiled=True)
    vec = lax.all_gather(lax.all_gather(vectors[0].astype(BF16), "dp", axis=1, tiled=True), "section", axis=0)
    vec_rows, width = vec.shape[1], D // (2 * SLOTS)
    order = tile_order()
    place = sorted(range(len(order)), key=order.__getitem__)
    wide = wide.reshape(2, SLOTS, 3, TILE, 7, D).transpose(0, 1, 4, 2, 3, 5).reshape(2, SLOTS, 21, TILE, D)
    tall = tall.reshape(2, SLOTS, 15, TILE, D)
    vec = vec.reshape(2, vec_rows, SLOTS, 2, width).transpose(0, 2, 3, 1, 4)
    vec = jnp.pad(vec, ((0, 0),) * 3 + ((0, TILE - vec_rows), (0, D - width)))
    tiles = jnp.concatenate((wide, tall, vec), axis=2)[:, :, jnp.array(place)]
    act, grads, g = plain_image(
        own_rows(inputs, section), own_rows(cotangent, section), tiles.reshape(2, SLOTS // 2, 2, 2 * HALF, D)
    )
    far_act, far_grads = (
        lax.ppermute(lax.dynamic_index_in_dim(array, 1 - section, keepdims=False), "section", [(0, 1), (1, 0)])
        for array in (act, grads)
    )
    g = g.reshape(2, SLOTS, len(order), TILE, D)[:, :, jnp.array(order)].astype(F32)
    wide = g[:, :, :21].reshape(2, SLOTS, 7, 3, TILE, D).transpose(0, 1, 3, 4, 2, 5).reshape(2, D, 7 * D)
    tall = g[:, :, 21:36].reshape(2, D + FF, D)
    vec = g[:, :, 36:, :vec_rows, :width].transpose(0, 3, 1, 2, 4).reshape(2, vec_rows, D)

    def reduced(array, dim):
        array = lax.psum_scatter(array, "section", scatter_dimension=0, tiled=False)
        return lax.psum_scatter(array, "dp", scatter_dimension=dim, tiled=True)

    return finish(
        section, act, grads, far_act, far_grads, reduced(wide, 0), reduced(tall, 0), reduced(vec, 1),
        wide_weights, wide_first, wide_second, tall_weights, tall_first, tall_second, vectors, vector_first, vector_second,
    )


def adamw(weights, first, second, grads, rate, decay):
    first_new = BETA_ONE * first + (1.0 - BETA_ONE) * grads
    second_new = BETA_TWO * second + (1.0 - BETA_TWO) * grads * grads
    corrected = (
        first_new
        / (1.0 - BETA_ONE**STEP)
        / (jnp.sqrt(second_new / (1.0 - BETA_TWO**STEP)) + ADAM_EPS)
    )
    return (first_new, second_new, weights - rate * (corrected + decay * weights))


def own_rows(array, section):
    return jnp.pad(lax.dynamic_slice_in_dim(array, section * IMG_TOK, IMG_TOK), ((0, ROWS - IMG_TOK), (0, 0)))


def finish(
    section, act, grads, far_act, far_grads, total_wide, total_tall, total_vec,
    wide_weights, wide_first, wide_second, tall_weights, tall_first, tall_second, vectors, vector_first, vector_second,
):
    def joined(array, other):
        mine = lax.dynamic_index_in_dim(array, section, keepdims=False)[:IMG_TOK]
        other = other[:IMG_TOK]
        return jnp.where(section == 0, jnp.concatenate((mine, other)), jnp.concatenate((other, mine)))

    wide_m, wide_s, wide_n = adamw(wide_weights[0], wide_first[0], wide_second[0], total_wide, RATE_MATRIX, DECAY)
    tall_m, tall_s, tall_n = adamw(tall_weights[0], tall_first[0], tall_second[0], total_tall, RATE_MATRIX, DECAY)
    vec_m, vec_s, vec_n = adamw(vectors[0], vector_first[0], vector_second[0], total_vec, RATE_VECTOR, 0.0)
    outs = (joined(act, far_act), joined(grads, far_grads), wide_m, wide_s, wide_n, tall_m, tall_s, tall_n, vec_m, vec_s, vec_n)
    return tuple(out[None] for out in outs)


OWN_ROWS = ("own_act", "own_grads", "far_act", "far_grads", "total")
MASTERS = ("wide_w", "wide_m", "wide_s", "tall_w", "tall_m", "tall_s", "vec_w", "vec_m", "vec_s")
RESULTS = ("act", "grads", "wide_m1", "wide_s1", "wide_w1", "tall_m1", "tall_s1", "tall_w1", "vec_m1", "vec_s1", "vec_w1")


def finish_kernel(*refs):
    names = OWN_ROWS + MASTERS
    given, results = refs[: len(names)], refs[len(names) : len(names) + len(RESULTS)]
    held = refs[len(names) + len(RESULTS) : -2]
    came, left = refs[-2:]
    section = lax.axis_index("section")
    first = lax.axis_index("dp") % 2 == 0
    s = Refs()
    copies = {}
    for index, (name, src, dst) in enumerate(zip(names, given, held)):
        setattr(s, name, dst)
        copies[name] = pltpu.make_async_copy(src, dst, came.at[index])
    for index, (name, src, dst) in enumerate(zip(RESULTS, held[len(names) :], results)):
        setattr(s, name, src)
        copies[name] = pltpu.make_async_copy(src, dst, left.at[index])
    for name in names:
        copies[name].start()

    def fetch(*wanted):
        for name in wanted:
            copies[name].wait()

    def put(*done):
        for name in done:
            copies[name].start()

    edge = IMG_TOK // TILE * TILE

    def join(low, high, out):
        out[0, 0:edge, :] = low[0:edge, :]
        rows = jnp.concatenate((low[edge:IMG_TOK, :].astype(F32), high[0:IMG_TOK, :].astype(F32)), axis=0)
        out[0, edge : 2 * IMG_TOK, :] = rows.astype(BF16)

    for own, far, out in (("own_act", "far_act", "act"), ("own_grads", "far_grads", "grads")):
        fetch(own, far)
        pl.when(section == 0)(lambda: join(getattr(s, own), getattr(s, far), getattr(s, out)))
        pl.when(section == 1)(lambda: join(getattr(s, far), getattr(s, own), getattr(s, out)))
        put(out)

    def tile(i):
        return s.total[i // 19, (i % 19) * TILE : (i % 19 + 1) * TILE, :]

    def own_half(rows):
        half = rows.shape[0] // 2
        return jnp.where(first, rows[:half], rows[half:])

    fetch("total", "wide_w", "wide_m", "wide_s")
    for block in range(7):
        tiles = [qkv_tile(3 * block + i) if block < 3 else up_tile(3 * (block - 3) + i) for i in range(3)]
        g = own_half(jnp.concatenate([tile(i) for i in tiles], axis=0))
        cols = slice(block * D, (block + 1) * D)
        s.wide_m1[0, :, cols], s.wide_s1[0, :, cols], s.wide_w1[0, :, cols] = adamw(
            s.wide_w[0, :, cols], s.wide_m[0, :, cols], s.wide_s[0, :, cols], g, RATE_MATRIX, DECAY
        )
    put("wide_m1", "wide_s1", "wide_w1")
    fetch("tall_w", "tall_m", "tall_s")
    g = own_half(jnp.concatenate([tile(tall_tile(i)) for i in range(15)], axis=0))
    s.tall_m1[0], s.tall_s1[0], s.tall_w1[0] = adamw(s.tall_w[0], s.tall_m[0], s.tall_s[0], g, RATE_MATRIX, DECAY)
    put("tall_m1", "tall_s1", "tall_w1")
    fetch("vec_w", "vec_m", "vec_s")
    count, _, width = s.vec_w.shape
    g = jnp.where(first, tile(vec_tile(0)), tile(vec_tile(1)))[0:count, 0:width]
    for i in range(count):
        s.vec_m1[i], s.vec_s1[i], s.vec_w1[i] = adamw(
            s.vec_w[i], s.vec_m[i], s.vec_s[i], g[i : i + 1], RATE_VECTOR, 0.0
        )
    put("vec_m1", "vec_s1", "vec_w1")
    for name in RESULTS:
        copies[name].wait()


def per_device(
    inputs, cotangent, wide_weights, wide_first, wide_second, tall_weights, tall_first, tall_second,
    vectors, vector_first, vector_second,
):
    vectors, vector_first, vector_second = (
        jnp.transpose(array, (1, 0, 2)) for array in (vectors, vector_first, vector_second)
    )
    sums = one_image(inputs, cotangent, wide_weights, tall_weights, vectors)
    given = list(sums) + [
        wide_weights, wide_first, wide_second, tall_weights, tall_first, tall_second, vectors, vector_first, vector_second,
    ]
    anywhere = pl.BlockSpec(memory_space=pl.ANY)
    rows = jax.ShapeDtypeStruct((1,) + inputs.shape, BF16)
    outs = [rows, rows] + [
        jax.ShapeDtypeStruct(array.shape, F32) for array in (wide_weights,) * 3 + (tall_weights,) * 3 + (vectors,) * 3
    ]
    results = pl.pallas_call(
        finish_kernel,
        out_shape=outs,
        in_specs=[anywhere] * len(given),
        out_specs=[anywhere] * len(outs),
        scratch_shapes=[pltpu.VMEM(array.shape, array.dtype) for array in given + outs]
        + [pltpu.SemaphoreType.DMA((len(given),)), pltpu.SemaphoreType.DMA((len(outs),))],
        compiler_params=pltpu.CompilerParams(vmem_limit_bytes=64 * 2**20),
        cost_estimate=pl.CostEstimate(flops=10**7, bytes_accessed=10**7, transcendentals=10**6),
    )(*given)
    return tuple(results[:8]) + tuple(jnp.transpose(array, (1, 0, 2)) for array in results[8:])


def solution(mesh):
    data = P("dp", None)
    matrix = P("section", "dp", None)
    vector = P("section", None, "dp")
    in_specs = (data, data) + (matrix,) * 6 + (vector,) * 3
    out_specs = (matrix,) * 8 + (vector,) * 3
    device_fn = per_device if mesh.shape["dp"] == 2 * SLOTS else any_mesh
    return jax.shard_map(device_fn, mesh=mesh, in_specs=in_specs, out_specs=out_specs, check_vma=False)
```
